256 devices in a mesh: gx: 32 (over z, y), gy: 8 (over x, core).
Axes of the slice: x: 4, y: 4, z: 8, core: 2. Of those that a mesh axis runs over, the one named last changes fastest.
Arguments:
- forcing: float32 [2, 256, 32768], P(None, 'gy', 'gx'), may hold values from -6 to 6
- ice_mask: int32 [256, 32768], P('gy', 'gx'), may hold values from 0 to 1, as said below
- viscosity_class: int32 [256, 32768], P('gy', 'gx'), may hold values from 0 to 15
- drag_class: int32 [256, 32768], P('gy', 'gx'), may hold values from 0 to 15
- viscosity_table: float32 [16], replicated, may hold values from 0.5 to 8
- drag_table: float32 [16], replicated, may hold values from 0.05 to 2
Outputs:
- velocity: float32 [2, 256, 32768], P(None, 'gy', 'gx')
The draws below stay inside these ranges and needn't reach their ends.
Inputs may be any that keep to these rules, and one draw needn't show every extreme that they name: `ice_mask`: ice lies in tiles of 32 rows and 256 columns; whole tiles may be empty, and a tile may be partly covered behind a ragged front.
All inputs are finite; a program needn't handle non-finite values.
Results may differ from the reference program's by a relative error of at most 0.0001.
Values sent between devices are 32-bit elements; how exact they have to be, the bound alone decides.
No kernel may reach another device: no remote copies, remote signals or barrier semaphores. Data moves between devices by JAX's collectives and lax.ppermute only.
A program may use at most 128 MiB of HBM per device.

```python
import math
import jax
import jax.numpy as jnp

CR = 32
CC = 1024
CLASSES = 16
NU = 2
COARSE_SWEEPS = 6
NR = 256
NC = 32768


def draw_ice_mask(key, part):
    key = jax.random.fold_in(key, 11)
    key_depth, key_front = jax.random.split(key)
    tile_rows = NR // CR
    tile_width = CC // 4
    tile_cols = NC // tile_width
    depth = jax.random.randint(key_depth, (tile_cols,), 1, tile_rows + 1)
    front = jax.random.randint(key_front, (NC,), 0, CR + 1)
    column_depth = jnp.repeat(depth, tile_width)[None, :]
    rows = jnp.arange(NR, dtype=jnp.int32)[:, None]
    tile_index = rows // CR
    inside = rows % CR
    ice = (tile_index < column_depth) | (tile_index == column_depth) & (inside < front[None, :])
    return ice.astype(jnp.int32)


def patch_classes(key):
    key_patch, key_jitter = jax.random.split(key)
    patches = jax.random.randint(key_patch, (NR // 8, NC // 8), 0, CLASSES)
    patches = jnp.repeat(jnp.repeat(patches, 8, axis=0), 8, axis=1)
    jitter = jax.random.randint(key_jitter, (NR, NC), 0, 3)
    return ((patches + jitter) % CLASSES).astype(jnp.int32)


def draw_viscosity_class(key, part):
    key = jax.random.fold_in(key, 23)
    return patch_classes(key)


def draw_drag_class(key, part):
    key = jax.random.fold_in(key, 37)
    return patch_classes(key)


def level_of(own_key, dims, shards, least, largest):
    loudness, own = 1.0, jax.random.fold_in(own_key, 6)
    for dim, parts in shards:
        steps = jnp.exp(jax.random.uniform(jax.random.fold_in(own, dim), (parts,), jnp.float32, least / len(shards), largest / len(shards)))
        loudness = loudness * jnp.repeat(steps, dims[dim] // parts).reshape([-1 if axis == dim else 1 for axis in range(len(dims))])
    return loudness


def normal_values(stream_key, shape, width, bound, shards=(), kind=jnp.bfloat16):
    values = jax.random.normal(stream_key, shape, jnp.float32) * width
    if len(shards) > 0:
        values = level_of(stream_key, shape, shards, -0.22, 0.18) * values
    return jnp.clip(values, min=-bound, max=bound).astype(kind)


def setup_inputs(seed: int = 0) -> dict:
    key_list = jax.random.split(jax.random.key(seed), 7)
    return {
        "forcing": normal_values(key_list[0], (2, NR, NC), 1.0, 6.0, ((1, 8), (2, 32)), jnp.float32),
        "ice_mask": draw_ice_mask(jax.random.fold_in(key_list[6], 71), 0),
        "viscosity_class": draw_viscosity_class(jax.random.fold_in(key_list[6], 71), 0),
        "drag_class": draw_drag_class(jax.random.fold_in(key_list[6], 71), 0),
        "viscosity_table": jnp.clip(jnp.exp(jax.random.uniform(key_list[4], (CLASSES,), jnp.float32, math.log(0.5), math.log(8.0))), 0.5, 8.0),
        "drag_table": jnp.clip(jnp.exp(jax.random.uniform(key_list[5], (CLASSES,), jnp.float32, math.log(0.05), math.log(2.0))), 0.05, 2.0),
    }


OMEGA = 0.6


def pad_last(x):
    return jnp.pad(x, [(0, 0)] * (x.ndim - 2) + [(1, 1), (1, 1)])


def shifted(a, dr, dc):
    rows = a.shape[-2]
    cols = a.shape[-1]
    return a[..., 1 + dr:rows - 1 + dr, 1 + dc:cols - 1 + dc]


def apply_operator(w_pad, coef_pad, beta):
    eta_pad = coef_pad[0]
    mask_pad = coef_pad[1]
    eta_here = shifted(eta_pad, 0, 0)
    mask_here = shifted(mask_pad, 0, 0)
    center = shifted(w_pad, 0, 0)
    flux = jnp.zeros_like(center)
    face_sum = jnp.zeros_like(eta_here)
    for dr, dc in ((1, 0), (-1, 0), (0, 1), (0, -1)):
        face = 0.5 * (eta_here + shifted(eta_pad, dr, dc)) * mask_here * shifted(mask_pad, dr, dc)
        flux = flux + face * (center - shifted(w_pad, dr, dc))
        face_sum = face_sum + face
    other = w_pad[::-1]
    mixed = 0.25 * (shifted(other, 1, 1) - shifted(other, 1, -1) - shifted(other, -1, 1) + shifted(other, -1, -1))
    base = beta + 1.0 - mask_here
    image = base * center + flux + 0.2 * eta_here * mask_here * mixed
    return image, base + face_sum


def block_sum(x):
    shape = x.shape
    return x.reshape(shape[:-2] + (shape[-2] // 2, 2, shape[-1] // 2, 2)).sum(axis=(-3, -1))


def block_max(x):
    shape = x.shape
    return x.reshape(shape[:-2] + (shape[-2] // 2, 2, shape[-1] // 2, 2)).max(axis=(-3, -1))


def sweep(w_field, right, coef_pad, beta):
    image, diag = apply_operator(pad_last(w_field), coef_pad, beta)
    return w_field + OMEGA * (right - image) / diag


def solve_level(level, right, levels):
    coef_pad, beta = levels[level]
    w_field = jnp.zeros_like(right)
    if level == 3:
        for step in range(COARSE_SWEEPS):
            w_field = sweep(w_field, right, coef_pad, beta)
        return w_field
    for step in range(NU):
        w_field = sweep(w_field, right, coef_pad, beta)
    image, diag = apply_operator(pad_last(w_field), coef_pad, beta)
    coarse = solve_level(level + 1, block_sum(right - image), levels)
    w_field = w_field + jnp.repeat(jnp.repeat(coarse, 2, axis=-2), 2, axis=-1)
    for step in range(NU):
        w_field = sweep(w_field, right, coef_pad, beta)
    return w_field


def reference(forcing, ice_mask, viscosity_class, drag_class, viscosity_table, drag_table):
    mask = ice_mask.astype(jnp.float32)
    eta = viscosity_table[viscosity_class] * mask
    beta = drag_table[drag_class] * mask
    levels = []
    for level in range(4):
        levels.append((pad_last(jnp.stack([eta, mask])), beta))
        mask = block_max(mask)
        eta = 0.5 * block_sum(eta)
        beta = block_sum(beta)
    return solve_level(0, forcing, levels)
```

```python
import jax
import jax.numpy as jnp
from jax import lax
from jax.experimental import pallas as pl
from jax.experimental.pallas import tpu as pltpu
from jax.sharding import PartitionSpec as P

OMEGA = 0.6
KEEP = 1.0 - OMEGA
ROWS, COLS = 32, 1024
EDGE = 128
HALO = 16
WIDE = COLS + 2 * EDGE
PLANES = (8, 4, 2)
LANES = (1280, 640, 384)
LANES3 = 256
VMEM_LIMIT = 48 * 1024 * 1024


def vmem(count):
    return [pl.BlockSpec(memory_space=pltpu.VMEM)] * count


def params():
    return pltpu.CompilerParams(vmem_limit_bytes=VMEM_LIMIT)


def shape(*dims):
    return jax.ShapeDtypeStruct(dims, jnp.float32)


def from_left(x):
    return pltpu.roll(x, 1, axis=1)


def from_right(x):
    return pltpu.roll(x, x.shape[1] - 1, axis=1)


def from_above(x):
    return pltpu.roll(x, 1, axis=0)


def from_below(x):
    return pltpu.roll(x, x.shape[0] - 1, axis=0)


def tiles(x):
    return [x[:, i : i + 128] for i in range(0, x.shape[1], 128)]


def lane(kind):
    return lax.broadcasted_iota(jnp.int32, (8, 128), kind)


def pick(x, index):
    return jnp.take_along_axis(x, index, axis=1, mode="promise_in_bounds")


def halve_lanes(x, lanes):
    at = lane(1)
    index = 2 * (at % 64)
    parts = [pick(t + from_right(t), index) for t in tiles(x)]
    out = []
    for i in range(0, len(parts), 2):
        high = parts[i + 1] if i + 1 < len(parts) else jnp.zeros_like(parts[i])
        out.append(jnp.where(at < 64, parts[i], high))
    while len(out) * 128 < lanes:
        out.append(jnp.zeros_like(out[0]))
    return jnp.concatenate(out[: lanes // 128], axis=1)


def double_lanes(x, lanes):
    index = lane(1) // 2
    parts = tiles(x)
    return jnp.concatenate(
        [pick(parts[i // 2], index + 64 * (i % 2)) for i in range(lanes // 128)], axis=1
    )


def coefficients(eta, beta, eta_below, face_above):
    ice = eta > 0.0
    eta_right = from_right(eta)
    right = jnp.where(ice & (eta_right > 0.0), 0.5 * (eta + eta_right), 0.0)
    left = from_left(right)
    below = jnp.where(ice & (eta_below > 0.0), 0.5 * (eta + eta_below), 0.0)
    above = face_above(below)
    base = beta + jnp.where(ice, 0.0, 1.0)
    diag = base + ((right + left) + (below + above))
    return right, left, below, above, 0.05 * eta_right, 0.05 * from_left(eta), diag


def gather_terms(right, left, cross_right, cross_left, below, above, here, under, over, other_step, force):
    from_west = from_left(right * here + cross_right * other_step)
    from_east = from_right(left * here - cross_left * other_step)
    return (force + (from_west + from_east)) + (below * under + above * over)


class Level:
    def __init__(self, planes, refs):
        self.planes = planes
        self.right, self.left, self.cross_right, self.cross_left, self.below, self.scale, self.force, self.field = refs

    @staticmethod
    def shapes(level):
        planes, lanes = PLANES[level], LANES[level]
        one = [(planes, 8, lanes)] * 4 + [(planes + 1, 8, lanes), (planes, 8, lanes)]
        return one + [(2, planes, 8, lanes), (2, planes + 2, 8, lanes)]

    def wrap(self, field):
        for k in range(2):
            field[k, 0] = from_above(field[k, self.planes])
            field[k, self.planes + 1] = from_below(field[k, 1])

    def terms(self, p, field):
        out = []
        steps = [field[k, p + 2] - field[k, p] for k in range(2)]
        for k in range(2):
            out.append(
                gather_terms(
                    self.right[p],
                    self.left[p],
                    self.cross_right[p],
                    self.cross_left[p],
                    self.below[p + 1],
                    self.below[p],
                    field[k, p + 1],
                    field[k, p + 2],
                    field[k, p],
                    steps[1 - k],
                    self.force[k, p],
                )
            )
        return out

    def sweep(self, source, target):
        for p in range(self.planes):
            terms = self.terms(p, source)
            for k in range(2):
                target[k, p + 1] = KEEP * source[k, p + 1] + self.scale[p] * terms[k]

    def setup(self, eta, beta, diag):
        planes = self.planes
        for p in range(planes):
            here = eta[p]
            ice = here > 0.0
            next_eta = eta[p + 1] if p + 1 < planes else from_below(eta[0])
            self.below[p + 1] = jnp.where(ice & (next_eta > 0.0), 0.5 * (here + next_eta), 0.0)
        self.below[0] = from_above(self.below[planes])
        for p in range(planes):
            here = eta[p]
            ice = here > 0.0
            eta_right = from_right(here)
            right = jnp.where(ice & (eta_right > 0.0), 0.5 * (here + eta_right), 0.0)
            left = from_left(right)
            base = beta[p] + jnp.where(ice, 0.0, 1.0)
            total = base + ((right + left) + (self.below[p + 1] + self.below[p]))
            self.right[p] = right
            self.left[p] = left
            self.cross_right[p] = 0.05 * eta_right
            self.cross_left[p] = 0.05 * from_left(here)
            diag[p] = total
            self.scale[p] = OMEGA / total

    def first_sweeps(self, other):
        for k in range(2):
            for p in range(self.planes):
                other[k, p + 1] = self.scale[p] * self.force[k, p]
        self.wrap(other)
        self.sweep(other, self.field)
        self.wrap(self.field)

    def restrict(self, diag, target, lanes):
        for p in range(0, self.planes, 2):
            rest = [0.0, 0.0]
            for q in (p, p + 1):
                terms = self.terms(q, self.field)
                for k in range(2):
                    rest[k] = rest[k] + (terms[k] - diag[q] * self.field[k, q + 1])
            for k in range(2):
                target(k, p // 2, halve_lanes(rest[k], lanes))

    def last_sweeps(self, coarse, result, other):
        for k in range(2):
            for p in range(0, self.planes, 2):
                add = double_lanes(coarse(k, p // 2), self.field.shape[-1])
                result[k, p + 1] = self.field[k, p + 1] + add
                result[k, p + 2] = self.field[k, p + 2] + add
        self.wrap(result)
        self.sweep(result, other)
        self.wrap(other)
        self.sweep(other, result)


def halve_planes(source, target, planes, lanes, scale):
    for p in range(0, planes, 2):
        both = halve_lanes(source[p] + source[p + 1], lanes)
        target[p // 2] = scale * both if scale != 1.0 else both


def lookup_kernel(v_table, d_table, forcing, mask, v_class, d_class, send_even, send_odd, coef):
    at = lane(1)
    tables = []
    for table in (v_table, d_table):
        row = jnp.zeros((8, 128), jnp.float32)
        for i in range(16):
            row = jnp.where(at == i, table[i], row)
        tables.append(row)
    for r in range(0, ROWS, 8):
        for c in range(0, COLS, 128):
            part = (pl.ds(r, 8), pl.ds(c, 128))
            ice = mask[part].astype(jnp.float32)
            for k, classes in enumerate((v_class, d_class)):
                coef[(k,) + part] = pick(tables[k], classes[part]) * ice
    even = lax.axis_index("gx") % 2 == 0
    for k in range(2):
        for source, row in ((forcing, k), (coef, k + 2)):
            low = source[k, :, 0:EDGE]
            high = source[k, :, COLS - EDGE : COLS]
            send_even[row] = jnp.where(even, high, low)
            send_odd[row] = jnp.where(even, low, high)


def side_columns(get_even, get_odd):
    gx = lax.axis_index("gx")
    even = gx % 2 == 0
    a, b = get_even, get_odd
    left = jnp.where(gx == 0, 0.0, jnp.where(even, b, a))
    right = jnp.where(gx == lax.axis_size("gx") - 1, 0.0, jnp.where(even, a, b))
    return left, right


def rows_kernel(forcing, coef, got_even, got_odd, send_even, send_odd):
    even = lax.axis_index("gy") % 2 == 0
    for row in range(4):
        source = forcing if row < 2 else coef
        top = slice(0, HALO)
        bottom = slice(ROWS - HALO, ROWS)
        for part, flag in ((send_even, even), (send_odd, jnp.logical_not(even))):
            lows = side_columns(got_even[row, top], got_odd[row, top])
            highs = side_columns(got_even[row, bottom], got_odd[row, bottom])
            part[row, :, 0:EDGE] = jnp.where(flag, highs[0], lows[0])
            part[row, :, WIDE - EDGE : WIDE] = jnp.where(flag, highs[1], lows[1])
            part[row, :, EDGE : WIDE - EDGE] = jnp.where(flag, source[row % 2, bottom], source[row % 2, top])


def own_rows(a, b):
    upper = lax.broadcasted_iota(jnp.int32, a.shape, 0) < 4
    return jnp.where(upper, pltpu.roll(a, 6, axis=0), pltpu.roll(b, 2, axis=0))


def down_kernel(forcing, coef, got_even, got_odd, rows_even, rows_odd, *refs):
    levels = [Level(PLANES[i], refs[8 * i : 8 * i + 8]) for i in range(3)]
    near, far = refs[24:26]
    natural = refs[26]
    etas, betas, diags, others = (refs[27 + 3 * i : 30 + 3 * i] for i in range(4))
    gy = lax.axis_index("gy")
    even = gy % 2 == 0
    first = gy == 0
    last = gy == lax.axis_size("gy") - 1
    for row in range(4):
        source = forcing if row < 2 else coef
        sides = side_columns(got_even[row], got_odd[row])
        for i in range(WIDE // 128):
            cols = slice(128 * i, 128 * i + 128)
            a, b = rows_even[row, :, cols], rows_odd[row, :, cols]
            natural[i, 0:HALO] = jnp.where(first, 0.0, jnp.where(even, b, a))
            natural[i, HALO + ROWS :] = jnp.where(last, 0.0, jnp.where(even, a, b))
            if i == 0:
                own = sides[0]
            elif i == WIDE // 128 - 1:
                own = sides[1]
            else:
                own = source[row % 2, :, 128 * i - 128 : 128 * i]
            natural[i, HALO : HALO + ROWS] = own
            for p in range(8):
                plane = natural[i, pl.ds(p, 8, stride=8), :]
                if row < 2:
                    levels[0].force[row, p, :, cols] = plane
                else:
                    (etas, betas)[row - 2][0][p, :, cols] = plane
    for level in range(3):
        here = levels[level]
        here.setup(etas[level], betas[level], diags[level])
        here.first_sweeps(others[level])
        if level < 2:
            lanes = LANES[level + 1]
            halve_planes(etas[level], etas[level + 1], here.planes, lanes, 0.5)
            halve_planes(betas[level], betas[level + 1], here.planes, lanes, 1.0)

            def store(k, p, value, target=levels[level + 1].force):
                target[k, p] = value

            here.restrict(diags[level], store, lanes)
    found = [None, None]

    def keep(k, p, value):
        found[k] = value

    levels[2].restrict(diags[2], keep, LANES3)
    eta = 0.5 * halve_lanes(etas[2][0] + etas[2][1], LANES3)
    beta = halve_lanes(betas[2][0] + betas[2][1], LANES3)
    head = jnp.concatenate([own_rows(found[0], found[1]), own_rows(eta, beta)], axis=1)
    far[...] = head
    near[:, 0 : 2 * LANES3] = head
    at = 2 * LANES3
    for p in range(2):
        near[:, at : at + 384] = own_rows(levels[2].field[0, p + 1], levels[2].field[1, p + 1])
        near[:, at + 768 : at + 1152] = own_rows(levels[2].force[0, p], levels[2].force[1, p])
        at += 384


def up_kernel(far, near_even, near_odd, far_above, far_below, *refs):
    levels = [Level(PLANES[i], refs[8 * i : 8 * i + 8]) for i in range(3)]
    velocity, natural, late_force, late_field = refs[24:28]
    fields, others = refs[28:31], refs[31:34]
    gy = lax.axis_index("gy")
    count = lax.axis_size("gy")
    even = gy % 2 == 0

    def above(part):
        return jnp.where(gy == 0, 0.0, jnp.where(even, near_odd[:, part], near_even[:, part]))

    def below(part):
        return jnp.where(gy == count - 1, 0.0, jnp.where(even, near_even[:, part], near_odd[:, part]))

    def sublanes(like):
        return lax.broadcasted_iota(jnp.int32, like.shape, 0)

    def stacked(part):
        m2 = jnp.where(gy < 2, 0.0, far_above[:, part])
        p2 = jnp.where(gy > count - 3, 0.0, far_below[:, part])
        m1, p1, own = above(part), below(part), far[:, part]
        upper = sublanes(own) < 4

        def halves(x, y, second):
            if second:
                return jnp.where(upper, pltpu.roll(x, 4, axis=0), y)
            return jnp.where(upper, x, pltpu.roll(y, 4, axis=0))

        zero = jnp.zeros_like(own)
        return [
            jnp.concatenate([halves(m2, m1, s), halves(own, p1, s), halves(p2, zero, s)], axis=0)
            for s in (False, True)
        ]

    force = stacked(slice(0, LANES3))
    eta, beta = stacked(slice(LANES3, 2 * LANES3))
    right, left, under, over, cross_right, cross_left, diag = coefficients(eta, beta, from_below(eta), from_above)
    scale = OMEGA / diag
    field = [scale * force[0], scale * force[1]]
    for _ in range(5):
        downs = [from_below(x) for x in field]
        ups = [from_above(x) for x in field]
        steps = [downs[k] - ups[k] for k in range(2)]
        field = [
            KEEP * field[k]
            + scale
            * gather_terms(
                right, left, cross_right, cross_left, under, over, field[k], downs[k], ups[k], steps[1 - k], force[k]
            )
            for k in range(2)
        ]
    coarsest = []
    for k in range(2):
        a, b = pltpu.roll(field[k][0:8], 2, axis=0), pltpu.roll(field[k][8:16], 2, axis=0)
        coarsest.append(jnp.where(sublanes(a) < 2, a, b))
    at = 2 * LANES3
    for p in range(2):
        for target, own, start, shift in (
            (late_field, levels[2].field, at, 1),
            (late_force, levels[2].force, at + 768, 0),
        ):
            up, down = above(slice(start, start + 384)), below(slice(start, start + 384))
            for k in range(2):
                turn = 2 if k else 6
                a, b = pltpu.roll(up, turn, axis=0), pltpu.roll(down, turn, axis=0)
                sub = sublanes(a)
                target[k, p + shift] = jnp.where(sub < 2, a, jnp.where(sub < 6, own[k, p + shift], b))
        at += 384
    levels[2].force = late_force
    levels[2].field = late_field
    coarse = lambda k, p: coarsest[k]
    for level in (2, 1, 0):
        levels[level].last_sweeps(coarse, fields[level], others[level])
        coarse = lambda k, p, result=fields[level]: result[k, p + 1]
    for k in range(2):
        for i in range(COLS // 128):
            for p in range(8):
                part = fields[0][k, p + 1, :, 128 * i + EDGE : 128 * i + EDGE + 128]
                natural[i, pl.ds(p, 4, stride=8), :] = pltpu.roll(part, 6, axis=0)[0:4]
            velocity[k, :, 128 * i : 128 * i + 128] = natural[i]


def swap(x, axis, odd):
    count = lax.axis_size(axis)
    pairs = []
    for i in range(odd, count, 2):
        j = (i + 1) % count
        pairs += [(i, j), (j, i)]
    return lax.ppermute(x, axis, pairs)


def turn(x, axis, step):
    count = lax.axis_size(axis)
    return lax.ppermute(x, axis, [(i, (i + step) % count) for i in range(count)])


def local(forcing, ice_mask, viscosity_class, drag_class, viscosity_table, drag_table):
    smem = [pl.BlockSpec(memory_space=pltpu.SMEM)] * 2
    send_even, send_odd, coef = pl.pallas_call(
        lookup_kernel,
        out_shape=(shape(4, ROWS, EDGE), shape(4, ROWS, EDGE), shape(2, ROWS, COLS)),
        in_specs=smem + vmem(4),
        out_specs=vmem(3),
        compiler_params=params(),
        name="lookup",
    )(viscosity_table, drag_table, forcing, ice_mask, viscosity_class, drag_class)
    got_even = swap(send_even, "gx", 0)
    got_odd = swap(send_odd, "gx", 1)
    send_even, send_odd = pl.pallas_call(
        rows_kernel,
        out_shape=(shape(4, HALO, WIDE),) * 2,
        in_specs=vmem(4),
        out_specs=vmem(2),
        compiler_params=params(),
        name="rows",
    )(forcing, coef, got_even, got_odd)
    rows_even = swap(send_even, "gy", 0)
    rows_odd = swap(send_odd, "gy", 1)
    kept = [shape(*dims) for level in range(3) for dims in Level.shapes(level)]
    planes = [(PLANES[i], 8, LANES[i]) for i in range(3)]
    rims = [(2, PLANES[i] + 2, 8, LANES[i]) for i in range(3)]
    scratch = [pltpu.VMEM(dims, jnp.float32) for dims in [(WIDE // 128, 64, 128)] + planes * 3 + rims]
    near_lanes = 2 * LANES3 + 4 * LANES[2]
    *kept, near, far = pl.pallas_call(
        down_kernel,
        out_shape=tuple(kept) + (shape(8, near_lanes), shape(8, 2 * LANES3)),
        in_specs=vmem(6),
        out_specs=tuple(vmem(26)),
        scratch_shapes=scratch,
        compiler_params=params(),
        name="down",
    )(forcing, coef, got_even, got_odd, rows_even, rows_odd)
    near_even = swap(near, "gy", 0)
    near_odd = swap(near, "gy", 1)
    far_above = turn(far, "gy", 2)
    far_below = turn(far, "gy", -2)
    late = [(2, 2, 8, LANES[2]), (2, 4, 8, LANES[2])]
    scratch = [pltpu.VMEM(dims, jnp.float32) for dims in [(COLS // 128, ROWS, 128)] + late + rims + rims]
    return pl.pallas_call(
        up_kernel,
        out_shape=shape(2, ROWS, COLS),
        in_specs=vmem(29),
        out_specs=vmem(1)[0],
        scratch_shapes=scratch,
        compiler_params=params(),
        name="up",
    )(far, near_even, near_odd, far_above, far_below, *kept)


def solution(mesh):
    in_specs = (P(None, "gy", "gx"), P("gy", "gx"), P("gy", "gx"), P("gy", "gx"), P(), P())
    out_specs = P(None, "gy", "gx")
    return jax.shard_map(local, mesh=mesh, in_specs=in_specs, out_specs=out_specs, check_vma=False)
```

```python
import jax
import jax.numpy as jnp
from jax import lax
from jax.experimental import pallas as pl
from jax.experimental.pallas import tpu as pltpu
from jax.sharding import PartitionSpec as P

OMEGA = 0.6
KEEP = 1.0 - OMEGA
ROWS, COLS = 32, 1024
EDGE = 128
HALO = 16
WIDE = COLS + 2 * EDGE
PLANES = (8, 4, 2)
LANES = (1280, 640, 384)
LANES3 = 256
VMEM_LIMIT = 48 * 1024 * 1024


def vmem(count):
    return [pl.BlockSpec(memory_space=pltpu.VMEM)] * count


def params():
    return pltpu.CompilerParams(vmem_limit_bytes=VMEM_LIMIT)


def shape(*dims):
    return jax.ShapeDtypeStruct(dims, jnp.float32)


def from_left(x):
    return pltpu.roll(x, 1, axis=1)


def from_right(x):
    return pltpu.roll(x, x.shape[1] - 1, axis=1)


def from_above(x):
    return pltpu.roll(x, 1, axis=0)


def from_below(x):
    return pltpu.roll(x, x.shape[0] - 1, axis=0)


def tiles(x):
    return [x[:, i : i + 128] for i in range(0, x.shape[1], 128)]


def lane(kind):
    return lax.broadcasted_iota(jnp.int32, (8, 128), kind)


def pick(x, index):
    return jnp.take_along_axis(x, index, axis=1, mode="promise_in_bounds")


def halve_lanes(x, lanes):
    at = lane(1)
    index = 2 * (at % 64)
    parts = [pick(t + from_right(t), index) for t in tiles(x)]
    out = []
    for i in range(0, len(parts), 2):
        high = parts[i + 1] if i + 1 < len(parts) else jnp.zeros_like(parts[i])
        out.append(jnp.where(at < 64, parts[i], high))
    while len(out) * 128 < lanes:
        out.append(jnp.zeros_like(out[0]))
    return jnp.concatenate(out[: lanes // 128], axis=1)


def double_lanes(x, lanes):
    index = lane(1) // 2
    parts = tiles(x)
    return jnp.concatenate(
        [pick(parts[i // 2], index + 64 * (i % 2)) for i in range(lanes // 128)], axis=1
    )


def coefficients(eta, beta, eta_below, face_above):
    ice = eta > 0.0
    eta_right = from_right(eta)
    right = jnp.where(ice & (eta_right > 0.0), 0.5 * (eta + eta_right), 0.0)
    left = from_left(right)
    below = jnp.where(ice & (eta_below > 0.0), 0.5 * (eta + eta_below), 0.0)
    above = face_above(below)
    base = beta + jnp.where(ice, 0.0, 1.0)
    diag = base + ((right + left) + (below + above))
    return right, left, below, above, 0.05 * eta_right, 0.05 * from_left(eta), diag


def gather_terms(right, left, cross_right, cross_left, below, above, here, under, over, other_step, force):
    from_west = from_left(right * here + cross_right * other_step)
    from_east = from_right(left * here - cross_left * other_step)
    return (force + (from_west + from_east)) + (below * under + above * over)


class Level:
    def __init__(self, planes, refs):
        self.planes = planes
        self.right, self.left, self.cross_right, self.cross_left, self.below, self.scale, self.force, self.field = refs

    @staticmethod
    def shapes(level):
        planes, lanes = PLANES[level], LANES[level]
        one = [(planes, 8, lanes)] * 4 + [(planes + 1, 8, lanes), (planes, 8, lanes)]
        return one + [(2, planes, 8, lanes), (2, planes + 2, 8, lanes)]

    def wrap(self, field):
        for k in range(2):
            field[k, 0] = from_above(field[k, self.planes])
            field[k, self.planes + 1] = from_below(field[k, 1])

    def terms(self, p, field):
        out = []
        steps = [field[k, p + 2] - field[k, p] for k in range(2)]
        for k in range(2):
            out.append(
                gather_terms(
                    self.right[p],
                    self.left[p],
                    self.cross_right[p],
                    self.cross_left[p],
                    self.below[p + 1],
                    self.below[p],
                    field[k, p + 1],
                    field[k, p + 2],
                    field[k, p],
                    steps[1 - k],
                    self.force[k, p],
                )
            )
        return out

    def sweep(self, source, target):
        for p in range(self.planes):
            terms = self.terms(p, source)
            for k in range(2):
                target[k, p + 1] = KEEP * source[k, p + 1] + self.scale[p] * terms[k]

    def setup(self, eta, beta, diag):
        planes = self.planes
        for p in range(planes):
            here = eta[p]
            ice = here > 0.0
            next_eta = eta[p + 1] if p + 1 < planes else from_below(eta[0])
            self.below[p + 1] = jnp.where(ice & (next_eta > 0.0), 0.5 * (here + next_eta), 0.0)
        self.below[0] = from_above(self.below[planes])
        for p in range(planes):
            here = eta[p]
            ice = here > 0.0
            eta_right = from_right(here)
            right = jnp.where(ice & (eta_right > 0.0), 0.5 * (here + eta_right), 0.0)
            left = from_left(right)
            base = beta[p] + jnp.where(ice, 0.0, 1.0)
            total = base + ((right + left) + (self.below[p + 1] + self.below[p]))
            self.right[p] = right
            self.left[p] = left
            self.cross_right[p] = 0.05 * eta_right
            self.cross_left[p] = 0.05 * from_left(here)
            diag[p] = total
            self.scale[p] = OMEGA / total

    def first_sweeps(self, other):
        for k in range(2):
            for p in range(self.planes):
                other[k, p + 1] = self.scale[p] * self.force[k, p]
        self.wrap(other)
        self.sweep(other, self.field)
        self.wrap(self.field)

    def restrict(self, diag, target, lanes):
        for p in range(0, self.planes, 2):
            rest = [0.0, 0.0]
            for q in (p, p + 1):
                terms = self.terms(q, self.field)
                for k in range(2):
                    rest[k] = rest[k] + (terms[k] - diag[q] * self.field[k, q + 1])
            for k in range(2):
                target(k, p // 2, halve_lanes(rest[k], lanes))

    def last_sweeps(self, coarse, result, other):
        for k in range(2):
            for p in range(0, self.planes, 2):
                add = double_lanes(coarse(k, p // 2), self.field.shape[-1])
                result[k, p + 1] = self.field[k, p + 1] + add
                result[k, p + 2] = self.field[k, p + 2] + add
        self.wrap(result)
        self.sweep(result, other)
        self.wrap(other)
        self.sweep(other, result)


def halve_planes(source, target, planes, lanes, scale):
    for p in range(0, planes, 2):
        both = halve_lanes(source[p] + source[p + 1], lanes)
        target[p // 2] = scale * both if scale != 1.0 else both


def look_up(tables, classes, ice):
    at = lane(1)
    rows = []
    for table in tables:
        row = jnp.zeros((8, 128), jnp.float32)
        for i in range(16):
            row = jnp.where(at == i, table[i], row)
        rows.append(row)
    return [pick(row, part) * ice for row, part in zip(rows, classes)]


def start_all(pairs, sems):
    copies = [pltpu.make_async_copy(a, b, sems.at[i]) for i, (a, b) in enumerate(pairs)]
    for copy in copies:
        copy.start()
    return copies


def edge_kernel(v_table, d_table, forcing, mask, v_class, d_class, send_even, send_odd, tables, force, ints, sems):
    pairs = [(v_table, tables[0]), (d_table, tables[1])]
    for side, start in enumerate((0, COLS - EDGE)):
        cols = pl.ds(start, EDGE)
        pairs.append((forcing.at[:, :, cols], force.at[side]))
        for i, source in enumerate((mask, v_class, d_class)):
            pairs.append((source.at[:, cols], ints.at[side, i]))
    for copy in start_all(pairs, sems):
        copy.wait()
    even = lax.axis_index("gx") % 2 == 0
    for r in range(0, ROWS, 8):
        part = slice(r, r + 8)
        sides = []
        for side in range(2):
            ice = ints[side, 0, part].astype(jnp.float32)
            found = look_up(tables, [ints[side, 1, part], ints[side, 2, part]], ice)
            sides.append([force[side, 0, part], force[side, 1, part]] + found)
        for row in range(4):
            send_even[row, part] = jnp.where(even, sides[1][row], sides[0][row])
            send_odd[row, part] = jnp.where(even, sides[0][row], sides[1][row])


def row_starts():
    even = lax.axis_index("gy") % 2 == 0
    first = pl.multiple_of(jnp.where(even, ROWS - HALO, 0), HALO)
    return first, pl.multiple_of(ROWS - HALO - first, HALO)


def lookup_kernel(v_table, d_table, forcing, mask, v_class, d_class, after, coef, send_even, send_odd, tables, ints, sems):
    pairs = [(v_table, tables[0]), (d_table, tables[1])]
    pairs += [(source, ints.at[i]) for i, source in enumerate((mask, v_class, d_class))]
    starts = row_starts()
    for start, target in zip(starts, (send_even, send_odd)):
        pairs.append((forcing.at[:, pl.ds(start, HALO), :], target.at[0:2]))
    copies = start_all(pairs, sems)
    for copy in copies[:5]:
        copy.wait()
    for r in range(0, ROWS, 8):
        for c in range(0, COLS, 128):
            part = (slice(r, r + 8), slice(c, c + 128))
            ice = ints[(0,) + part].astype(jnp.float32)
            found = look_up(tables, [ints[(1,) + part], ints[(2,) + part]], ice)
            for k in range(2):
                coef[(k,) + part] = found[k]
    for copy in copies[5:]:
        copy.wait()
    for start, target in zip(starts, (send_even, send_odd)):
        for k in range(2):
            target[2 + k] = coef[k, pl.ds(start, HALO), :]


def side_columns(get_even, get_odd):
    gx = lax.axis_index("gx")
    even = gx % 2 == 0
    a, b = get_even, get_odd
    left = jnp.where(gx == 0, 0.0, jnp.where(even, b, a))
    right = jnp.where(gx == lax.axis_size("gx") - 1, 0.0, jnp.where(even, a, b))
    return left, right


def corner_kernel(got_even, got_odd, send_even, send_odd):
    for start, target in zip(row_starts(), (send_even, send_odd)):
        rows = pl.ds(start, HALO)
        for row in range(4):
            left, right = side_columns(got_even[row, rows], got_odd[row, rows])
            target[row, :, 0:EDGE] = left
            target[row, :, EDGE : 2 * EDGE] = right


def own_rows(a, b):
    upper = lax.broadcasted_iota(jnp.int32, a.shape, 0) < 4
    return jnp.where(upper, pltpu.roll(a, 6, axis=0), pltpu.roll(b, 2, axis=0))


def down_kernel(forcing, coef, got_even, got_odd, rows_even, rows_odd, corner_even, corner_odd, *refs):
    levels = [Level(PLANES[i], refs[8 * i : 8 * i + 8]) for i in range(3)]
    near, far = refs[24:26]
    natural = refs[26]
    etas, betas, diags, others = (refs[27 + 3 * i : 30 + 3 * i] for i in range(4))
    gy = lax.axis_index("gy")
    even = gy % 2 == 0
    first = gy == 0
    last = gy == lax.axis_size("gy") - 1
    for row in range(4):
        source = forcing if row < 2 else coef
        sides = side_columns(got_even[row], got_odd[row])
        for i in range(WIDE // 128):
            cols = slice(128 * i, 128 * i + 128)
            if 0 < i < WIDE // 128 - 1:
                inner = slice(128 * i - 128, 128 * i)
                a, b = rows_even[row, :, inner], rows_odd[row, :, inner]
            else:
                outer = slice(0, EDGE) if i == 0 else slice(EDGE, 2 * EDGE)
                a, b = corner_even[row, :, outer], corner_odd[row, :, outer]
            natural[i, 0:HALO] = jnp.where(first, 0.0, jnp.where(even, b, a))
            natural[i, HALO + ROWS :] = jnp.where(last, 0.0, jnp.where(even, a, b))
            if i == 0:
                own = sides[0]
            elif i == WIDE // 128 - 1:
                own = sides[1]
            else:
                own = source[row % 2, :, 128 * i - 128 : 128 * i]
            natural[i, HALO : HALO + ROWS] = own
            for p in range(8):
                plane = natural[i, pl.ds(p, 8, stride=8), :]
                if row < 2:
                    levels[0].force[row, p, :, cols] = plane
                else:
                    (etas, betas)[row - 2][0][p, :, cols] = plane
    for level in range(3):
        here = levels[level]
        here.setup(etas[level], betas[level], diags[level])
        here.first_sweeps(others[level])
        if level < 2:
            lanes = LANES[level + 1]
            halve_planes(etas[level], etas[level + 1], here.planes, lanes, 0.5)
            halve_planes(betas[level], betas[level + 1], here.planes, lanes, 1.0)

            def store(k, p, value, target=levels[level + 1].force):
                target[k, p] = value

            here.restrict(diags[level], store, lanes)
    found = [None, None]

    def keep(k, p, value):
        found[k] = value

    levels[2].restrict(diags[2], keep, LANES3)
    eta = 0.5 * halve_lanes(etas[2][0] + etas[2][1], LANES3)
    beta = halve_lanes(betas[2][0] + betas[2][1], LANES3)
    head = jnp.concatenate([own_rows(found[0], found[1]), own_rows(eta, beta)], axis=1)
    far[...] = head
    near[:, 0 : 2 * LANES3] = head
    at = 2 * LANES3
    for p in range(2):
        near[:, at : at + 384] = own_rows(levels[2].field[0, p + 1], levels[2].field[1, p + 1])
        near[:, at + 768 : at + 1152] = own_rows(levels[2].force[0, p], levels[2].force[1, p])
        at += 384


def up_kernel(far, near_even, near_odd, far_above, far_below, *refs):
    levels = [Level(PLANES[i], refs[8 * i : 8 * i + 8]) for i in range(3)]
    velocity, natural, late_force, late_field = refs[24:28]
    fields, others = refs[28:31], refs[31:34]
    gy = lax.axis_index("gy")
    count = lax.axis_size("gy")
    even = gy % 2 == 0

    def above(part):
        return jnp.where(gy == 0, 0.0, jnp.where(even, near_odd[:, part], near_even[:, part]))

    def below(part):
        return jnp.where(gy == count - 1, 0.0, jnp.where(even, near_even[:, part], near_odd[:, part]))

    def sublanes(like):
        return lax.broadcasted_iota(jnp.int32, like.shape, 0)

    def stacked(part):
        m2 = jnp.where(gy < 2, 0.0, far_above[:, part])
        p2 = jnp.where(gy > count - 3, 0.0, far_below[:, part])
        m1, p1, own = above(part), below(part), far[:, part]
        upper = sublanes(own) < 4

        def halves(x, y, second):
            if second:
                return jnp.where(upper, pltpu.roll(x, 4, axis=0), y)
            return jnp.where(upper, x, pltpu.roll(y, 4, axis=0))

        zero = jnp.zeros_like(own)
        return [
            jnp.concatenate([halves(m2, m1, s), halves(own, p1, s), halves(p2, zero, s)], axis=0)
            for s in (False, True)
        ]

    force = stacked(slice(0, LANES3))
    eta, beta = stacked(slice(LANES3, 2 * LANES3))
    right, left, under, over, cross_right, cross_left, diag = coefficients(eta, beta, from_below(eta), from_above)
    scale = OMEGA / diag
    field = [scale * force[0], scale * force[1]]
    for _ in range(5):
        downs = [from_below(x) for x in field]
        ups = [from_above(x) for x in field]
        steps = [downs[k] - ups[k] for k in range(2)]
        field = [
            KEEP * field[k]
            + scale
            * gather_terms(
                right, left, cross_right, cross_left, under, over, field[k], downs[k], ups[k], steps[1 - k], force[k]
            )
            for k in range(2)
        ]
    coarsest = []
    for k in range(2):
        a, b = pltpu.roll(field[k][0:8], 2, axis=0), pltpu.roll(field[k][8:16], 2, axis=0)
        coarsest.append(jnp.where(sublanes(a) < 2, a, b))
    at = 2 * LANES3
    for p in range(2):
        for target, own, start, shift in (
            (late_field, levels[2].field, at, 1),
            (late_force, levels[2].force, at + 768, 0),
        ):
            up, down = above(slice(start, start + 384)), below(slice(start, start + 384))
            for k in range(2):
                turn = 2 if k else 6
                a, b = pltpu.roll(up, turn, axis=0), pltpu.roll(down, turn, axis=0)
                sub = sublanes(a)
                target[k, p + shift] = jnp.where(sub < 2, a, jnp.where(sub < 6, own[k, p + shift], b))
        at += 384
    levels[2].force = late_force
    levels[2].field = late_field
    coarse = lambda k, p: coarsest[k]
    for level in (2, 1, 0):
        levels[level].last_sweeps(coarse, fields[level], others[level])
        coarse = lambda k, p, result=fields[level]: result[k, p + 1]
    for k in range(2):
        for i in range(COLS // 128):
            for p in range(8):
                part = fields[0][k, p + 1, :, 128 * i + EDGE : 128 * i + EDGE + 128]
                natural[i, pl.ds(p, 4, stride=8), :] = pltpu.roll(part, 6, axis=0)[0:4]
            velocity[k, :, 128 * i : 128 * i + 128] = natural[i]


def swap(x, axis, odd):
    count = lax.axis_size(axis)
    pairs = []
    for i in range(odd, count, 2):
        j = (i + 1) % count
        pairs += [(i, j), (j, i)]
    return lax.ppermute(x, axis, pairs)


def turn(x, axis, step):
    count = lax.axis_size(axis)
    return lax.ppermute(x, axis, [(i, (i + step) % count) for i in range(count)])


def local(forcing, ice_mask, viscosity_class, drag_class, viscosity_table, drag_table):
    inputs = [
        pltpu.with_memory_space_constraint(x, pltpu.HBM)
        for x in (viscosity_table, drag_table, forcing, ice_mask, viscosity_class, drag_class)
    ]
    hbm = [pl.BlockSpec(memory_space=pltpu.HBM)] * 6
    table = pltpu.SMEM((16,), jnp.float32)
    send_even, send_odd = pl.pallas_call(
        edge_kernel,
        out_shape=(shape(4, ROWS, EDGE),) * 2,
        in_specs=hbm,
        out_specs=tuple(vmem(2)),
        scratch_shapes=[
            [table, table],
            pltpu.VMEM((2, 2, ROWS, EDGE), jnp.float32),
            pltpu.VMEM((2, 3, ROWS, EDGE), jnp.int32),
            pltpu.SemaphoreType.DMA((10,)),
        ],
        compiler_params=params(),
        name="edges",
    )(*inputs)
    got_even = swap(send_even, "gx", 0)
    got_odd = swap(send_odd, "gx", 1)
    coef, send_even, send_odd = pl.pallas_call(
        lookup_kernel,
        out_shape=(shape(2, ROWS, COLS), shape(4, HALO, COLS), shape(4, HALO, COLS)),
        in_specs=hbm + [pl.BlockSpec(memory_space=pl.ANY)],
        out_specs=tuple(vmem(3)),
        scratch_shapes=[[table, table], pltpu.VMEM((3, ROWS, COLS), jnp.int32), pltpu.SemaphoreType.DMA((7,))],
        compiler_params=params(),
        name="lookup",
    )(*inputs, send_even)
    rows_even = swap(send_even, "gy", 0)
    rows_odd = swap(send_odd, "gy", 1)
    send_even, send_odd = pl.pallas_call(
        corner_kernel,
        out_shape=(shape(4, HALO, 2 * EDGE),) * 2,
        in_specs=vmem(2),
        out_specs=tuple(vmem(2)),
        compiler_params=params(),
        name="corners",
    )(got_even, got_odd)
    corner_even = swap(send_even, "gy", 0)
    corner_odd = swap(send_odd, "gy", 1)
    kept = [shape(*dims) for level in range(3) for dims in Level.shapes(level)]
    planes = [(PLANES[i], 8, LANES[i]) for i in range(3)]
    rims = [(2, PLANES[i] + 2, 8, LANES[i]) for i in range(3)]
    scratch = [pltpu.VMEM(dims, jnp.float32) for dims in [(WIDE // 128, 64, 128)] + planes * 3 + rims]
    near_lanes = 2 * LANES3 + 4 * LANES[2]
    *kept, near, far = pl.pallas_call(
        down_kernel,
        out_shape=tuple(kept) + (shape(8, near_lanes), shape(8, 2 * LANES3)),
        in_specs=vmem(8),
        out_specs=tuple(vmem(26)),
        scratch_shapes=scratch,
        compiler_params=params(),
        name="down",
    )(forcing, coef, got_even, got_odd, rows_even, rows_odd, corner_even, corner_odd)
    near_even = swap(near, "gy", 0)
    near_odd = swap(near, "gy", 1)
    far_above = turn(far, "gy", 2)
    far_below = turn(far, "gy", -2)
    late = [(2, 2, 8, LANES[2]), (2, 4, 8, LANES[2])]
    scratch = [pltpu.VMEM(dims, jnp.float32) for dims in [(COLS // 128, ROWS, 128)] + late + rims + rims]
    return pl.pallas_call(
        up_kernel,
        out_shape=shape(2, ROWS, COLS),
        in_specs=vmem(29),
        out_specs=vmem(1)[0],
        scratch_shapes=scratch,
        compiler_params=params(),
        name="up",
    )(far, near_even, near_odd, far_above, far_below, *kept)


def solution(mesh):
    in_specs = (P(None, "gy", "gx"), P("gy", "gx"), P("gy", "gx"), P("gy", "gx"), P(), P())
    out_specs = P(None, "gy", "gx")
    return jax.shard_map(local, mesh=mesh, in_specs=in_specs, out_specs=out_specs, check_vma=False)
```

```python
import jax
import jax.numpy as jnp
from jax import lax
from jax.experimental import pallas as pl
from jax.experimental.pallas import tpu as pltpu
from jax.sharding import PartitionSpec as P

OMEGA = 0.6
KEEP = 1.0 - OMEGA
ROWS, COLS = 32, 1024
EDGE = 128
HALO = 16
WIDE = COLS + 2 * EDGE
PLANES = (8, 4, 2)
LANES = (1280, 640, 384)
LANES3 = 256
VMEM_LIMIT = 48 * 1024 * 1024


def vmem(count):
    return [pl.BlockSpec(memory_space=pltpu.VMEM)] * count


def params():
    return pltpu.CompilerParams(vmem_limit_bytes=VMEM_LIMIT)


def shape(*dims):
    return jax.ShapeDtypeStruct(dims, jnp.float32)


def from_left(x):
    return pltpu.roll(x, 1, axis=1)


def from_right(x):
    return pltpu.roll(x, x.shape[1] - 1, axis=1)


def from_above(x):
    return pltpu.roll(x, 1, axis=0)


def from_below(x):
    return pltpu.roll(x, x.shape[0] - 1, axis=0)


def tiles(x):
    return [x[:, i : i + 128] for i in range(0, x.shape[1], 128)]


def lane(kind):
    return lax.broadcasted_iota(jnp.int32, (8, 128), kind)


def pick(x, index):
    return jnp.take_along_axis(x, index, axis=1, mode="promise_in_bounds")


def halve_lanes(x, lanes):
    at = lane(1)
    index = 2 * (at % 64)
    parts = [pick(t + from_right(t), index) for t in tiles(x)]
    out = []
    for i in range(0, len(parts), 2):
        high = parts[i + 1] if i + 1 < len(parts) else jnp.zeros_like(parts[i])
        out.append(jnp.where(at < 64, parts[i], high))
    while len(out) * 128 < lanes:
        out.append(jnp.zeros_like(out[0]))
    return jnp.concatenate(out[: lanes // 128], axis=1)


def double_lanes(x, lanes):
    index = lane(1) // 2
    parts = tiles(x)
    return jnp.concatenate(
        [pick(parts[i // 2], index + 64 * (i % 2)) for i in range(lanes // 128)], axis=1
    )


def coefficients(eta, beta, eta_below, face_above):
    ice = eta > 0.0
    eta_right = from_right(eta)
    right = jnp.where(ice & (eta_right > 0.0), 0.5 * (eta + eta_right), 0.0)
    left = from_left(right)
    below = jnp.where(ice & (eta_below > 0.0), 0.5 * (eta + eta_below), 0.0)
    above = face_above(below)
    base = beta + jnp.where(ice, 0.0, 1.0)
    diag = base + ((right + left) + (below + above))
    return right, left, below, above, 0.05 * eta_right, 0.05 * from_left(eta), diag


def gather_terms(right, left, cross_right, cross_left, below, above, here, under, over, other_step, force):
    from_west = from_left(right * here + cross_right * other_step)
    from_east = from_right(left * here - cross_left * other_step)
    return (force + (from_west + from_east)) + (below * under + above * over)


class Level:
    def __init__(self, planes, refs):
        self.planes = planes
        self.right, self.left, self.cross_right, self.cross_left, self.below, self.scale, self.force, self.field = refs

    @staticmethod
    def shapes(level):
        planes, lanes = PLANES[level], LANES[level]
        one = [(planes, 8, lanes)] * 4 + [(planes + 1, 8, lanes), (planes, 8, lanes)]
        return one + [(2, planes, 8, lanes), (2, planes + 2, 8, lanes)]

    def wrap(self, field):
        for k in range(2):
            field[k, 0] = from_above(field[k, self.planes])
            field[k, self.planes + 1] = from_below(field[k, 1])

    def terms(self, p, field):
        out = []
        steps = [field[k, p + 2] - field[k, p] for k in range(2)]
        for k in range(2):
            out.append(
                gather_terms(
                    self.right[p],
                    self.left[p],
                    self.cross_right[p],
                    self.cross_left[p],
                    self.below[p + 1],
                    self.below[p],
                    field[k, p + 1],
                    field[k, p + 2],
                    field[k, p],
                    steps[1 - k],
                    self.force[k, p],
                )
            )
        return out

    def sweep(self, source, target):
        for p in range(self.planes):
            terms = self.terms(p, source)
            for k in range(2):
                target[k, p + 1] = KEEP * source[k, p + 1] + self.scale[p] * terms[k]

    def setup(self, eta, beta, diag):
        planes = self.planes
        for p in range(planes):
            here = eta[p]
            ice = here > 0.0
            next_eta = eta[p + 1] if p + 1 < planes else from_below(eta[0])
            self.below[p + 1] = jnp.where(ice & (next_eta > 0.0), 0.5 * (here + next_eta), 0.0)
        self.below[0] = from_above(self.below[planes])
        for p in range(planes):
            here = eta[p]
            ice = here > 0.0
            eta_right = from_right(here)
            right = jnp.where(ice & (eta_right > 0.0), 0.5 * (here + eta_right), 0.0)
            left = from_left(right)
            base = beta[p] + jnp.where(ice, 0.0, 1.0)
            total = base + ((right + left) + (self.below[p + 1] + self.below[p]))
            self.right[p] = right
            self.left[p] = left
            self.cross_right[p] = 0.05 * eta_right
            self.cross_left[p] = 0.05 * from_left(here)
            diag[p] = total
            self.scale[p] = OMEGA / total

    def first_sweeps(self, other):
        for k in range(2):
            for p in range(self.planes):
                other[k, p + 1] = self.scale[p] * self.force[k, p]
        self.wrap(other)
        self.sweep(other, self.field)
        self.wrap(self.field)

    def restrict(self, diag, target, lanes):
        for p in range(0, self.planes, 2):
            rest = [0.0, 0.0]
            for q in (p, p + 1):
                terms = self.terms(q, self.field)
                for k in range(2):
                    rest[k] = rest[k] + (terms[k] - diag[q] * self.field[k, q + 1])
            for k in range(2):
                target(k, p // 2, halve_lanes(rest[k], lanes))

    def last_sweeps(self, coarse, result, other):
        for k in range(2):
            for p in range(0, self.planes, 2):
                add = double_lanes(coarse(k, p // 2), self.field.shape[-1])
                result[k, p + 1] = self.field[k, p + 1] + add
                result[k, p + 2] = self.field[k, p + 2] + add
        self.wrap(result)
        self.sweep(result, other)
        self.wrap(other)
        self.sweep(other, result)


def halve_planes(source, target, planes, lanes, scale):
    for p in range(0, planes, 2):
        both = halve_lanes(source[p] + source[p + 1], lanes)
        target[p // 2] = scale * both if scale != 1.0 else both


def look_up(tables, classes, ice):
    at = lane(1)
    rows = []
    for table in tables:
        row = jnp.zeros((8, 128), jnp.float32)
        for i in range(16):
            row = jnp.where(at == i, table[i], row)
        rows.append(row)
    return [pick(row, part) * ice for row, part in zip(rows, classes)]


def start_all(pairs, sems):
    copies = [pltpu.make_async_copy(a, b, sems.at[i]) for i, (a, b) in enumerate(pairs)]
    for copy in copies:
        copy.start()
    return copies


def edge_kernel(v_table, d_table, forcing, mask, v_class, d_class, send_even, send_odd, tables, force, ints, sems):
    pairs = [(v_table, tables[0]), (d_table, tables[1])]
    for side, start in enumerate((0, COLS - EDGE)):
        cols = pl.ds(start, EDGE)
        pairs.append((forcing.at[:, :, cols], force.at[side]))
        for i, source in enumerate((mask, v_class, d_class)):
            pairs.append((source.at[:, cols], ints.at[side, i]))
    for copy in start_all(pairs, sems):
        copy.wait()
    even = lax.axis_index("gx") % 2 == 0
    for r in range(0, ROWS, 8):
        part = slice(r, r + 8)
        sides = []
        for side in range(2):
            ice = ints[side, 0, part].astype(jnp.float32)
            found = look_up(tables, [ints[side, 1, part], ints[side, 2, part]], ice)
            sides.append([force[side, 0, part], force[side, 1, part]] + found)
        for row in range(4):
            send_even[row, part] = jnp.where(even, sides[1][row], sides[0][row])
            send_odd[row, part] = jnp.where(even, sides[0][row], sides[1][row])


def row_starts():
    even = lax.axis_index("gy") % 2 == 0
    first = pl.multiple_of(jnp.where(even, ROWS - HALO, 0), HALO)
    return first, pl.multiple_of(ROWS - HALO - first, HALO)


def lookup_kernel(v_table, d_table, forcing, mask, v_class, d_class, after, coef, send_even, send_odd, tables, ints, sems):
    pairs = [(v_table, tables[0]), (d_table, tables[1])]
    pairs += [(source, ints.at[i]) for i, source in enumerate((mask, v_class, d_class))]
    starts = row_starts()
    for start, target in zip(starts, (send_even, send_odd)):
        pairs.append((forcing.at[:, pl.ds(start, HALO), :], target.at[0:2]))
    copies = start_all(pairs, sems)
    for copy in copies[:5]:
        copy.wait()
    for r in range(0, ROWS, 8):
        for c in range(0, COLS, 128):
            part = (slice(r, r + 8), slice(c, c + 128))
            ice = ints[(0,) + part].astype(jnp.float32)
            found = look_up(tables, [ints[(1,) + part], ints[(2,) + part]], ice)
            for k in range(2):
                coef[(k,) + part] = found[k]
    for copy in copies[5:]:
        copy.wait()
    for start, target in zip(starts, (send_even, send_odd)):
        for k in range(2):
            target[2 + k] = coef[k, pl.ds(start, HALO), :]


def side_columns(get_even, get_odd):
    gx = lax.axis_index("gx")
    even = gx % 2 == 0
    a, b = get_even, get_odd
    left = jnp.where(gx == 0, 0.0, jnp.where(even, b, a))
    right = jnp.where(gx == lax.axis_size("gx") - 1, 0.0, jnp.where(even, a, b))
    return left, right


def corner_kernel(got_even, got_odd, send_even, send_odd):
    for start, target in zip(row_starts(), (send_even, send_odd)):
        rows = pl.ds(start, HALO)
        for row in range(4):
            left, right = side_columns(got_even[row, rows], got_odd[row, rows])
            target[row, :, 0:EDGE] = left
            target[row, :, EDGE : 2 * EDGE] = right


def own_rows(a, b):
    upper = lax.broadcasted_iota(jnp.int32, a.shape, 0) < 4
    return jnp.where(upper, pltpu.roll(a, 6, axis=0), pltpu.roll(b, 2, axis=0))


def down_kernel(forcing, coef, got_even, got_odd, rows_even, rows_odd, corner_even, corner_odd, *refs):
    levels = [Level(PLANES[i], refs[8 * i : 8 * i + 8]) for i in range(3)]
    near, far = refs[24:26]
    natural = refs[26]
    etas, betas, diags, others = (refs[27 + 3 * i : 30 + 3 * i] for i in range(4))
    gy = lax.axis_index("gy")
    even = gy % 2 == 0
    first = gy == 0
    last = gy == lax.axis_size("gy") - 1
    for row in range(4):
        source = forcing if row < 2 else coef
        sides = side_columns(got_even[row], got_odd[row])
        for i in range(WIDE // 128):
            cols = slice(128 * i, 128 * i + 128)
            if 0 < i < WIDE // 128 - 1:
                inner = slice(128 * i - 128, 128 * i)
                a, b = rows_even[row, :, inner], rows_odd[row, :, inner]
            else:
                outer = slice(0, EDGE) if i == 0 else slice(EDGE, 2 * EDGE)
                a, b = corner_even[row, :, outer], corner_odd[row, :, outer]
            natural[i, 0:HALO] = jnp.where(first, 0.0, jnp.where(even, b, a))
            natural[i, HALO + ROWS :] = jnp.where(last, 0.0, jnp.where(even, a, b))
            if i == 0:
                own = sides[0]
            elif i == WIDE // 128 - 1:
                own = sides[1]
            else:
                own = source[row % 2, :, 128 * i - 128 : 128 * i]
            natural[i, HALO : HALO + ROWS] = own
            for p in range(8):
                plane = natural[i, pl.ds(p, 8, stride=8), :]
                if row < 2:
                    levels[0].force[row, p, :, cols] = plane
                else:
                    (etas, betas)[row - 2][0][p, :, cols] = plane
    for level in range(3):
        here = levels[level]
        here.setup(etas[level], betas[level], diags[level])
        here.first_sweeps(others[level])
        if level < 2:
            lanes = LANES[level + 1]
            halve_planes(etas[level], etas[level + 1], here.planes, lanes, 0.5)
            halve_planes(betas[level], betas[level + 1], here.planes, lanes, 1.0)

            def store(k, p, value, target=levels[level + 1].force):
                target[k, p] = value

            here.restrict(diags[level], store, lanes)
    found = [None, None]

    def keep(k, p, value):
        found[k] = value

    levels[2].restrict(diags[2], keep, LANES3)
    eta = 0.5 * halve_lanes(etas[2][0] + etas[2][1], LANES3)
    beta = halve_lanes(betas[2][0] + betas[2][1], LANES3)
    head = jnp.concatenate([own_rows(found[0], found[1]), own_rows(eta, beta)], axis=1)
    far[...] = head
    near[:, 0 : 2 * LANES3] = head
    at = 2 * LANES3
    for p in range(2):
        near[:, at : at + 384] = own_rows(levels[2].field[0, p + 1], levels[2].field[1, p + 1])
        near[:, at + 768 : at + 1152] = own_rows(levels[2].force[0, p], levels[2].force[1, p])
        at += 384


def up_kernel(far, near_even, near_odd, far_above, far_below, *refs):
    levels = [Level(PLANES[i], refs[8 * i : 8 * i + 8]) for i in range(3)]
    velocity, natural, late_force, late_field = refs[24:28]
    fields, others = refs[28:31], refs[31:34]
    gy = lax.axis_index("gy")
    count = lax.axis_size("gy")
    even = gy % 2 == 0

    def above(part):
        return jnp.where(gy == 0, 0.0, jnp.where(even, near_odd[:, part], near_even[:, part]))

    def below(part):
        return jnp.where(gy == count - 1, 0.0, jnp.where(even, near_even[:, part], near_odd[:, part]))

    def sublanes(like):
        return lax.broadcasted_iota(jnp.int32, like.shape, 0)

    def stacked(part):
        m2 = jnp.where(gy < 2, 0.0, far_above[:, part])
        p2 = jnp.where(gy > count - 3, 0.0, far_below[:, part])
        m1, p1, own = above(part), below(part), far[:, part]
        upper = sublanes(own) < 4

        def halves(x, y, second):
            if second:
                return jnp.where(upper, pltpu.roll(x, 4, axis=0), y)
            return jnp.where(upper, x, pltpu.roll(y, 4, axis=0))

        zero = jnp.zeros_like(own)
        return [
            jnp.concatenate([halves(m2, m1, s), halves(own, p1, s), halves(p2, zero, s)], axis=0)
            for s in (False, True)
        ]

    force = stacked(slice(0, LANES3))
    eta, beta = stacked(slice(LANES3, 2 * LANES3))
    right, left, under, over, cross_right, cross_left, diag = coefficients(eta, beta, from_below(eta), from_above)
    scale = OMEGA / diag
    field = [scale * force[0], scale * force[1]]
    for _ in range(5):
        downs = [from_below(x) for x in field]
        ups = [from_above(x) for x in field]
        steps = [downs[k] - ups[k] for k in range(2)]
        field = [
            KEEP * field[k]
            + scale
            * gather_terms(
                right, left, cross_right, cross_left, under, over, field[k], downs[k], ups[k], steps[1 - k], force[k]
            )
            for k in range(2)
        ]
    coarsest = []
    for k in range(2):
        a, b = pltpu.roll(field[k][0:8], 2, axis=0), pltpu.roll(field[k][8:16], 2, axis=0)
        coarsest.append(jnp.where(sublanes(a) < 2, a, b))
    at = 2 * LANES3
    for p in range(2):
        for target, own, start, shift in (
            (late_field, levels[2].field, at, 1),
            (late_force, levels[2].force, at + 768, 0),
        ):
            up, down = above(slice(start, start + 384)), below(slice(start, start + 384))
            for k in range(2):
                turn = 2 if k else 6
                a, b = pltpu.roll(up, turn, axis=0), pltpu.roll(down, turn, axis=0)
                sub = sublanes(a)
                target[k, p + shift] = jnp.where(sub < 2, a, jnp.where(sub < 6, own[k, p + shift], b))
        at += 384
    levels[2].force = late_force
    levels[2].field = late_field
    coarse = lambda k, p: coarsest[k]
    for level in (2, 1, 0):
        levels[level].last_sweeps(coarse, fields[level], others[level])
        coarse = lambda k, p, result=fields[level]: result[k, p + 1]
    for k in range(2):
        for i in range(COLS // 128):
            for p in range(8):
                part = fields[0][k, p + 1, :, 128 * i + EDGE : 128 * i + EDGE + 128]
                natural[i, pl.ds(p, 4, stride=8), :] = pltpu.roll(part, 6, axis=0)[0:4]
            velocity[k, :, 128 * i : 128 * i + 128] = natural[i]


def swap(x, axis, odd):
    rows, cols = lax.axis_size("gy"), lax.axis_size("gx")
    count, across = (rows, cols) if axis == "gy" else (cols, rows)
    pairs = []
    for j in range(across):
        for i in range(odd, count - 1, 2):
            pairs += [((i, j), (i + 1, j)), ((i + 1, j), (i, j))]
        if odd and axis == "gy":
            pairs += [((0, j), (count - 1, j)), ((count - 1, j), (0, j))]
        elif odd:
            pairs += [((i, j), (i, j ^ 1)) for i in (0, count - 1)]
    place = (lambda i, j: j * rows + i) if axis == "gy" else (lambda i, j: i * rows + j)
    return lax.ppermute(x, ("gx", "gy"), [(place(*a), place(*b)) for a, b in pairs])


def turn(x, axis, step):
    count = lax.axis_size(axis)
    return lax.ppermute(x, axis, [(i, (i + step) % count) for i in range(count)])


def local(forcing, ice_mask, viscosity_class, drag_class, viscosity_table, drag_table):
    inputs = [
        pltpu.with_memory_space_constraint(x, pltpu.HBM)
        for x in (viscosity_table, drag_table, forcing, ice_mask, viscosity_class, drag_class)
    ]
    hbm = [pl.BlockSpec(memory_space=pltpu.HBM)] * 6
    table = pltpu.SMEM((16,), jnp.float32)
    send_even, send_odd = pl.pallas_call(
        edge_kernel,
        out_shape=(shape(4, ROWS, EDGE),) * 2,
        in_specs=hbm,
        out_specs=tuple(vmem(2)),
        scratch_shapes=[
            [table, table],
            pltpu.VMEM((2, 2, ROWS, EDGE), jnp.float32),
            pltpu.VMEM((2, 3, ROWS, EDGE), jnp.int32),
            pltpu.SemaphoreType.DMA((10,)),
        ],
        compiler_params=params(),
        name="edges",
    )(*inputs)
    got_even = swap(send_even, "gx", 0)
    got_odd = swap(send_odd, "gx", 1)
    coef, send_even, send_odd = pl.pallas_call(
        lookup_kernel,
        out_shape=(shape(2, ROWS, COLS), shape(4, HALO, COLS), shape(4, HALO, COLS)),
        in_specs=hbm + [pl.BlockSpec(memory_space=pl.ANY)],
        out_specs=tuple(vmem(3)),
        scratch_shapes=[[table, table], pltpu.VMEM((3, ROWS, COLS), jnp.int32), pltpu.SemaphoreType.DMA((7,))],
        compiler_params=params(),
        cost_estimate=pl.CostEstimate(flops=1 << 22, bytes_accessed=8 << 20, transcendentals=0),
        name="lookup",
    )(*inputs, send_even)
    rows_even = swap(send_even, "gy", 0)
    rows_odd = swap(send_odd, "gy", 1)
    send_even, send_odd = pl.pallas_call(
        corner_kernel,
        out_shape=(shape(4, HALO, 2 * EDGE),) * 2,
        in_specs=vmem(2),
        out_specs=tuple(vmem(2)),
        compiler_params=params(),
        name="corners",
    )(got_even, got_odd)
    corner_even = swap(send_even, "gy", 0)
    corner_odd = swap(send_odd, "gy", 1)
    kept = [shape(*dims) for level in range(3) for dims in Level.shapes(level)]
    planes = [(PLANES[i], 8, LANES[i]) for i in range(3)]
    rims = [(2, PLANES[i] + 2, 8, LANES[i]) for i in range(3)]
    scratch = [pltpu.VMEM(dims, jnp.float32) for dims in [(WIDE // 128, 64, 128)] + planes * 3 + rims]
    near_lanes = 2 * LANES3 + 4 * LANES[2]
    *kept, near, far = pl.pallas_call(
        down_kernel,
        out_shape=tuple(kept) + (shape(8, near_lanes), shape(8, 2 * LANES3)),
        in_specs=vmem(8),
        out_specs=tuple(vmem(26)),
        scratch_shapes=scratch,
        compiler_params=params(),
        name="down",
    )(forcing, coef, got_even, got_odd, rows_even, rows_odd, corner_even, corner_odd)
    near_even = swap(near, "gy", 0)
    near_odd = swap(near, "gy", 1)
    far_above = turn(far, "gy", 2)
    far_below = turn(far, "gy", -2)
    late = [(2, 2, 8, LANES[2]), (2, 4, 8, LANES[2])]
    scratch = [pltpu.VMEM(dims, jnp.float32) for dims in [(COLS // 128, ROWS, 128)] + late + rims + rims]
    return pl.pallas_call(
        up_kernel,
        out_shape=shape(2, ROWS, COLS),
        in_specs=vmem(29),
        out_specs=vmem(1)[0],
        scratch_shapes=scratch,
        compiler_params=params(),
        name="up",
    )(far, near_even, near_odd, far_above, far_below, *kept)


def solution(mesh):
    in_specs = (P(None, "gy", "gx"), P("gy", "gx"), P("gy", "gx"), P("gy", "gx"), P(), P())
    out_specs = P(None, "gy", "gx")
    return jax.shard_map(local, mesh=mesh, in_specs=in_specs, out_specs=out_specs, check_vma=False)
```

```python
import jax
import jax.numpy as jnp
from jax import lax
from jax.experimental import pallas as pl
from jax.experimental.pallas import tpu as pltpu
from jax.sharding import PartitionSpec as P

OMEGA = 0.6
KEEP = 1.0 - OMEGA
ROWS, COLS = 32, 1024
EDGE = 128
HALO = 16
WIDE = COLS + 2 * EDGE
PLANES = (8, 4, 2)
LANES = (1280, 640, 384)
LANES3 = 256
VMEM_LIMIT = 48 * 1024 * 1024


def vmem(count):
    return [pl.BlockSpec(memory_space=pltpu.VMEM)] * count


def params():
    return pltpu.CompilerParams(vmem_limit_bytes=VMEM_LIMIT)


def shape(*dims):
    return jax.ShapeDtypeStruct(dims, jnp.float32)


def from_left(x):
    return pltpu.roll(x, 1, axis=1)


def from_right(x):
    return pltpu.roll(x, x.shape[1] - 1, axis=1)


def from_above(x):
    return pltpu.roll(x, 1, axis=0)


def from_below(x):
    return pltpu.roll(x, x.shape[0] - 1, axis=0)


def tiles(x):
    return [x[:, i : i + 128] for i in range(0, x.shape[1], 128)]


def lane(kind):
    return lax.broadcasted_iota(jnp.int32, (8, 128), kind)


def pick(x, index):
    return jnp.take_along_axis(x, index, axis=1, mode="promise_in_bounds")


def halve_lanes(x, lanes):
    at = lane(1)
    index = 2 * (at % 64)
    parts = [pick(t + from_right(t), index) for t in tiles(x)]
    out = []
    for i in range(0, len(parts), 2):
        high = parts[i + 1] if i + 1 < len(parts) else jnp.zeros_like(parts[i])
        out.append(jnp.where(at < 64, parts[i], high))
    while len(out) * 128 < lanes:
        out.append(jnp.zeros_like(out[0]))
    return jnp.concatenate(out[: lanes // 128], axis=1)


def double_lanes(x, lanes):
    index = lane(1) // 2
    parts = tiles(x)
    return jnp.concatenate(
        [pick(parts[i // 2], index + 64 * (i % 2)) for i in range(lanes // 128)], axis=1
    )


def coefficients(eta, beta, eta_below, face_above):
    ice = eta > 0.0
    eta_right = from_right(eta)
    right = jnp.where(ice & (eta_right > 0.0), 0.5 * (eta + eta_right), 0.0)
    left = from_left(right)
    below = jnp.where(ice & (eta_below > 0.0), 0.5 * (eta + eta_below), 0.0)
    above = face_above(below)
    base = beta + jnp.where(ice, 0.0, 1.0)
    diag = base + ((right + left) + (below + above))
    return right, left, below, above, 0.05 * eta_right, 0.05 * from_left(eta), diag


def gather_terms(right, left, cross_right, cross_left, below, above, here, under, over, other_step, force):
    from_west = from_left(right * here + cross_right * other_step)
    from_east = from_right(left * here - cross_left * other_step)
    return (force + (from_west + from_east)) + (below * under + above * over)


class Level:
    def __init__(self, planes, refs):
        self.planes = planes
        self.right, self.left, self.cross_right, self.cross_left, self.below, self.scale, self.force, self.field = refs

    @staticmethod
    def shapes(level):
        planes, lanes = PLANES[level], LANES[level]
        one = [(planes, 8, lanes)] * 4 + [(planes + 1, 8, lanes), (planes, 8, lanes)]
        return one + [(2, planes, 8, lanes), (2, planes + 2, 8, lanes)]

    def wrap(self, field):
        for k in range(2):
            field[k, 0] = from_above(field[k, self.planes])
            field[k, self.planes + 1] = from_below(field[k, 1])

    def terms(self, p, field):
        out = []
        steps = [field[k, p + 2] - field[k, p] for k in range(2)]
        for k in range(2):
            out.append(
                gather_terms(
                    self.right[p],
                    self.left[p],
                    self.cross_right[p],
                    self.cross_left[p],
                    self.below[p + 1],
                    self.below[p],
                    field[k, p + 1],
                    field[k, p + 2],
                    field[k, p],
                    steps[1 - k],
                    self.force[k, p],
                )
            )
        return out

    def sweep(self, source, target):
        for p in range(self.planes):
            terms = self.terms(p, source)
            for k in range(2):
                target[k, p + 1] = KEEP * source[k, p + 1] + self.scale[p] * terms[k]

    def setup(self, eta, beta, diag):
        planes = self.planes
        for p in range(planes):
            here = eta[p]
            ice = here > 0.0
            next_eta = eta[p + 1] if p + 1 < planes else from_below(eta[0])
            self.below[p + 1] = jnp.where(ice & (next_eta > 0.0), 0.5 * (here + next_eta), 0.0)
        self.below[0] = from_above(self.below[planes])
        for p in range(planes):
            here = eta[p]
            ice = here > 0.0
            eta_right = from_right(here)
            right = jnp.where(ice & (eta_right > 0.0), 0.5 * (here + eta_right), 0.0)
            left = from_left(right)
            base = beta[p] + jnp.where(ice, 0.0, 1.0)
            total = base + ((right + left) + (self.below[p + 1] + self.below[p]))
            self.right[p] = right
            self.left[p] = left
            self.cross_right[p] = 0.05 * eta_right
            self.cross_left[p] = 0.05 * from_left(here)
            diag[p] = total
            self.scale[p] = OMEGA / total

    def first_sweeps(self, other):
        for k in range(2):
            for p in range(self.planes):
                other[k, p + 1] = self.scale[p] * self.force[k, p]
        self.wrap(other)
        self.sweep(other, self.field)
        self.wrap(self.field)

    def restrict(self, diag, target, lanes):
        for p in range(0, self.planes, 2):
            rest = [0.0, 0.0]
            for q in (p, p + 1):
                terms = self.terms(q, self.field)
                for k in range(2):
                    rest[k] = rest[k] + (terms[k] - diag[q] * self.field[k, q + 1])
            for k in range(2):
                target(k, p // 2, halve_lanes(rest[k], lanes))

    def last_sweeps(self, coarse, result, other):
        for k in range(2):
            for p in range(0, self.planes, 2):
                add = double_lanes(coarse(k, p // 2), self.field.shape[-1])
                result[k, p + 1] = self.field[k, p + 1] + add
                result[k, p + 2] = self.field[k, p + 2] + add
        self.wrap(result)
        self.sweep(result, other)
        self.wrap(other)
        self.sweep(other, result)


def halve_planes(source, target, planes, lanes, scale):
    for p in range(0, planes, 2):
        both = halve_lanes(source[p] + source[p + 1], lanes)
        target[p // 2] = scale * both if scale != 1.0 else both


def look_up(tables, classes, ice):
    at = lane(1)
    rows = []
    for table in tables:
        row = jnp.zeros((8, 128), jnp.float32)
        for i in range(16):
            row = jnp.where(at == i, table[i], row)
        rows.append(row)
    return [pick(row, part) * ice for row, part in zip(rows, classes)]


def start_all(pairs, sems):
    copies = [pltpu.make_async_copy(a, b, sems.at[i]) for i, (a, b) in enumerate(pairs)]
    for copy in copies:
        copy.start()
    return copies


def halves_of(axis, size, part):
    even = lax.axis_index(axis) % 2 == 0
    first = pl.multiple_of(jnp.where(even, size - part, 0), part)
    return first, pl.multiple_of(size - part - first, part)


def lookup_kernel(v_table, d_table, forcing, mask, v_class, d_class, coef, *refs):
    sides, rows = refs[0:2], refs[2:4]
    tables, ints, sems = refs[4:]
    pairs = [(v_table, tables[0]), (d_table, tables[1])]
    pairs += [(source, ints.at[i]) for i, source in enumerate((mask, v_class, d_class))]
    side_starts = halves_of("gx", COLS, EDGE)
    row_starts = halves_of("gy", ROWS, HALO)
    for start, target in zip(side_starts, sides):
        pairs.append((forcing.at[:, :, pl.ds(start, EDGE)], target.at[0:2]))
    for start, target in zip(row_starts, rows):
        pairs.append((forcing.at[:, pl.ds(start, HALO), :], target.at[0:2]))
    copies = start_all(pairs, sems)
    for copy in copies[:5]:
        copy.wait()
    for r in range(0, ROWS, 8):
        for c in range(0, COLS, 128):
            part = (slice(r, r + 8), slice(c, c + 128))
            ice = ints[(0,) + part].astype(jnp.float32)
            found = look_up(tables, [ints[(1,) + part], ints[(2,) + part]], ice)
            for k in range(2):
                coef[(k,) + part] = found[k]
    for k in range(2):
        for start, target in zip(side_starts, sides):
            target[2 + k] = coef[k, :, pl.ds(start, EDGE)]
        for start, target in zip(row_starts, rows):
            target[2 + k] = coef[k, pl.ds(start, HALO), :]
    for copy in copies[5:]:
        copy.wait()


def side_columns(get_even, get_odd):
    gx = lax.axis_index("gx")
    even = gx % 2 == 0
    a, b = get_even, get_odd
    left = jnp.where(gx == 0, 0.0, jnp.where(even, b, a))
    right = jnp.where(gx == lax.axis_size("gx") - 1, 0.0, jnp.where(even, a, b))
    return left, right


def corner_kernel(got_even, got_odd, send_even, send_odd):
    for start, target in zip(halves_of("gy", ROWS, HALO), (send_even, send_odd)):
        rows = pl.ds(start, HALO)
        for row in range(4):
            left, right = side_columns(got_even[row, rows], got_odd[row, rows])
            target[row, :, 0:EDGE] = left
            target[row, :, EDGE : 2 * EDGE] = right


def own_rows(a, b):
    upper = lax.broadcasted_iota(jnp.int32, a.shape, 0) < 4
    return jnp.where(upper, pltpu.roll(a, 6, axis=0), pltpu.roll(b, 2, axis=0))


def down_kernel(forcing, coef, got_even, got_odd, rows_even, rows_odd, corner_even, corner_odd, *refs):
    levels = [Level(PLANES[i], refs[8 * i : 8 * i + 8]) for i in range(3)]
    near, far = refs[24:26]
    natural = refs[26]
    etas, betas, diags, others = (refs[27 + 3 * i : 30 + 3 * i] for i in range(4))
    gy = lax.axis_index("gy")
    even = gy % 2 == 0
    first = gy == 0
    last = gy == lax.axis_size("gy") - 1
    for row in range(4):
        source = forcing if row < 2 else coef
        sides = side_columns(got_even[row], got_odd[row])
        for i in range(WIDE // 128):
            cols = slice(128 * i, 128 * i + 128)
            if 0 < i < WIDE // 128 - 1:
                inner = slice(128 * i - 128, 128 * i)
                a, b = rows_even[row, :, inner], rows_odd[row, :, inner]
            else:
                outer = slice(0, EDGE) if i == 0 else slice(EDGE, 2 * EDGE)
                a, b = corner_even[row, :, outer], corner_odd[row, :, outer]
            natural[i, 0:HALO] = jnp.where(first, 0.0, jnp.where(even, b, a))
            natural[i, HALO + ROWS :] = jnp.where(last, 0.0, jnp.where(even, a, b))
            if i == 0:
                own = sides[0]
            elif i == WIDE // 128 - 1:
                own = sides[1]
            else:
                own = source[row % 2, :, 128 * i - 128 : 128 * i]
            natural[i, HALO : HALO + ROWS] = own
            for p in range(8):
                plane = natural[i, pl.ds(p, 8, stride=8), :]
                if row < 2:
                    levels[0].force[row, p, :, cols] = plane
                else:
                    (etas, betas)[row - 2][0][p, :, cols] = plane
    for level in range(3):
        here = levels[level]
        here.setup(etas[level], betas[level], diags[level])
        here.first_sweeps(others[level])
        if level < 2:
            lanes = LANES[level + 1]
            halve_planes(etas[level], etas[level + 1], here.planes, lanes, 0.5)
            halve_planes(betas[level], betas[level + 1], here.planes, lanes, 1.0)

            def store(k, p, value, target=levels[level + 1].force):
                target[k, p] = value

            here.restrict(diags[level], store, lanes)
    found = [None, None]

    def keep(k, p, value):
        found[k] = value

    levels[2].restrict(diags[2], keep, LANES3)
    eta = 0.5 * halve_lanes(etas[2][0] + etas[2][1], LANES3)
    beta = halve_lanes(betas[2][0] + betas[2][1], LANES3)
    head = jnp.concatenate([own_rows(found[0], found[1]), own_rows(eta, beta)], axis=1)
    far[...] = head
    near[:, 0 : 2 * LANES3] = head
    at = 2 * LANES3
    for p in range(2):
        near[:, at : at + 384] = own_rows(levels[2].field[0, p + 1], levels[2].field[1, p + 1])
        near[:, at + 768 : at + 1152] = own_rows(levels[2].force[0, p], levels[2].force[1, p])
        at += 384


def up_kernel(far, near_even, near_odd, far_above, far_below, *refs):
    levels = [Level(PLANES[i], refs[8 * i : 8 * i + 8]) for i in range(3)]
    velocity, natural, late_force, late_field = refs[24:28]
    fields, others = refs[28:31], refs[31:34]
    gy = lax.axis_index("gy")
    count = lax.axis_size("gy")
    even = gy % 2 == 0

    def above(part):
        return jnp.where(gy == 0, 0.0, jnp.where(even, near_odd[:, part], near_even[:, part]))

    def below(part):
        return jnp.where(gy == count - 1, 0.0, jnp.where(even, near_even[:, part], near_odd[:, part]))

    def sublanes(like):
        return lax.broadcasted_iota(jnp.int32, like.shape, 0)

    def stacked(part):
        m2 = jnp.where(gy < 2, 0.0, far_above[:, part])
        p2 = jnp.where(gy > count - 3, 0.0, far_below[:, part])
        m1, p1, own = above(part), below(part), far[:, part]
        upper = sublanes(own) < 4

        def halves(x, y, second):
            if second:
                return jnp.where(upper, pltpu.roll(x, 4, axis=0), y)
            return jnp.where(upper, x, pltpu.roll(y, 4, axis=0))

        zero = jnp.zeros_like(own)
        return [
            jnp.concatenate([halves(m2, m1, s), halves(own, p1, s), halves(p2, zero, s)], axis=0)
            for s in (False, True)
        ]

    force = stacked(slice(0, LANES3))
    eta, beta = stacked(slice(LANES3, 2 * LANES3))
    right, left, under, over, cross_right, cross_left, diag = coefficients(eta, beta, from_below(eta), from_above)
    scale = OMEGA / diag
    field = [scale * force[0], scale * force[1]]
    for _ in range(5):
        downs = [from_below(x) for x in field]
        ups = [from_above(x) for x in field]
        steps = [downs[k] - ups[k] for k in range(2)]
        field = [
            KEEP * field[k]
            + scale
            * gather_terms(
                right, left, cross_right, cross_left, under, over, field[k], downs[k], ups[k], steps[1 - k], force[k]
            )
            for k in range(2)
        ]
    coarsest = []
    for k in range(2):
        a, b = pltpu.roll(field[k][0:8], 2, axis=0), pltpu.roll(field[k][8:16], 2, axis=0)
        coarsest.append(jnp.where(sublanes(a) < 2, a, b))
    at = 2 * LANES3
    for p in range(2):
        for target, own, start, shift in (
            (late_field, levels[2].field, at, 1),
            (late_force, levels[2].force, at + 768, 0),
        ):
            up, down = above(slice(start, start + 384)), below(slice(start, start + 384))
            for k in range(2):
                turn = 2 if k else 6
                a, b = pltpu.roll(up, turn, axis=0), pltpu.roll(down, turn, axis=0)
                sub = sublanes(a)
                target[k, p + shift] = jnp.where(sub < 2, a, jnp.where(sub < 6, own[k, p + shift], b))
        at += 384
    levels[2].force = late_force
    levels[2].field = late_field
    coarse = lambda k, p: coarsest[k]
    for level in (2, 1, 0):
        levels[level].last_sweeps(coarse, fields[level], others[level])
        coarse = lambda k, p, result=fields[level]: result[k, p + 1]
    for k in range(2):
        for i in range(COLS // 128):
            for p in range(8):
                part = fields[0][k, p + 1, :, 128 * i + EDGE : 128 * i + EDGE + 128]
                natural[i, pl.ds(p, 4, stride=8), :] = pltpu.roll(part, 6, axis=0)[0:4]
            velocity[k, :, 128 * i : 128 * i + 128] = natural[i]


def swap(x, axis, odd):
    rows, cols = lax.axis_size("gy"), lax.axis_size("gx")
    count, across = (rows, cols) if axis == "gy" else (cols, rows)
    pairs = []
    for j in range(across):
        for i in range(odd, count - 1, 2):
            pairs += [((i, j), (i + 1, j)), ((i + 1, j), (i, j))]
        if odd and axis == "gy":
            pairs += [((0, j), (count - 1, j)), ((count - 1, j), (0, j))]
        elif odd:
            pairs += [((i, j), (i, j ^ 1)) for i in (0, count - 1)]
    place = (lambda i, j: j * rows + i) if axis == "gy" else (lambda i, j: i * rows + j)
    return lax.ppermute(x, ("gx", "gy"), [(place(*a), place(*b)) for a, b in pairs])


def turn(x, axis, step):
    count = lax.axis_size(axis)
    return lax.ppermute(x, axis, [(i, (i + step) % count) for i in range(count)])


def local(forcing, ice_mask, viscosity_class, drag_class, viscosity_table, drag_table):
    inputs = [
        pltpu.with_memory_space_constraint(x, pltpu.HBM)
        for x in (viscosity_table, drag_table, forcing, ice_mask, viscosity_class, drag_class)
    ]
    hbm = [pl.BlockSpec(memory_space=pltpu.HBM)] * 6
    table = pltpu.SMEM((16,), jnp.float32)
    coef, side_even, side_odd, main_even, main_odd = pl.pallas_call(
        lookup_kernel,
        out_shape=(shape(2, ROWS, COLS),) + (shape(4, ROWS, EDGE),) * 2 + (shape(4, HALO, COLS),) * 2,
        in_specs=hbm,
        out_specs=tuple(vmem(5)),
        scratch_shapes=[[table, table], pltpu.VMEM((3, ROWS, COLS), jnp.int32), pltpu.SemaphoreType.DMA((9,))],
        compiler_params=params(),
        name="lookup",
    )(*inputs)
    got_even = swap(side_even, "gx", 0)
    got_odd = swap(side_odd, "gx", 1)
    rows_odd = swap(main_odd, "gy", 1)
    send_even, send_odd = pl.pallas_call(
        corner_kernel,
        out_shape=(shape(4, HALO, 2 * EDGE),) * 2,
        in_specs=vmem(2),
        out_specs=tuple(vmem(2)),
        compiler_params=params(),
        name="corners",
    )(got_even, got_odd)
    main_even, send_even = lax.optimization_barrier((main_even, send_even))
    rows_even = swap(main_even, "gy", 0)
    corner_even = swap(send_even, "gy", 0)
    corner_odd = swap(send_odd, "gy", 1)
    kept = [shape(*dims) for level in range(3) for dims in Level.shapes(level)]
    planes = [(PLANES[i], 8, LANES[i]) for i in range(3)]
    rims = [(2, PLANES[i] + 2, 8, LANES[i]) for i in range(3)]
    scratch = [pltpu.VMEM(dims, jnp.float32) for dims in [(WIDE // 128, 64, 128)] + planes * 3 + rims]
    near_lanes = 2 * LANES3 + 4 * LANES[2]
    *kept, near, far = pl.pallas_call(
        down_kernel,
        out_shape=tuple(kept) + (shape(8, near_lanes), shape(8, 2 * LANES3)),
        in_specs=vmem(8),
        out_specs=tuple(vmem(26)),
        scratch_shapes=scratch,
        compiler_params=params(),
        name="down",
    )(forcing, coef, got_even, got_odd, rows_even, rows_odd, corner_even, corner_odd)
    near_even = swap(near, "gy", 0)
    near_odd = swap(near, "gy", 1)
    far_above = turn(far, "gy", 2)
    far_below = turn(far, "gy", -2)
    late = [(2, 2, 8, LANES[2]), (2, 4, 8, LANES[2])]
    scratch = [pltpu.VMEM(dims, jnp.float32) for dims in [(COLS // 128, ROWS, 128)] + late + rims + rims]
    return pl.pallas_call(
        up_kernel,
        out_shape=shape(2, ROWS, COLS),
        in_specs=vmem(29),
        out_specs=vmem(1)[0],
        scratch_shapes=scratch,
        compiler_params=params(),
        name="up",
    )(far, near_even, near_odd, far_above, far_below, *kept)


def solution(mesh):
    in_specs = (P(None, "gy", "gx"), P("gy", "gx"), P("gy", "gx"), P("gy", "gx"), P(), P())
    out_specs = P(None, "gy", "gx")
    return jax.shard_map(local, mesh=mesh, in_specs=in_specs, out_specs=out_specs, check_vma=False)
```

```python
import jax
import jax.numpy as jnp
from jax import lax
from jax.experimental import pallas as pl
from jax.experimental.pallas import tpu as pltpu
from jax.sharding import PartitionSpec as P

OMEGA = 0.6
KEEP = 1.0 - OMEGA
ROWS, COLS = 32, 1024
EDGE = 128
HALO = 16
PLANES = (8, 4, 2)
MAIN = (1024, 512, 256, 128)
RIM = (512, 256, 128, 128)
MERGED = (1152, 640, 384, 256)
VMEM_LIMIT = 16 * 1024 * 1024


def vmem(count):
    return [pl.BlockSpec(memory_space=pltpu.VMEM)] * count


def params():
    return pltpu.CompilerParams(vmem_limit_bytes=VMEM_LIMIT)


def shape(*dims):
    return jax.ShapeDtypeStruct(dims, jnp.float32)


def from_left(x):
    return pltpu.roll(x, 1, axis=1)


def from_right(x):
    return pltpu.roll(x, x.shape[1] - 1, axis=1)


def from_above(x):
    return pltpu.roll(x, 1, axis=0)


def from_below(x):
    return pltpu.roll(x, x.shape[0] - 1, axis=0)


def tiles(x):
    return [x[:, i : i + 128] for i in range(0, x.shape[1], 128)]


def lane(kind):
    return lax.broadcasted_iota(jnp.int32, (8, 128), kind)


def pick(x, index):
    return jnp.take_along_axis(x, index, axis=1, mode="promise_in_bounds")


def halve_lanes(x):
    at = lane(1)
    even = at % 2 == 0
    index = jnp.where(at < 64, 2 * at, 2 * at - 127)
    parts = tiles(x)
    if len(parts) % 2:
        parts.append(jnp.zeros_like(parts[0]))
    out = []
    for a, b in zip(parts[0::2], parts[1::2]):
        out.append(pick(jnp.where(even, a, b), index) + pick(jnp.where(even, b, a), index ^ 1))
    return jnp.concatenate(out, axis=1)


def double_lanes(x, lanes):
    at = lane(1)
    parts = tiles(x)
    count = lanes // 128 - 1
    out = [pick(parts[i // 2], at // 2 + 64 * (i % 2)) for i in range(count)]
    out.append(pick(parts[-1], jnp.where(at < 64, at // 2, at // 2 + 64)))
    return jnp.concatenate(out, axis=1)


def merge_tiles(level, main, rim):
    at = lane(1)
    if level == 0:
        low, left, right, high = rim
    else:
        low = left = pltpu.roll(rim[0], (64, 96, 112)[level - 1], axis=1)
        high = right = pltpu.roll(rim[-1], (64, 32, 80)[level - 1], axis=1)
    out = list(main)
    out[0] = jnp.where(at < 64 >> level, left, out[0])
    out[-1] = jnp.where(at < 128 - (64 >> level), out[-1], right)
    beside = jnp.where(at < 64, high, low)
    if level > 1:
        beside = jnp.where((at < EDGE >> level) | (at >= 128 - (EDGE >> level)), beside, 0.0)
    return out + [beside]


def merge(level, main, rim):
    return jnp.concatenate(merge_tiles(level, tiles(main), tiles(rim)), axis=1)


def coefficients(eta, beta, eta_below, face_above):
    ice = eta > 0.0
    eta_right = from_right(eta)
    right = jnp.where(ice & (eta_right > 0.0), 0.5 * (eta + eta_right), 0.0)
    left = from_left(right)
    below = jnp.where(ice & (eta_below > 0.0), 0.5 * (eta + eta_below), 0.0)
    above = face_above(below)
    base = beta + jnp.where(ice, 0.0, 1.0)
    diag = base + ((right + left) + (below + above))
    return right, left, below, above, 0.05 * eta_right, 0.05 * from_left(eta), diag


def gather_terms(right, left, cross_right, cross_left, below, above, here, under, over, other_step, force):
    from_west = from_left(right * here + cross_right * other_step)
    from_east = from_right(left * here - cross_left * other_step)
    return (force + (from_west + from_east)) + (below * under + above * over)


class Level:
    def __init__(self, planes, refs):
        self.planes = planes
        self.right, self.left, self.cross_right, self.cross_left, self.below, self.scale, self.force, self.field = refs

    @staticmethod
    def shapes(level, widths):
        planes, lanes = PLANES[level], widths[level]
        one = [(planes, 8, lanes)] * 4 + [(planes + 1, 8, lanes), (planes, 8, lanes)]
        return one + [(2, planes, 8, lanes), (2, planes + 2, 8, lanes)]

    def wrap(self, field):
        for k in range(2):
            field[k, 0] = from_above(field[k, self.planes])
            field[k, self.planes + 1] = from_below(field[k, 1])

    def terms(self, p, field):
        out = []
        steps = [field[k, p + 2] - field[k, p] for k in range(2)]
        for k in range(2):
            out.append(
                gather_terms(
                    self.right[p],
                    self.left[p],
                    self.cross_right[p],
                    self.cross_left[p],
                    self.below[p + 1],
                    self.below[p],
                    field[k, p + 1],
                    field[k, p + 2],
                    field[k, p],
                    steps[1 - k],
                    self.force[k, p],
                )
            )
        return out

    def sweep(self, source, target):
        for p in range(self.planes):
            terms = self.terms(p, source)
            for k in range(2):
                target[k, p + 1] = KEEP * source[k, p + 1] + self.scale[p] * terms[k]

    def setup(self, eta, beta, diag):
        planes = self.planes
        for p in range(planes):
            here = eta[p]
            ice = here > 0.0
            next_eta = eta[p + 1] if p + 1 < planes else from_below(eta[0])
            self.below[p + 1] = jnp.where(ice & (next_eta > 0.0), 0.5 * (here + next_eta), 0.0)
        self.below[0] = from_above(self.below[planes])
        for p in range(planes):
            here = eta[p]
            ice = here > 0.0
            eta_right = from_right(here)
            right = jnp.where(ice & (eta_right > 0.0), 0.5 * (here + eta_right), 0.0)
            left = from_left(right)
            base = beta[p] + jnp.where(ice, 0.0, 1.0)
            total = base + ((right + left) + (self.below[p + 1] + self.below[p]))
            self.right[p] = right
            self.left[p] = left
            self.cross_right[p] = 0.05 * eta_right
            self.cross_left[p] = 0.05 * from_left(here)
            diag[p] = total
            self.scale[p] = OMEGA / total

    def first_sweeps(self, other):
        for k in range(2):
            for p in range(self.planes):
                other[k, p + 1] = self.scale[p] * self.force[k, p]
        self.wrap(other)
        self.sweep(other, self.field)
        self.wrap(self.field)

    def restrict(self, diag, target):
        for p in range(0, self.planes, 2):
            rest = [0.0, 0.0]
            for q in (p, p + 1):
                terms = self.terms(q, self.field)
                for k in range(2):
                    rest[k] = rest[k] + (terms[k] - diag[q] * self.field[k, q + 1])
            for k in range(2):
                target(k, p // 2, halve_lanes(rest[k]))

    def last_sweeps(self, coarse, result, other):
        for k in range(2):
            for p in range(0, self.planes, 2):
                add = double_lanes(coarse(k, p // 2), self.field.shape[-1])
                result[k, p + 1] = self.field[k, p + 1] + add
                result[k, p + 2] = self.field[k, p + 2] + add
        self.wrap(result)
        self.sweep(result, other)
        self.wrap(other)
        self.sweep(other, result)


def halve_planes(source, target, planes, scale):
    for p in range(0, planes, 2):
        both = halve_lanes(source[p] + source[p + 1])
        target[p // 2] = scale * both if scale != 1.0 else both


def look_up(tables, classes, ice):
    at = lane(1)
    rows = []
    for table in tables:
        row = jnp.zeros((8, 128), jnp.float32)
        for i in range(16):
            row = jnp.where(at == i, table[i], row)
        rows.append(row)
    return [pick(row, part) * ice for row, part in zip(rows, classes)]


def start_all(pairs, sems):
    copies = [pltpu.make_async_copy(a, b, sems.at[i]) for i, (a, b) in enumerate(pairs)]
    for copy in copies:
        copy.start()
    return copies


def halves_of(axis, size, part):
    even = lax.axis_index(axis) % 2 == 0
    first = pl.multiple_of(jnp.where(even, size - part, 0), part)
    return first, pl.multiple_of(size - part - first, part)


def lookup_kernel(v_table, d_table, forcing, mask, v_class, d_class, coef, *refs):
    sides, rows = refs[0:2], refs[2:4]
    tables, ints, sems = refs[4:]
    pairs = [(v_table, tables[0]), (d_table, tables[1])]
    pairs += [(source, ints.at[i]) for i, source in enumerate((mask, v_class, d_class))]
    side_starts = halves_of("gx", COLS, EDGE)
    row_starts = halves_of("gy", ROWS, HALO)
    for start, target in zip(side_starts, sides):
        pairs.append((forcing.at[:, :, pl.ds(start, EDGE)], target.at[0:2]))
    for start, target in zip(row_starts, rows):
        pairs.append((forcing.at[:, pl.ds(start, HALO), :], target.at[0:2]))
    copies = start_all(pairs, sems)
    for copy in copies[:5]:
        copy.wait()
    for r in range(0, ROWS, 8):
        for c in range(0, COLS, 128):
            part = (slice(r, r + 8), slice(c, c + 128))
            ice = ints[(0,) + part].astype(jnp.float32)
            found = look_up(tables, [ints[(1,) + part], ints[(2,) + part]], ice)
            for k in range(2):
                coef[(k,) + part] = found[k]
    for k in range(2):
        for start, target in zip(side_starts, sides):
            target[2 + k] = coef[k, :, pl.ds(start, EDGE)]
        for start, target in zip(row_starts, rows):
            target[2 + k] = coef[k, pl.ds(start, HALO), :]
    for copy in copies[5:]:
        copy.wait()


def side_columns(get_even, get_odd):
    gx = lax.axis_index("gx")
    even = gx % 2 == 0
    a, b = get_even, get_odd
    left = jnp.where(gx == 0, 0.0, jnp.where(even, b, a))
    right = jnp.where(gx == lax.axis_size("gx") - 1, 0.0, jnp.where(even, a, b))
    return left, right


def corner_kernel(got_even, got_odd, send_even, send_odd):
    for start, target in zip(halves_of("gy", ROWS, HALO), (send_even, send_odd)):
        rows = pl.ds(start, HALO)
        for row in range(4):
            left, right = side_columns(got_even[row, rows], got_odd[row, rows])
            target[row, :, 0:EDGE] = left
            target[row, :, EDGE : 2 * EDGE] = right


def own_rows(a, b):
    upper = lax.broadcasted_iota(jnp.int32, a.shape, 0) < 4
    return jnp.where(upper, pltpu.roll(a, 6, axis=0), pltpu.roll(b, 2, axis=0))


def levels_of(refs):
    return [Level(PLANES[i], refs[8 * i : 8 * i + 8]) for i in range(3)]


def spread(above, own, below, natural, targets, cols):
    gy = lax.axis_index("gy")
    even = gy % 2 == 0
    (above_even, above_odd), (below_even, below_odd) = above, below
    natural[0:HALO] = jnp.where(gy == 0, 0.0, jnp.where(even, above_odd, above_even))
    natural[HALO : HALO + ROWS] = own
    natural[HALO + ROWS :] = jnp.where(gy == lax.axis_size("gy") - 1, 0.0, jnp.where(even, below_even, below_odd))
    for p in range(8):
        targets(p, cols, natural[pl.ds(p, 8, stride=8), :])


def descend(levels, etas, betas, diags, others):
    for level in range(3):
        here = levels[level]
        here.setup(etas[level], betas[level], diags[level])
        here.first_sweeps(others[level])
        if level < 2:
            halve_planes(etas[level], etas[level + 1], here.planes, 0.5)
            halve_planes(betas[level], betas[level + 1], here.planes, 1.0)

            def store(k, p, value, target=levels[level + 1].force):
                target[k, p] = value

            here.restrict(diags[level], store)
    found = [None, None]

    def keep(k, p, value):
        found[k] = value

    levels[2].restrict(diags[2], keep)
    eta = 0.5 * halve_lanes(etas[2][0] + etas[2][1])
    beta = halve_lanes(betas[2][0] + betas[2][1])
    return found + [eta, beta]


def plane_targets(row, levels, etas, betas):
    def target(p, cols, plane):
        if row < 2:
            levels[0].force[row, p, :, cols] = plane
        else:
            (etas, betas)[row - 2][0][p, :, cols] = plane

    return target


def main_kernel(forcing, coef, rows_even, rows_odd, *refs):
    levels = levels_of(refs)
    top, natural = refs[24:26]
    etas, betas, diags, others = (refs[26 + 3 * i : 29 + 3 * i] for i in range(4))
    for row in range(4):
        source = forcing if row < 2 else coef
        target = plane_targets(row, levels, etas, betas)
        for i in range(COLS // 128):
            cols = slice(128 * i, 128 * i + 128)
            halo = (rows_even[row, :, cols], rows_odd[row, :, cols])
            spread(halo, source[row % 2, :, cols], halo, natural.at[(8 * row + i) % 2], target, cols)
    for i, value in enumerate(descend(levels, etas, betas, diags, others)):
        top[i] = value


def rim_kernel(
    forcing,
    coef,
    got_even,
    got_odd,
    rows_even,
    rows_odd,
    corner_even,
    corner_odd,
    top,
    late_force,
    late_field,
    *refs,
):
    levels = levels_of(refs)
    near, far, natural = refs[24:27]
    etas, betas, diags, others = (refs[27 + 3 * i : 30 + 3 * i] for i in range(4))
    for row in range(4):
        source = forcing if row < 2 else coef
        target = plane_targets(row, levels, etas, betas)
        sides = side_columns(got_even[row], got_odd[row])
        for i in range(4):
            if i in (0, 3):
                part = slice(0, EDGE) if i == 0 else slice(EDGE, 2 * EDGE)
                halo = (corner_even[row, :, part], corner_odd[row, :, part])
                own = sides[i // 3]
            else:
                part = slice(0, EDGE) if i == 1 else slice(COLS - EDGE, COLS)
                halo = (rows_even[row, :, part], rows_odd[row, :, part])
                own = source[row % 2, :, part]
            spread(halo, own, halo, natural.at[i % 2], target, slice(128 * i, 128 * i + 128))
    rim = descend(levels, etas, betas, diags, others)
    both = [merge(3, top[i], rim[i]) for i in range(4)]
    head = jnp.concatenate([own_rows(both[0], both[1]), own_rows(both[2], both[3])], axis=1)
    far[...] = head
    at = head.shape[1]
    near[:, 0:at] = head
    for source, rims, shift in ((late_field, levels[2].field, 1), (late_force, levels[2].force, 0)):
        for p in range(2):
            parts = [merge(2, source[k, p + shift], rims[k, p + shift]) for k in range(2)]
            near[:, at : at + MERGED[2]] = own_rows(parts[0], parts[1])
            at += MERGED[2]


def merge_kernel(*refs):
    for level in range(3):
        for i in range(8):
            main, rim, target = (refs[24 * j + 8 * level + i] for j in range(3))
            planes = PLANES[level]
            if i < 6:
                for p in range(main.shape[0]):
                    target[p] = merge(level, main[p], rim[p])
            else:
                for k in range(2):
                    for p in range(i - 6, planes + i - 6):
                        target[k, p] = merge(level, main[k, p], rim[k, p])


def up_kernel(far, near_even, near_odd, far_above, far_below, *refs):
    levels = levels_of(refs)
    velocity, natural, late_force, late_field = refs[24:28]
    fields, others = refs[28:31], refs[31:34]
    gy = lax.axis_index("gy")
    count = lax.axis_size("gy")
    even = gy % 2 == 0

    def above(part):
        return jnp.where(gy == 0, 0.0, jnp.where(even, near_odd[:, part], near_even[:, part]))

    def below(part):
        return jnp.where(gy == count - 1, 0.0, jnp.where(even, near_even[:, part], near_odd[:, part]))

    def sublanes(like):
        return lax.broadcasted_iota(jnp.int32, like.shape, 0)

    def stacked(part):
        m2 = jnp.where(gy < 2, 0.0, far_above[:, part])
        p2 = jnp.where(gy > count - 3, 0.0, far_below[:, part])
        m1, p1, own = above(part), below(part), far[:, part]
        upper = sublanes(own) < 4

        def halves(x, y, second):
            if second:
                return jnp.where(upper, pltpu.roll(x, 4, axis=0), y)
            return jnp.where(upper, x, pltpu.roll(y, 4, axis=0))

        zero = jnp.zeros_like(own)
        return [
            jnp.concatenate([halves(m2, m1, s), halves(own, p1, s), halves(p2, zero, s)], axis=0)
            for s in (False, True)
        ]

    force = stacked(slice(0, MERGED[3]))
    eta, beta = stacked(slice(MERGED[3], 2 * MERGED[3]))
    right, left, under, over, cross_right, cross_left, diag = coefficients(eta, beta, from_below(eta), from_above)
    scale = OMEGA / diag
    field = [scale * force[0], scale * force[1]]
    for _ in range(5):
        downs = [from_below(x) for x in field]
        ups = [from_above(x) for x in field]
        steps = [downs[k] - ups[k] for k in range(2)]
        field = [
            KEEP * field[k]
            + scale
            * gather_terms(
                right, left, cross_right, cross_left, under, over, field[k], downs[k], ups[k], steps[1 - k], force[k]
            )
            for k in range(2)
        ]
    coarsest = []
    for k in range(2):
        a, b = pltpu.roll(field[k][0:8], 2, axis=0), pltpu.roll(field[k][8:16], 2, axis=0)
        coarsest.append(jnp.where(sublanes(a) < 2, a, b))
    at = 2 * MERGED[3]
    for target, own, shift in ((late_field, levels[2].field, 1), (late_force, levels[2].force, 0)):
        for p in range(2):
            part = slice(at, at + MERGED[2])
            up, down = above(part), below(part)
            for k in range(2):
                turn = 2 if k else 6
                a, b = pltpu.roll(up, turn, axis=0), pltpu.roll(down, turn, axis=0)
                sub = sublanes(a)
                target[k, p + shift] = jnp.where(sub < 2, a, jnp.where(sub < 6, own[k, p + shift], b))
            at += MERGED[2]
    levels[2].force = late_force
    levels[2].field = late_field
    coarse = lambda k, p: coarsest[k]
    for level in (2, 1, 0):
        levels[level].last_sweeps(coarse, fields[level], others[level])
        coarse = lambda k, p, result=fields[level]: result[k, p + 1]
    for k in range(2):
        for i in range(COLS // 128):
            for p in range(8):
                part = fields[0][k, p + 1, :, 128 * i : 128 * i + 128]
                natural[i, pl.ds(p, 4, stride=8), :] = pltpu.roll(part, 6, axis=0)[0:4]
            velocity[k, :, 128 * i : 128 * i + 128] = natural[i]


def swap(x, axis, odd):
    rows, cols = lax.axis_size("gy"), lax.axis_size("gx")
    count, across = (rows, cols) if axis == "gy" else (cols, rows)
    pairs = []
    for j in range(across):
        for i in range(odd, count - 1, 2):
            pairs += [((i, j), (i + 1, j)), ((i + 1, j), (i, j))]
        if odd and axis == "gy":
            pairs += [((0, j), (count - 1, j)), ((count - 1, j), (0, j))]
        elif odd:
            pairs += [((i, j), (i, j ^ 1)) for i in (0, count - 1)]
    place = (lambda i, j: j * rows + i) if axis == "gy" else (lambda i, j: i * rows + j)
    return lax.ppermute(x, ("gx", "gy"), [(place(*a), place(*b)) for a, b in pairs])


def turn(x, axis, step):
    count = lax.axis_size(axis)
    return lax.ppermute(x, axis, [(i, (i + step) % count) for i in range(count)])


def local(forcing, ice_mask, viscosity_class, drag_class, viscosity_table, drag_table):
    inputs = [
        pltpu.with_memory_space_constraint(x, pltpu.HBM)
        for x in (viscosity_table, drag_table, forcing, ice_mask, viscosity_class, drag_class)
    ]
    hbm = [pl.BlockSpec(memory_space=pltpu.HBM)] * 6
    table = pltpu.SMEM((16,), jnp.float32)
    coef, side_even, side_odd, main_even, main_odd = pl.pallas_call(
        lookup_kernel,
        out_shape=(shape(2, ROWS, COLS),) + (shape(4, ROWS, EDGE),) * 2 + (shape(4, HALO, COLS),) * 2,
        in_specs=hbm,
        out_specs=tuple(vmem(5)),
        scratch_shapes=[[table, table], pltpu.VMEM((3, ROWS, COLS), jnp.int32), pltpu.SemaphoreType.DMA((9,))],
        compiler_params=params(),
        name="lookup",
    )(*inputs)
    got_even = swap(side_even, "gx", 0)
    got_odd = swap(side_odd, "gx", 1)
    rows_odd = swap(main_odd, "gy", 1)
    send_even, send_odd = pl.pallas_call(
        corner_kernel,
        out_shape=(shape(4, HALO, 2 * EDGE),) * 2,
        in_specs=vmem(2),
        out_specs=tuple(vmem(2)),
        compiler_params=params(),
        name="corners",
    )(got_even, got_odd)
    main_even, send_even = lax.optimization_barrier((main_even, send_even))
    rows_even = swap(main_even, "gy", 0)
    corner_even = swap(send_even, "gy", 0)
    corner_odd = swap(send_odd, "gy", 1)

    def kept(widths):
        return [dims for level in range(3) for dims in Level.shapes(level, widths)]

    def scratch(dims):
        return [pltpu.VMEM(one, jnp.float32) for one in dims]

    def rims(widths):
        return [(2, PLANES[i] + 2, 8, widths[i]) for i in range(3)]

    def work(widths):
        return scratch([(2, 64, 128)] + [(PLANES[i], 8, widths[i]) for i in range(3)] * 3 + rims(widths))

    *main, top = pl.pallas_call(
        main_kernel,
        out_shape=tuple(shape(*dims) for dims in kept(MAIN) + [(4, 8, MAIN[3])]),
        in_specs=vmem(4),
        out_specs=tuple(vmem(25)),
        scratch_shapes=work(MAIN),
        compiler_params=params(),
        name="main",
    )(forcing, coef, rows_even, rows_odd)
    near_lanes = 2 * MERGED[3] + 4 * MERGED[2]
    *rim, near, far = pl.pallas_call(
        rim_kernel,
        out_shape=tuple(shape(*dims) for dims in kept(RIM) + [(8, near_lanes), (8, 2 * MERGED[3])]),
        in_specs=vmem(11),
        out_specs=tuple(vmem(26)),
        scratch_shapes=work(RIM),
        compiler_params=params(),
        name="rim",
    )(forcing, coef, got_even, got_odd, rows_even, rows_odd, corner_even, corner_odd, top, main[22], main[23])
    near_even = swap(near, "gy", 0)
    near_odd = swap(near, "gy", 1)
    far_above = turn(far, "gy", 2)
    far_below = turn(far, "gy", -2)
    merged = pl.pallas_call(
        merge_kernel,
        out_shape=tuple(shape(*dims) for dims in kept(MERGED)),
        in_specs=vmem(48),
        out_specs=tuple(vmem(24)),
        compiler_params=params(),
        name="merge",
    )(*main, *rim)
    late = [(2, 2, 8, MERGED[2]), (2, 4, 8, MERGED[2])]
    return pl.pallas_call(
        up_kernel,
        out_shape=shape(2, ROWS, COLS),
        in_specs=vmem(29),
        out_specs=vmem(1)[0],
        scratch_shapes=scratch([(COLS // 128, ROWS, 128)] + late + rims(MERGED) + rims(MERGED)),
        compiler_params=params(),
        name="up",
    )(far, near_even, near_odd, far_above, far_below, *merged)


def solution(mesh):
    in_specs = (P(None, "gy", "gx"), P("gy", "gx"), P("gy", "gx"), P("gy", "gx"), P(), P())
    out_specs = P(None, "gy", "gx")
    return jax.shard_map(local, mesh=mesh, in_specs=in_specs, out_specs=out_specs, check_vma=False)
```

```python
import jax
import jax.numpy as jnp
from jax import lax
from jax.experimental import pallas as pl
from jax.experimental.pallas import tpu as pltpu
from jax.sharding import PartitionSpec as P

OMEGA = 0.6
KEEP = 1.0 - OMEGA
ROWS, COLS = 32, 1024
EDGE = 128
HALO = 16
PLANES = (8, 4, 2)
MAIN = (1024, 512, 256, 128)
RIM = (512, 256, 128, 128)
MERGED = (1152, 640, 384, 256)
VMEM_LIMIT = 16 * 1024 * 1024


def vmem(count):
    return [pl.BlockSpec(memory_space=pltpu.VMEM)] * count


def params():
    return pltpu.CompilerParams(vmem_limit_bytes=VMEM_LIMIT)


def shape(*dims):
    return jax.ShapeDtypeStruct(dims, jnp.float32)


def from_left(x):
    return pltpu.roll(x, 1, axis=1)


def from_right(x):
    return pltpu.roll(x, x.shape[1] - 1, axis=1)


def from_above(x):
    return pltpu.roll(x, 1, axis=0)


def from_below(x):
    return pltpu.roll(x, x.shape[0] - 1, axis=0)


def tiles(x):
    return [x[:, i : i + 128] for i in range(0, x.shape[1], 128)]


def lane(kind):
    return lax.broadcasted_iota(jnp.int32, (8, 128), kind)


def pick(x, index):
    return jnp.take_along_axis(x, index, axis=1, mode="promise_in_bounds")


def halve_lanes(x):
    at = lane(1)
    even = at % 2 == 0
    index = jnp.where(at < 64, 2 * at, 2 * at - 127)
    parts = tiles(x)
    if len(parts) % 2:
        parts.append(jnp.zeros_like(parts[0]))
    out = []
    for a, b in zip(parts[0::2], parts[1::2]):
        out.append(pick(jnp.where(even, a, b), index) + pick(jnp.where(even, b, a), index ^ 1))
    return jnp.concatenate(out, axis=1)


def double_lanes(x, lanes):
    at = lane(1)
    parts = tiles(x)
    count = lanes // 128 - 1
    out = [pick(parts[i // 2], at // 2 + 64 * (i % 2)) for i in range(count)]
    out.append(pick(parts[-1], jnp.where(at < 64, at // 2, at // 2 + 64)))
    return jnp.concatenate(out, axis=1)


def merge_tiles(level, main, rim):
    at = lane(1)
    if level == 0:
        low, left, right, high = rim
    else:
        low = left = pltpu.roll(rim[0], (64, 96, 112)[level - 1], axis=1)
        high = right = pltpu.roll(rim[-1], (64, 32, 80)[level - 1], axis=1)
    out = list(main)
    out[0] = jnp.where(at < 64 >> level, left, out[0])
    out[-1] = jnp.where(at < 128 - (64 >> level), out[-1], right)
    beside = jnp.where(at < 64, high, low)
    if level > 1:
        beside = jnp.where((at < EDGE >> level) | (at >= 128 - (EDGE >> level)), beside, 0.0)
    return out + [beside]


def merge(level, main, rim):
    return jnp.concatenate(merge_tiles(level, tiles(main), tiles(rim)), axis=1)


def coefficients(eta, beta, eta_below, face_above):
    ice = eta > 0.0
    eta_right = from_right(eta)
    right = jnp.where(ice & (eta_right > 0.0), 0.5 * (eta + eta_right), 0.0)
    left = from_left(right)
    below = jnp.where(ice & (eta_below > 0.0), 0.5 * (eta + eta_below), 0.0)
    above = face_above(below)
    base = beta + jnp.where(ice, 0.0, 1.0)
    diag = base + ((right + left) + (below + above))
    return right, left, below, above, 0.05 * eta_right, 0.05 * from_left(eta), diag


def gather_terms(right, left, cross_right, cross_left, below, above, here, under, over, other_step, force):
    from_west = from_left(right * here + cross_right * other_step)
    from_east = from_right(left * here - cross_left * other_step)
    return (force + (from_west + from_east)) + (below * under + above * over)


class Level:
    def __init__(self, planes, refs):
        self.planes = planes
        self.right, self.left, self.cross_right, self.cross_left, self.below, self.scale, self.force, self.field = refs

    @staticmethod
    def shapes(level, widths):
        planes, lanes = PLANES[level], widths[level]
        one = [(planes, 8, lanes)] * 4 + [(planes + 1, 8, lanes), (planes, 8, lanes)]
        return one + [(2, planes, 8, lanes), (2, planes + 2, 8, lanes)]

    def wrap(self, field):
        for k in range(2):
            field[k, 0] = from_above(field[k, self.planes])
            field[k, self.planes + 1] = from_below(field[k, 1])

    def terms(self, p, field):
        out = []
        steps = [field[k, p + 2] - field[k, p] for k in range(2)]
        for k in range(2):
            out.append(
                gather_terms(
                    self.right[p],
                    self.left[p],
                    self.cross_right[p],
                    self.cross_left[p],
                    self.below[p + 1],
                    self.below[p],
                    field[k, p + 1],
                    field[k, p + 2],
                    field[k, p],
                    steps[1 - k],
                    self.force[k, p],
                )
            )
        return out

    def sweep(self, source, target):
        for p in range(self.planes):
            terms = self.terms(p, source)
            for k in range(2):
                target[k, p + 1] = KEEP * source[k, p + 1] + self.scale[p] * terms[k]

    def setup(self, eta, beta, diag):
        planes = self.planes
        for p in range(planes):
            here = eta[p]
            ice = here > 0.0
            next_eta = eta[p + 1] if p + 1 < planes else from_below(eta[0])
            self.below[p + 1] = jnp.where(ice & (next_eta > 0.0), 0.5 * (here + next_eta), 0.0)
        self.below[0] = from_above(self.below[planes])
        for p in range(planes):
            here = eta[p]
            ice = here > 0.0
            eta_right = from_right(here)
            right = jnp.where(ice & (eta_right > 0.0), 0.5 * (here + eta_right), 0.0)
            left = from_left(right)
            base = beta[p] + jnp.where(ice, 0.0, 1.0)
            total = base + ((right + left) + (self.below[p + 1] + self.below[p]))
            self.right[p] = right
            self.left[p] = left
            self.cross_right[p] = 0.05 * eta_right
            self.cross_left[p] = 0.05 * from_left(here)
            diag[p] = total
            self.scale[p] = OMEGA / total

    def first_sweeps(self, other):
        for k in range(2):
            for p in range(self.planes):
                other[k, p + 1] = self.scale[p] * self.force[k, p]
        self.wrap(other)
        self.sweep(other, self.field)
        self.wrap(self.field)

    def restrict(self, diag, target):
        for p in range(0, self.planes, 2):
            rest = [0.0, 0.0]
            for q in (p, p + 1):
                terms = self.terms(q, self.field)
                for k in range(2):
                    rest[k] = rest[k] + (terms[k] - diag[q] * self.field[k, q + 1])
            for k in range(2):
                target(k, p // 2, halve_lanes(rest[k]))

    def last_sweeps(self, coarse, result, other):
        for k in range(2):
            for p in range(0, self.planes, 2):
                add = double_lanes(coarse(k, p // 2), self.field.shape[-1])
                result[k, p + 1] = self.field[k, p + 1] + add
                result[k, p + 2] = self.field[k, p + 2] + add
        self.wrap(result)
        self.sweep(result, other)
        self.wrap(other)
        self.sweep(other, result)


def halve_planes(source, target, planes, scale):
    for p in range(0, planes, 2):
        both = halve_lanes(source[p] + source[p + 1])
        target[p // 2] = scale * both if scale != 1.0 else both


def look_up(tables, classes, ice):
    at = lane(1)
    rows = []
    for table in tables:
        row = jnp.zeros((8, 128), jnp.float32)
        for i in range(16):
            row = jnp.where(at == i, table[i], row)
        rows.append(row)
    return [pick(row, part) * ice for row, part in zip(rows, classes)]


def start_all(pairs, sems):
    copies = [pltpu.make_async_copy(a, b, sems.at[i]) for i, (a, b) in enumerate(pairs)]
    for copy in copies:
        copy.start()
    return copies


def halves_of(axis, size, part):
    even = lax.axis_index(axis) % 2 == 0
    first = pl.multiple_of(jnp.where(even, size - part, 0), part)
    return first, pl.multiple_of(size - part - first, part)


def lookup_kernel(v_table, d_table, forcing, mask, v_class, d_class, coef, *refs):
    sides, rows = refs[0:2], refs[2:4]
    tables, ints, sems = refs[4:]
    pairs = [(v_table, tables[0]), (d_table, tables[1])]
    pairs += [(source, ints.at[i]) for i, source in enumerate((mask, v_class, d_class))]
    side_starts = halves_of("gx", COLS, EDGE)
    row_starts = halves_of("gy", ROWS, HALO)
    for start, target in zip(side_starts, sides):
        pairs.append((forcing.at[:, :, pl.ds(start, EDGE)], target.at[0:2]))
    for start, target in zip(row_starts, rows):
        pairs.append((forcing.at[:, pl.ds(start, HALO), :], target.at[0:2]))
    copies = start_all(pairs, sems)
    for copy in copies[:5]:
        copy.wait()
    for r in range(0, ROWS, 8):
        for c in range(0, COLS, 128):
            part = (slice(r, r + 8), slice(c, c + 128))
            ice = ints[(0,) + part].astype(jnp.float32)
            found = look_up(tables, [ints[(1,) + part], ints[(2,) + part]], ice)
            for k in range(2):
                coef[(k,) + part] = found[k]
    for k in range(2):
        for start, target in zip(side_starts, sides):
            target[2 + k] = coef[k, :, pl.ds(start, EDGE)]
        for start, target in zip(row_starts, rows):
            target[2 + k] = coef[k, pl.ds(start, HALO), :]
    for copy in copies[5:]:
        copy.wait()


def side_columns(get_even, get_odd):
    gx = lax.axis_index("gx")
    even = gx % 2 == 0
    a, b = get_even, get_odd
    left = jnp.where(gx == 0, 0.0, jnp.where(even, b, a))
    right = jnp.where(gx == lax.axis_size("gx") - 1, 0.0, jnp.where(even, a, b))
    return left, right


def corner_kernel(got_even, got_odd, send_even, send_odd):
    for start, target in zip(halves_of("gy", ROWS, HALO), (send_even, send_odd)):
        rows = pl.ds(start, HALO)
        for row in range(4):
            left, right = side_columns(got_even[row, rows], got_odd[row, rows])
            target[row, :, 0:EDGE] = left
            target[row, :, EDGE : 2 * EDGE] = right


def own_rows(a, b):
    upper = lax.broadcasted_iota(jnp.int32, a.shape, 0) < 4
    return jnp.where(upper, pltpu.roll(a, 6, axis=0), pltpu.roll(b, 2, axis=0))


def levels_of(refs):
    return [Level(PLANES[i], refs[8 * i : 8 * i + 8]) for i in range(3)]


def spread(above, own, below, natural, targets, cols):
    gy = lax.axis_index("gy")
    even = gy % 2 == 0
    (above_even, above_odd), (below_even, below_odd) = above, below
    natural[0:HALO] = jnp.where(gy == 0, 0.0, jnp.where(even, above_odd, above_even))
    natural[HALO : HALO + ROWS] = own
    natural[HALO + ROWS :] = jnp.where(gy == lax.axis_size("gy") - 1, 0.0, jnp.where(even, below_even, below_odd))
    for p in range(8):
        targets(p, cols, natural[pl.ds(p, 8, stride=8), :])


def descend(levels, etas, betas, diags, others):
    for level in range(3):
        here = levels[level]
        here.setup(etas[level], betas[level], diags[level])
        here.first_sweeps(others[level])
        if level < 2:
            halve_planes(etas[level], etas[level + 1], here.planes, 0.5)
            halve_planes(betas[level], betas[level + 1], here.planes, 1.0)

            def store(k, p, value, target=levels[level + 1].force):
                target[k, p] = value

            here.restrict(diags[level], store)
    found = [None, None]

    def keep(k, p, value):
        found[k] = value

    levels[2].restrict(diags[2], keep)
    eta = 0.5 * halve_lanes(etas[2][0] + etas[2][1])
    beta = halve_lanes(betas[2][0] + betas[2][1])
    return found + [eta, beta]


def plane_targets(row, levels, etas, betas):
    def target(p, cols, plane):
        if row < 2:
            levels[0].force[row, p, :, cols] = plane
        else:
            (etas, betas)[row - 2][0][p, :, cols] = plane

    return target


def main_kernel(forcing, coef, rows_even, rows_odd, *refs):
    levels = levels_of(refs)
    top, natural = refs[24:26]
    etas, betas, diags, others = (refs[26 + 3 * i : 29 + 3 * i] for i in range(4))
    for row in range(4):
        source = forcing if row < 2 else coef
        target = plane_targets(row, levels, etas, betas)
        for i in range(COLS // 128):
            cols = slice(128 * i, 128 * i + 128)
            halo = (rows_even[row, :, cols], rows_odd[row, :, cols])
            spread(halo, source[row % 2, :, cols], halo, natural.at[8 * row + i], target, cols)
    for i, value in enumerate(descend(levels, etas, betas, diags, others)):
        top[i] = value


def rim_kernel(
    forcing,
    coef,
    got_even,
    got_odd,
    rows_even,
    rows_odd,
    corner_even,
    corner_odd,
    top,
    late_force,
    late_field,
    *refs,
):
    levels = levels_of(refs)
    near, far, natural = refs[24:27]
    etas, betas, diags, others = (refs[27 + 3 * i : 30 + 3 * i] for i in range(4))
    for row in range(4):
        source = forcing if row < 2 else coef
        target = plane_targets(row, levels, etas, betas)
        sides = side_columns(got_even[row], got_odd[row])
        for i in range(4):
            if i in (0, 3):
                part = slice(0, EDGE) if i == 0 else slice(EDGE, 2 * EDGE)
                halo = (corner_even[row, :, part], corner_odd[row, :, part])
                own = sides[i // 3]
            else:
                part = slice(0, EDGE) if i == 1 else slice(COLS - EDGE, COLS)
                halo = (rows_even[row, :, part], rows_odd[row, :, part])
                own = source[row % 2, :, part]
            spread(halo, own, halo, natural.at[4 * row + i], target, slice(128 * i, 128 * i + 128))
    rim = descend(levels, etas, betas, diags, others)
    both = [merge(3, top[i], rim[i]) for i in range(4)]
    head = jnp.concatenate([own_rows(both[0], both[1]), own_rows(both[2], both[3])], axis=1)
    far[...] = head
    at = head.shape[1]
    near[:, 0:at] = head
    for source, rims, shift in ((late_field, levels[2].field, 1), (late_force, levels[2].force, 0)):
        for p in range(2):
            parts = [merge(2, source[k, p + shift], rims[k, p + shift]) for k in range(2)]
            near[:, at : at + MERGED[2]] = own_rows(parts[0], parts[1])
            at += MERGED[2]


def merge_kernel(*refs):
    late = refs[48:]
    mains, rims = levels_of(refs[:24]), levels_of(refs[24:48])

    def joined(name, *index):
        return merge(0, getattr(mains[0], name)[index], getattr(rims[0], name)[index])

    names = ("right", "left", "cross_right", "cross_left", "scale")
    for i, name in enumerate(names):
        for p in range(8):
            value = joined(name, p)
            late[i][p] = own_rows(value, value)
            if p in (0, 7):
                late[8][i, p // 7] = value
    for p in range(9):
        value = joined("below", p)
        late[5][p] = own_rows(value, value)
        if p in (0, 1, 7, 8):
            late[9][(0, 1, 7, 8).index(p)] = value
    for p in range(8):
        force = [joined("force", k, p) for k in range(2)]
        field = [joined("field", k, p + 1) for k in range(2)]
        late[6][p] = own_rows(force[0], force[1])
        late[7][p] = own_rows(field[0], field[1])
        for k in range(2):
            if p in (0, 7):
                late[10][k, p // 7] = force[k]
            if p in (0, 1, 6, 7):
                late[11][k, (0, 1, 6, 7).index(p)] = field[k]
    for level in (1, 2):
        for i in range(8):
            main, rim = (refs[24 * j + 8 * level + i] for j in range(2))
            target = late[4 + 8 * level + i]
            planes = PLANES[level]
            if i < 6:
                for p in range(main.shape[0]):
                    target[p] = merge(level, main[p], rim[p])
            else:
                for k in range(2):
                    for p in range(i - 6, planes + i - 6):
                        target[k, p] = merge(level, main[k, p], rim[k, p])


def finest_up(refs, coarse, packed, next_packed, natural, velocity, sems):
    right, left, cross_right, cross_left, scale, below, force, field = refs[:8]
    edge_coef, edge_below, edge_force, edge_field = refs[8:]
    wide = MERGED[0]
    edges = [[None] * 8, [None] * 8]
    for p in range(0, 8, 2):
        adds = [double_lanes(coarse(k, p // 2), wide) for k in range(2)]
        both = own_rows(adds[0], adds[1])
        for q in (p, p + 1):
            packed[q] = field[q] + both
            if q in (0, 1, 6, 7):
                for k in range(2):
                    edges[k][q] = edge_field[k, (0, 1, 6, 7).index(q)] + adds[k]
    found = {}
    for i, p in enumerate((0, 7)):
        under = [edges[k][1] if p == 0 else from_below(edges[k][0]) for k in range(2)]
        over = [from_above(edges[k][7]) if p == 0 else edges[k][6] for k in range(2)]
        for k in range(2):
            terms = gather_terms(
                edge_coef[0, i],
                edge_coef[1, i],
                edge_coef[2, i],
                edge_coef[3, i],
                edge_below[2 * i + 1],
                edge_below[2 * i],
                edges[k][p],
                under[k],
                over[k],
                under[1 - k] - over[1 - k],
                edge_force[k, i],
            )
            found[k, p] = KEEP * edges[k][p] + edge_coef[4, i] * terms
    next_packed[1] = own_rows(found[0, 0], found[1, 0])
    next_packed[8] = own_rows(found[0, 7], found[1, 7])
    next_packed[0] = own_rows(from_above(found[0, 7]), from_above(found[1, 7]))
    next_packed[9] = own_rows(from_below(found[0, 0]), from_below(found[1, 0]))

    def sweep(p, above, here, under, first, count, part):
        mid = slice(128, 128 + 128 * count)
        low, high = slice(0, 128 + 128 * count), slice(128, 256 + 128 * count)
        over, w, down = part(above), part(here), part(under)
        step = pltpu.roll(down - over, 4, axis=0)
        west = from_left((part(right[p]) * w + part(cross_right[p]) * step)[:, low])[:, 128:]
        east = from_right((part(left[p]) * w - part(cross_left[p]) * step)[:, high])[:, : 128 * count]
        cols = slice(128 * first, 128 * (first + count))
        terms = (force[p][:, cols] + (west + east)) + (below[p + 1][:, cols] * down[:, mid] + below[p][:, cols] * over[:, mid])
        return KEEP * w[:, mid] + scale[p][:, cols] * terms

    for p in range(1, 7):
        over, here, under = packed[p - 1], packed[p], packed[p + 1]
        terms = gather_terms(
            right[p],
            left[p],
            cross_right[p],
            cross_left[p],
            below[p + 1],
            below[p],
            here,
            under,
            over,
            pltpu.roll(under - over, 4, axis=0),
            force[p],
        )
        next_packed[p + 1] = KEEP * here + scale[p] * terms
    copies = []
    first = 0
    for count in (4, 2, 2):

        def part(x):
            end = x[:, 128 * max(first - 1, 0) : 128 * (first + count + 1)]
            return end if first else jnp.concatenate([x[:, wide - 128 :], end], axis=1)

        for p in range(8):
            done = sweep(p, next_packed[p], next_packed[p + 1], next_packed[p + 2], first, count, part)
            for i in range(count):
                tile = done[:, 128 * i : 128 * i + 128]
                for k in range(2):
                    natural[k, first + i, pl.ds(p, 4, stride=8), :] = tile[4 * k : 4 * k + 4]
        for i in range(first, first + count):
            for k in range(2):
                target = velocity.at[k, :, pl.ds(128 * i, 128)]
                copy = pltpu.make_async_copy(natural.at[k, i], target, sems.at[2 * i + k])
                copy.start()
                copies.append(copy)
        first += count
    for copy in copies:
        copy.wait()


def up_kernel(far, near_even, near_odd, far_above, far_below, *refs):
    levels = [None] + [Level(PLANES[i], refs[4 + 8 * i : 12 + 8 * i]) for i in (1, 2)]
    velocity, natural, sems, packed, next_packed, late_force, late_field = refs[28:35]
    fields, others = (None,) + refs[35:37], (None,) + refs[37:39]
    gy = lax.axis_index("gy")
    count = lax.axis_size("gy")
    even = gy % 2 == 0

    def above(part):
        return jnp.where(gy == 0, 0.0, jnp.where(even, near_odd[:, part], near_even[:, part]))

    def below(part):
        return jnp.where(gy == count - 1, 0.0, jnp.where(even, near_even[:, part], near_odd[:, part]))

    def sublanes(like):
        return lax.broadcasted_iota(jnp.int32, like.shape, 0)

    def stacked(part):
        m2 = jnp.where(gy < 2, 0.0, far_above[:, part])
        p2 = jnp.where(gy > count - 3, 0.0, far_below[:, part])
        m1, p1, own = above(part), below(part), far[:, part]
        upper = sublanes(own) < 4

        def halves(x, y, second):
            if second:
                return jnp.where(upper, pltpu.roll(x, 4, axis=0), y)
            return jnp.where(upper, x, pltpu.roll(y, 4, axis=0))

        zero = jnp.zeros_like(own)
        return [
            jnp.concatenate([halves(m2, m1, s), halves(own, p1, s), halves(p2, zero, s)], axis=0)
            for s in (False, True)
        ]

    force = stacked(slice(0, MERGED[3]))
    eta, beta = stacked(slice(MERGED[3], 2 * MERGED[3]))
    right, left, under, over, cross_right, cross_left, diag = coefficients(eta, beta, from_below(eta), from_above)
    scale = OMEGA / diag
    field = [scale * force[0], scale * force[1]]
    for _ in range(5):
        downs = [from_below(x) for x in field]
        ups = [from_above(x) for x in field]
        steps = [downs[k] - ups[k] for k in range(2)]
        field = [
            KEEP * field[k]
            + scale
            * gather_terms(
                right, left, cross_right, cross_left, under, over, field[k], downs[k], ups[k], steps[1 - k], force[k]
            )
            for k in range(2)
        ]
    coarsest = []
    for k in range(2):
        a, b = pltpu.roll(field[k][0:8], 2, axis=0), pltpu.roll(field[k][8:16], 2, axis=0)
        coarsest.append(jnp.where(sublanes(a) < 2, a, b))
    at = 2 * MERGED[3]
    for target, own, shift in ((late_field, levels[2].field, 1), (late_force, levels[2].force, 0)):
        for p in range(2):
            part = slice(at, at + MERGED[2])
            up, down = above(part), below(part)
            for k in range(2):
                turn = 2 if k else 6
                a, b = pltpu.roll(up, turn, axis=0), pltpu.roll(down, turn, axis=0)
                sub = sublanes(a)
                target[k, p + shift] = jnp.where(sub < 2, a, jnp.where(sub < 6, own[k, p + shift], b))
            at += MERGED[2]
    levels[2].force = late_force
    levels[2].field = late_field
    coarse = lambda k, p: coarsest[k]
    for level in (2, 1):
        levels[level].last_sweeps(coarse, fields[level], others[level])
        coarse = lambda k, p, result=fields[level]: result[k, p + 1]
    finest_up(refs[:12], coarse, packed, next_packed, natural, velocity, sems)


def swap(x, axis, odd):
    rows, cols = lax.axis_size("gy"), lax.axis_size("gx")
    count, across = (rows, cols) if axis == "gy" else (cols, rows)
    pairs = []
    for j in range(across):
        for i in range(odd, count - 1, 2):
            pairs += [((i, j), (i + 1, j)), ((i + 1, j), (i, j))]
        if odd and axis == "gy":
            pairs += [((0, j), (count - 1, j)), ((count - 1, j), (0, j))]
        elif odd:
            pairs += [((i, j), (i, j ^ 1)) for i in (0, count - 1)]
    place = (lambda i, j: j * rows + i) if axis == "gy" else (lambda i, j: i * rows + j)
    return lax.ppermute(x, ("gx", "gy"), [(place(*a), place(*b)) for a, b in pairs])


def turn(x, axis, step):
    count = lax.axis_size(axis)
    return lax.ppermute(x, axis, [(i, (i + step) % count) for i in range(count)])


def local(forcing, ice_mask, viscosity_class, drag_class, viscosity_table, drag_table):
    inputs = [
        pltpu.with_memory_space_constraint(x, pltpu.HBM)
        for x in (viscosity_table, drag_table, forcing, ice_mask, viscosity_class, drag_class)
    ]
    hbm = [pl.BlockSpec(memory_space=pltpu.HBM)] * 6
    table = pltpu.SMEM((16,), jnp.float32)
    coef, side_even, side_odd, main_even, main_odd = pl.pallas_call(
        lookup_kernel,
        out_shape=(shape(2, ROWS, COLS),) + (shape(4, ROWS, EDGE),) * 2 + (shape(4, HALO, COLS),) * 2,
        in_specs=hbm,
        out_specs=tuple(vmem(5)),
        scratch_shapes=[[table, table], pltpu.VMEM((3, ROWS, COLS), jnp.int32), pltpu.SemaphoreType.DMA((9,))],
        compiler_params=params(),
        name="lookup",
    )(*inputs)
    got_even = swap(side_even, "gx", 0)
    got_odd = swap(side_odd, "gx", 1)
    rows_odd = swap(main_odd, "gy", 1)
    send_even, send_odd = pl.pallas_call(
        corner_kernel,
        out_shape=(shape(4, HALO, 2 * EDGE),) * 2,
        in_specs=vmem(2),
        out_specs=tuple(vmem(2)),
        compiler_params=params(),
        name="corners",
    )(got_even, got_odd)
    main_even, send_even = lax.optimization_barrier((main_even, send_even))
    rows_even = swap(main_even, "gy", 0)
    corner_even = swap(send_even, "gy", 0)
    corner_odd = swap(send_odd, "gy", 1)

    def kept(widths):
        return [dims for level in range(3) for dims in Level.shapes(level, widths)]

    def scratch(dims):
        return [pltpu.VMEM(one, jnp.float32) for one in dims]

    def rims(widths):
        return [(2, PLANES[i] + 2, 8, widths[i]) for i in range(3)]

    def work(widths):
        return scratch([(32, 64, 128)] + [(PLANES[i], 8, widths[i]) for i in range(3)] * 3 + rims(widths))

    *main, top = pl.pallas_call(
        main_kernel,
        out_shape=tuple(shape(*dims) for dims in kept(MAIN) + [(4, 8, MAIN[3])]),
        in_specs=vmem(4),
        out_specs=tuple(vmem(25)),
        scratch_shapes=work(MAIN),
        compiler_params=params(),
        name="main",
    )(forcing, coef, rows_even, rows_odd)
    near_lanes = 2 * MERGED[3] + 4 * MERGED[2]
    *rim, near, far = pl.pallas_call(
        rim_kernel,
        out_shape=tuple(shape(*dims) for dims in kept(RIM) + [(8, near_lanes), (8, 2 * MERGED[3])]),
        in_specs=vmem(11),
        out_specs=tuple(vmem(26)),
        scratch_shapes=work(RIM),
        compiler_params=params(),
        name="rim",
    )(forcing, coef, got_even, got_odd, rows_even, rows_odd, corner_even, corner_odd, top, main[22], main[23])
    near_even = swap(near, "gy", 0)
    near_odd = swap(near, "gy", 1)
    far_above = turn(far, "gy", 2)
    far_below = turn(far, "gy", -2)
    wide = MERGED[0]
    finest = [(8, 8, wide)] * 5 + [(9, 8, wide)] + [(8, 8, wide)] * 2
    finest += [(5, 2, 8, wide), (4, 8, wide), (2, 2, 8, wide), (2, 4, 8, wide)]
    merged = pl.pallas_call(
        merge_kernel,
        out_shape=tuple(shape(*dims) for dims in finest + kept(MERGED)[8:]),
        in_specs=vmem(48),
        out_specs=tuple(vmem(28)),
        compiler_params=params(),
        name="merge",
    )(*main, *rim)
    late = [(8, 8, wide), (10, 8, wide), (2, 2, 8, MERGED[2]), (2, 4, 8, MERGED[2])]
    return pl.pallas_call(
        up_kernel,
        out_shape=shape(2, ROWS, COLS),
        in_specs=vmem(33),
        out_specs=pl.BlockSpec(memory_space=pltpu.HBM),
        scratch_shapes=scratch([(2, COLS // 128, ROWS, 128)])
        + [pltpu.SemaphoreType.DMA((2 * COLS // 128,))]
        + scratch(late + rims(MERGED)[1:] + rims(MERGED)[1:]),
        compiler_params=params(),
        name="up",
    )(far, near_even, near_odd, far_above, far_below, *merged)


def solution(mesh):
    in_specs = (P(None, "gy", "gx"), P("gy", "gx"), P("gy", "gx"), P("gy", "gx"), P(), P())
    out_specs = P(None, "gy", "gx")
    return jax.shard_map(local, mesh=mesh, in_specs=in_specs, out_specs=out_specs, check_vma=False)
```

```python
import jax
import jax.numpy as jnp
from jax import lax
from jax.experimental import pallas as pl
from jax.experimental.pallas import tpu as pltpu
from jax.sharding import PartitionSpec as P

OMEGA = 0.6
KEEP = 1.0 - OMEGA
ROWS, COLS = 32, 1024
EDGE = 128
HALO = 16
PLANES = (8, 4, 2)
MAIN = (1024, 512, 256, 128)
RIM = (512, 256, 128, 128)
MERGED = (1152, 640, 384, 256)
VMEM_LIMIT = 16 * 1024 * 1024


def vmem(count):
    return [pl.BlockSpec(memory_space=pltpu.VMEM)] * count


def params():
    return pltpu.CompilerParams(vmem_limit_bytes=VMEM_LIMIT)


def shape(*dims):
    return jax.ShapeDtypeStruct(dims, jnp.float32)


def from_left(x):
    return pltpu.roll(x, 1, axis=1)


def from_right(x):
    return pltpu.roll(x, x.shape[1] - 1, axis=1)


def from_above(x):
    return pltpu.roll(x, 1, axis=0)


def from_below(x):
    return pltpu.roll(x, x.shape[0] - 1, axis=0)


def tiles(x):
    return [x[:, i : i + 128] for i in range(0, x.shape[1], 128)]


def lane(kind):
    return lax.broadcasted_iota(jnp.int32, (8, 128), kind)


def pick(x, index):
    return jnp.take_along_axis(x, index, axis=1, mode="promise_in_bounds")


def halve_lanes(x):
    at = lane(1)
    even = at % 2 == 0
    index = jnp.where(at < 64, 2 * at, 2 * at - 127)
    parts = tiles(x)
    if len(parts) % 2:
        parts.append(jnp.zeros_like(parts[0]))
    out = []
    for a, b in zip(parts[0::2], parts[1::2]):
        out.append(pick(jnp.where(even, a, b), index) + pick(jnp.where(even, b, a), index ^ 1))
    return jnp.concatenate(out, axis=1)


def double_lanes(x, lanes):
    at = lane(1)
    parts = tiles(x)
    count = lanes // 128 - 1
    out = [pick(parts[i // 2], at // 2 + 64 * (i % 2)) for i in range(count)]
    out.append(pick(parts[-1], jnp.where(at < 64, at // 2, at // 2 + 64)))
    return jnp.concatenate(out, axis=1)


def merge_tiles(level, main, rim):
    at = lane(1)
    if level == 0:
        low, left, right, high = rim
    else:
        low = left = pltpu.roll(rim[0], (64, 96, 112)[level - 1], axis=1)
        high = right = pltpu.roll(rim[-1], (64, 32, 80)[level - 1], axis=1)
    out = list(main)
    out[0] = jnp.where(at < 64 >> level, left, out[0])
    out[-1] = jnp.where(at < 128 - (64 >> level), out[-1], right)
    beside = jnp.where(at < 64, high, low)
    if level > 1:
        beside = jnp.where((at < EDGE >> level) | (at >= 128 - (EDGE >> level)), beside, 0.0)
    return out + [beside]


def merge(level, main, rim):
    return jnp.concatenate(merge_tiles(level, tiles(main), tiles(rim)), axis=1)


def coefficients(eta, beta, eta_below, face_above):
    ice = eta > 0.0
    eta_right = from_right(eta)
    right = jnp.where(ice & (eta_right > 0.0), 0.5 * (eta + eta_right), 0.0)
    left = from_left(right)
    below = jnp.where(ice & (eta_below > 0.0), 0.5 * (eta + eta_below), 0.0)
    above = face_above(below)
    base = beta + jnp.where(ice, 0.0, 1.0)
    diag = base + ((right + left) + (below + above))
    return right, left, below, above, 0.05 * eta_right, 0.05 * from_left(eta), diag


def gather_terms(right, left, cross_right, cross_left, below, above, here, under, over, other_step, force):
    from_west = from_left(right * here + cross_right * other_step)
    from_east = from_right(left * here - cross_left * other_step)
    return (force + (from_west + from_east)) + (below * under + above * over)


class Level:
    def __init__(self, planes, refs):
        self.planes = planes
        self.right, self.left, self.cross_right, self.cross_left, self.below, self.scale, self.force, self.field = refs

    @staticmethod
    def shapes(level, widths):
        planes, lanes = PLANES[level], widths[level]
        one = [(planes, 8, lanes)] * 4 + [(planes + 1, 8, lanes), (planes, 8, lanes)]
        return one + [(2, planes, 8, lanes), (2, planes + 2, 8, lanes)]

    def wrap(self, field):
        for k in range(2):
            field[k, 0] = from_above(field[k, self.planes])
            field[k, self.planes + 1] = from_below(field[k, 1])

    def terms(self, p, field):
        out = []
        steps = [field[k, p + 2] - field[k, p] for k in range(2)]
        for k in range(2):
            out.append(
                gather_terms(
                    self.right[p],
                    self.left[p],
                    self.cross_right[p],
                    self.cross_left[p],
                    self.below[p + 1],
                    self.below[p],
                    field[k, p + 1],
                    field[k, p + 2],
                    field[k, p],
                    steps[1 - k],
                    self.force[k, p],
                )
            )
        return out

    def sweep(self, source, target):
        for p in range(self.planes):
            terms = self.terms(p, source)
            for k in range(2):
                target[k, p + 1] = KEEP * source[k, p + 1] + self.scale[p] * terms[k]

    def setup(self, eta, beta, diag):
        planes = self.planes
        for p in range(planes):
            here = eta[p]
            ice = here > 0.0
            next_eta = eta[p + 1] if p + 1 < planes else from_below(eta[0])
            self.below[p + 1] = jnp.where(ice & (next_eta > 0.0), 0.5 * (here + next_eta), 0.0)
        self.below[0] = from_above(self.below[planes])
        for p in range(planes):
            here = eta[p]
            ice = here > 0.0
            eta_right = from_right(here)
            right = jnp.where(ice & (eta_right > 0.0), 0.5 * (here + eta_right), 0.0)
            left = from_left(right)
            base = beta[p] + jnp.where(ice, 0.0, 1.0)
            total = base + ((right + left) + (self.below[p + 1] + self.below[p]))
            self.right[p] = right
            self.left[p] = left
            self.cross_right[p] = 0.05 * eta_right
            self.cross_left[p] = 0.05 * from_left(here)
            diag[p] = total
            self.scale[p] = OMEGA / total

    def first_sweeps(self, other):
        for k in range(2):
            for p in range(self.planes):
                other[k, p + 1] = self.scale[p] * self.force[k, p]
        self.wrap(other)
        self.sweep(other, self.field)
        self.wrap(self.field)

    def restrict(self, diag, target):
        for p in range(0, self.planes, 2):
            rest = [0.0, 0.0]
            for q in (p, p + 1):
                terms = self.terms(q, self.field)
                for k in range(2):
                    rest[k] = rest[k] + (terms[k] - diag[q] * self.field[k, q + 1])
            for k in range(2):
                target(k, p // 2, halve_lanes(rest[k]))

    def last_sweeps(self, coarse, result, other):
        for k in range(2):
            for p in range(0, self.planes, 2):
                add = double_lanes(coarse(k, p // 2), self.field.shape[-1])
                result[k, p + 1] = self.field[k, p + 1] + add
                result[k, p + 2] = self.field[k, p + 2] + add
        self.wrap(result)
        self.sweep(result, other)
        self.wrap(other)
        self.sweep(other, result)


def halve_planes(source, target, planes, scale):
    for p in range(0, planes, 2):
        both = halve_lanes(source[p] + source[p + 1])
        target[p // 2] = scale * both if scale != 1.0 else both


def look_up(tables, classes, ice):
    at = lane(1)
    rows = []
    for table in tables:
        row = jnp.zeros((8, 128), jnp.float32)
        for i in range(16):
            row = jnp.where(at == i, table[i], row)
        rows.append(row)
    return [pick(row, part) * ice for row, part in zip(rows, classes)]


def start_all(pairs, sems):
    copies = [pltpu.make_async_copy(a, b, sems.at[i]) for i, (a, b) in enumerate(pairs)]
    for copy in copies:
        copy.start()
    return copies


def halves_of(axis, size, part):
    even = lax.axis_index(axis) % 2 == 0
    first = pl.multiple_of(jnp.where(even, size - part, 0), part)
    return first, pl.multiple_of(size - part - first, part)


def lookup_kernel(v_table, d_table, forcing, mask, v_class, d_class, coef, *refs):
    sides, rows = refs[0:2], refs[2:4]
    tables, ints, sems = refs[4:]
    pairs = [(v_table, tables[0]), (d_table, tables[1])]
    pairs += [(source, ints.at[i]) for i, source in enumerate((mask, v_class, d_class))]
    side_starts = halves_of("gx", COLS, EDGE)
    row_starts = halves_of("gy", ROWS, HALO)
    for start, target in zip(side_starts, sides):
        pairs.append((forcing.at[:, :, pl.ds(start, EDGE)], target.at[0:2]))
    for start, target in zip(row_starts, rows):
        pairs.append((forcing.at[:, pl.ds(start, HALO), :], target.at[0:2]))
    copies = start_all(pairs, sems)
    for copy in copies[:5]:
        copy.wait()
    for r in range(0, ROWS, 8):
        for c in range(0, COLS, 128):
            part = (slice(r, r + 8), slice(c, c + 128))
            ice = ints[(0,) + part].astype(jnp.float32)
            found = look_up(tables, [ints[(1,) + part], ints[(2,) + part]], ice)
            for k in range(2):
                coef[(k,) + part] = found[k]
    for k in range(2):
        for start, target in zip(side_starts, sides):
            target[2 + k] = coef[k, :, pl.ds(start, EDGE)]
        for start, target in zip(row_starts, rows):
            target[2 + k] = coef[k, pl.ds(start, HALO), :]
    for copy in copies[5:]:
        copy.wait()


def side_columns(get_even, get_odd):
    gx = lax.axis_index("gx")
    even = gx % 2 == 0
    a, b = get_even, get_odd
    left = jnp.where(gx == 0, 0.0, jnp.where(even, b, a))
    right = jnp.where(gx == lax.axis_size("gx") - 1, 0.0, jnp.where(even, a, b))
    return left, right


def corner_kernel(got_odd, got_even, send_even, send_odd):
    for start, target in zip(halves_of("gy", ROWS, HALO), (send_even, send_odd)):
        rows = pl.ds(start, HALO)
        for row in range(4):
            left, right = side_columns(got_even[row, rows], got_odd[row, rows])
            target[row, :, 0:EDGE] = left
            target[row, :, EDGE : 2 * EDGE] = right


def own_rows(a, b):
    upper = lax.broadcasted_iota(jnp.int32, a.shape, 0) < 4
    return jnp.where(upper, pltpu.roll(a, 6, axis=0), pltpu.roll(b, 2, axis=0))


def levels_of(refs):
    return [Level(PLANES[i], refs[8 * i : 8 * i + 8]) for i in range(3)]


def spread(above, own, below, natural, targets, cols):
    gy = lax.axis_index("gy")
    even = gy % 2 == 0
    (above_even, above_odd), (below_even, below_odd) = above, below
    natural[0:HALO] = jnp.where(gy == 0, 0.0, jnp.where(even, above_odd, above_even))
    natural[HALO : HALO + ROWS] = own
    natural[HALO + ROWS :] = jnp.where(gy == lax.axis_size("gy") - 1, 0.0, jnp.where(even, below_even, below_odd))
    for p in range(8):
        targets(p, cols, natural[pl.ds(p, 8, stride=8), :])


def descend(levels, etas, betas, diags, others):
    for level in range(3):
        here = levels[level]
        here.setup(etas[level], betas[level], diags[level])
        here.first_sweeps(others[level])
        if level < 2:
            halve_planes(etas[level], etas[level + 1], here.planes, 0.5)
            halve_planes(betas[level], betas[level + 1], here.planes, 1.0)

            def store(k, p, value, target=levels[level + 1].force):
                target[k, p] = value

            here.restrict(diags[level], store)
    found = [None, None]

    def keep(k, p, value):
        found[k] = value

    levels[2].restrict(diags[2], keep)
    eta = 0.5 * halve_lanes(etas[2][0] + etas[2][1])
    beta = halve_lanes(betas[2][0] + betas[2][1])
    return found + [eta, beta]


def plane_targets(row, levels, etas, betas):
    def target(p, cols, plane):
        if row < 2:
            levels[0].force[row, p, :, cols] = plane
        else:
            (etas, betas)[row - 2][0][p, :, cols] = plane

    return target


def main_kernel(forcing, coef, rows_even, rows_odd, *refs):
    levels = levels_of(refs)
    top, natural = refs[24:26]
    etas, betas, diags, others = (refs[26 + 3 * i : 29 + 3 * i] for i in range(4))
    for row in range(4):
        source = forcing if row < 2 else coef
        target = plane_targets(row, levels, etas, betas)
        for i in range(COLS // 128):
            cols = slice(128 * i, 128 * i + 128)
            halo = (rows_even[row, :, cols], rows_odd[row, :, cols])
            spread(halo, source[row % 2, :, cols], halo, natural.at[8 * row + i], target, cols)
    for i, value in enumerate(descend(levels, etas, betas, diags, others)):
        top[i] = value


def rim_kernel(
    forcing,
    coef,
    got_odd,
    got_even,
    rows_even,
    rows_odd,
    corner_odd,
    corner_even,
    top,
    late_force,
    late_field,
    *refs,
):
    levels = levels_of(refs)
    near, far, natural = refs[24:27]
    etas, betas, diags, others = (refs[27 + 3 * i : 30 + 3 * i] for i in range(4))
    for row in range(4):
        source = forcing if row < 2 else coef
        target = plane_targets(row, levels, etas, betas)
        sides = side_columns(got_even[row], got_odd[row])
        for i in range(4):
            if i in (0, 3):
                part = slice(0, EDGE) if i == 0 else slice(EDGE, 2 * EDGE)
                halo = (corner_even[row, :, part], corner_odd[row, :, part])
                own = sides[i // 3]
            else:
                part = slice(0, EDGE) if i == 1 else slice(COLS - EDGE, COLS)
                halo = (rows_even[row, :, part], rows_odd[row, :, part])
                own = source[row % 2, :, part]
            spread(halo, own, halo, natural.at[4 * row + i], target, slice(128 * i, 128 * i + 128))
    rim = descend(levels, etas, betas, diags, others)
    both = [merge(3, top[i], rim[i]) for i in range(4)]
    head = jnp.concatenate([own_rows(both[0], both[1]), own_rows(both[2], both[3])], axis=1)
    far[...] = head
    at = head.shape[1]
    near[:, 0:at] = head
    for source, rims, shift in ((late_field, levels[2].field, 1), (late_force, levels[2].force, 0)):
        for p in range(2):
            parts = [merge(2, source[k, p + shift], rims[k, p + shift]) for k in range(2)]
            near[:, at : at + MERGED[2]] = own_rows(parts[0], parts[1])
            at += MERGED[2]


def merge_kernel(*refs):
    late = refs[48:]
    mains, rims = levels_of(refs[:24]), levels_of(refs[24:48])

    def joined(name, *index):
        return merge(0, getattr(mains[0], name)[index], getattr(rims[0], name)[index])

    names = ("right", "left", "cross_right", "cross_left", "scale")
    for i, name in enumerate(names):
        for p in range(8):
            value = joined(name, p)
            late[i][p] = own_rows(value, value)
            if p in (0, 7):
                late[8][i, p // 7] = value
    for p in range(9):
        value = joined("below", p)
        late[5][p] = own_rows(value, value)
        if p in (0, 1, 7, 8):
            late[9][(0, 1, 7, 8).index(p)] = value
    for p in range(8):
        force = [joined("force", k, p) for k in range(2)]
        field = [joined("field", k, p + 1) for k in range(2)]
        late[6][p] = own_rows(force[0], force[1])
        late[7][p] = own_rows(field[0], field[1])
        for k in range(2):
            if p in (0, 7):
                late[10][k, p // 7] = force[k]
            if p in (0, 1, 6, 7):
                late[11][k, (0, 1, 6, 7).index(p)] = field[k]
    for level in (1, 2):
        for i in range(8):
            main, rim = (refs[24 * j + 8 * level + i] for j in range(2))
            target = late[4 + 8 * level + i]
            planes = PLANES[level]
            if i < 6:
                for p in range(main.shape[0]):
                    target[p] = merge(level, main[p], rim[p])
            else:
                for k in range(2):
                    for p in range(i - 6, planes + i - 6):
                        target[k, p] = merge(level, main[k, p], rim[k, p])


def finest_up(refs, coarse, packed, next_packed, natural, velocity, sems):
    right, left, cross_right, cross_left, scale, below, force, field = refs[:8]
    edge_coef, edge_below, edge_force, edge_field = refs[8:]
    wide = MERGED[0]
    edges = [[None] * 8, [None] * 8]
    for p in range(0, 8, 2):
        adds = [double_lanes(coarse(k, p // 2), wide) for k in range(2)]
        both = own_rows(adds[0], adds[1])
        for q in (p, p + 1):
            packed[q] = field[q] + both
            if q in (0, 1, 6, 7):
                for k in range(2):
                    edges[k][q] = edge_field[k, (0, 1, 6, 7).index(q)] + adds[k]
    found = {}
    for i, p in enumerate((0, 7)):
        under = [edges[k][1] if p == 0 else from_below(edges[k][0]) for k in range(2)]
        over = [from_above(edges[k][7]) if p == 0 else edges[k][6] for k in range(2)]
        for k in range(2):
            terms = gather_terms(
                edge_coef[0, i],
                edge_coef[1, i],
                edge_coef[2, i],
                edge_coef[3, i],
                edge_below[2 * i + 1],
                edge_below[2 * i],
                edges[k][p],
                under[k],
                over[k],
                under[1 - k] - over[1 - k],
                edge_force[k, i],
            )
            found[k, p] = KEEP * edges[k][p] + edge_coef[4, i] * terms
    next_packed[1] = own_rows(found[0, 0], found[1, 0])
    next_packed[8] = own_rows(found[0, 7], found[1, 7])
    next_packed[0] = own_rows(from_above(found[0, 7]), from_above(found[1, 7]))
    next_packed[9] = own_rows(from_below(found[0, 0]), from_below(found[1, 0]))

    def sweep(p, above, here, under, first, count, part):
        mid = slice(128, 128 + 128 * count)
        low, high = slice(0, 128 + 128 * count), slice(128, 256 + 128 * count)
        over, w, down = part(above), part(here), part(under)
        step = pltpu.roll(down - over, 4, axis=0)
        west = from_left((part(right[p]) * w + part(cross_right[p]) * step)[:, low])[:, 128:]
        east = from_right((part(left[p]) * w - part(cross_left[p]) * step)[:, high])[:, : 128 * count]
        cols = slice(128 * first, 128 * (first + count))
        terms = (force[p][:, cols] + (west + east)) + (below[p + 1][:, cols] * down[:, mid] + below[p][:, cols] * over[:, mid])
        return KEEP * w[:, mid] + scale[p][:, cols] * terms

    for p in range(1, 7):
        over, here, under = packed[p - 1], packed[p], packed[p + 1]
        terms = gather_terms(
            right[p],
            left[p],
            cross_right[p],
            cross_left[p],
            below[p + 1],
            below[p],
            here,
            under,
            over,
            pltpu.roll(under - over, 4, axis=0),
            force[p],
        )
        next_packed[p + 1] = KEEP * here + scale[p] * terms
    copies = []
    first = 0
    for count in (4, 2, 2):

        def part(x):
            end = x[:, 128 * max(first - 1, 0) : 128 * (first + count + 1)]
            return end if first else jnp.concatenate([x[:, wide - 128 :], end], axis=1)

        for p in range(8):
            done = sweep(p, next_packed[p], next_packed[p + 1], next_packed[p + 2], first, count, part)
            for i in range(count):
                tile = done[:, 128 * i : 128 * i + 128]
                for k in range(2):
                    natural[k, first + i, pl.ds(p, 4, stride=8), :] = tile[4 * k : 4 * k + 4]
        for i in range(first, first + count):
            for k in range(2):
                target = velocity.at[k, :, pl.ds(128 * i, 128)]
                copy = pltpu.make_async_copy(natural.at[k, i], target, sems.at[2 * i + k])
                copy.start()
                copies.append(copy)
        first += count
    for copy in copies:
        copy.wait()


def up_kernel(far, near_even, near_odd, far_above, far_below, *refs):
    levels = [None] + [Level(PLANES[i], refs[4 + 8 * i : 12 + 8 * i]) for i in (1, 2)]
    velocity, natural, sems, packed, next_packed, late_force, late_field = refs[28:35]
    fields, others = (None,) + refs[35:37], (None,) + refs[37:39]
    gy = lax.axis_index("gy")
    count = lax.axis_size("gy")
    even = gy % 2 == 0

    def above(part):
        return jnp.where(gy == 0, 0.0, jnp.where(even, near_odd[:, part], near_even[:, part]))

    def below(part):
        return jnp.where(gy == count - 1, 0.0, jnp.where(even, near_even[:, part], near_odd[:, part]))

    def sublanes(like):
        return lax.broadcasted_iota(jnp.int32, like.shape, 0)

    def stacked(part):
        m2 = jnp.where(gy < 2, 0.0, far_above[:, part])
        p2 = jnp.where(gy > count - 3, 0.0, far_below[:, part])
        m1, p1, own = above(part), below(part), far[:, part]
        upper = sublanes(own) < 4

        def halves(x, y, second):
            if second:
                return jnp.where(upper, pltpu.roll(x, 4, axis=0), y)
            return jnp.where(upper, x, pltpu.roll(y, 4, axis=0))

        zero = jnp.zeros_like(own)
        return [
            jnp.concatenate([halves(m2, m1, s), halves(own, p1, s), halves(p2, zero, s)], axis=0)
            for s in (False, True)
        ]

    force = stacked(slice(0, MERGED[3]))
    eta, beta = stacked(slice(MERGED[3], 2 * MERGED[3]))
    right, left, under, over, cross_right, cross_left, diag = coefficients(eta, beta, from_below(eta), from_above)
    scale = OMEGA / diag
    field = [scale * force[0], scale * force[1]]
    for _ in range(5):
        downs = [from_below(x) for x in field]
        ups = [from_above(x) for x in field]
        steps = [downs[k] - ups[k] for k in range(2)]
        field = [
            KEEP * field[k]
            + scale
            * gather_terms(
                right, left, cross_right, cross_left, under, over, field[k], downs[k], ups[k], steps[1 - k], force[k]
            )
            for k in range(2)
        ]
    coarsest = []
    for k in range(2):
        a, b = pltpu.roll(field[k][0:8], 2, axis=0), pltpu.roll(field[k][8:16], 2, axis=0)
        coarsest.append(jnp.where(sublanes(a) < 2, a, b))
    at = 2 * MERGED[3]
    for target, own, shift in ((late_field, levels[2].field, 1), (late_force, levels[2].force, 0)):
        for p in range(2):
            part = slice(at, at + MERGED[2])
            up, down = above(part), below(part)
            for k in range(2):
                turn = 2 if k else 6
                a, b = pltpu.roll(up, turn, axis=0), pltpu.roll(down, turn, axis=0)
                sub = sublanes(a)
                target[k, p + shift] = jnp.where(sub < 2, a, jnp.where(sub < 6, own[k, p + shift], b))
            at += MERGED[2]
    levels[2].force = late_force
    levels[2].field = late_field
    coarse = lambda k, p: coarsest[k]
    for level in (2, 1):
        levels[level].last_sweeps(coarse, fields[level], others[level])
        coarse = lambda k, p, result=fields[level]: result[k, p + 1]
    finest_up(refs[:12], coarse, packed, next_packed, natural, velocity, sems)


def swap(x, axis, odd):
    rows, cols = lax.axis_size("gy"), lax.axis_size("gx")
    count, across = (rows, cols) if axis == "gy" else (cols, rows)
    pairs = []
    for j in range(across):
        for i in range(odd, count - 1, 2):
            pairs += [((i, j), (i + 1, j)), ((i + 1, j), (i, j))]
        if odd:
            pairs += [((i, j), (i, j ^ 1)) for i in (0, count - 1)]
    place = (lambda i, j: j * rows + i) if axis == "gy" else (lambda i, j: i * rows + j)
    return lax.ppermute(x, ("gx", "gy"), [(place(*a), place(*b)) for a, b in pairs])


def turn(x, axis, step):
    count = lax.axis_size(axis)
    return lax.ppermute(x, axis, [(i, (i + step) % count) for i in range(count)])


def local(forcing, ice_mask, viscosity_class, drag_class, viscosity_table, drag_table):
    inputs = [
        pltpu.with_memory_space_constraint(x, pltpu.HBM)
        for x in (viscosity_table, drag_table, forcing, ice_mask, viscosity_class, drag_class)
    ]
    hbm = [pl.BlockSpec(memory_space=pltpu.HBM)] * 6
    table = pltpu.SMEM((16,), jnp.float32)
    coef, side_even, side_odd, main_even, main_odd = pl.pallas_call(
        lookup_kernel,
        out_shape=(shape(2, ROWS, COLS),) + (shape(4, ROWS, EDGE),) * 2 + (shape(4, HALO, COLS),) * 2,
        in_specs=hbm,
        out_specs=tuple(vmem(5)),
        scratch_shapes=[[table, table], pltpu.VMEM((3, ROWS, COLS), jnp.int32), pltpu.SemaphoreType.DMA((9,))],
        compiler_params=params(),
        name="lookup",
    )(*inputs)
    got_odd = swap(side_odd, "gx", 1)
    got_even = swap(side_even, "gx", 0)
    rows_odd = swap(main_odd, "gy", 1)
    send_even, send_odd = pl.pallas_call(
        corner_kernel,
        out_shape=(shape(4, HALO, 2 * EDGE),) * 2,
        in_specs=vmem(2),
        out_specs=tuple(vmem(2)),
        compiler_params=params(),
        name="corners",
    )(got_odd, got_even)
    main_even, send_even = lax.optimization_barrier((main_even, send_even))
    corner_odd = swap(send_odd, "gy", 1)
    corner_even = swap(send_even, "gy", 0)
    rows_even = swap(main_even, "gy", 0)

    def kept(widths):
        return [dims for level in range(3) for dims in Level.shapes(level, widths)]

    def scratch(dims):
        return [pltpu.VMEM(one, jnp.float32) for one in dims]

    def rims(widths):
        return [(2, PLANES[i] + 2, 8, widths[i]) for i in range(3)]

    def work(widths):
        return scratch([(32, 64, 128)] + [(PLANES[i], 8, widths[i]) for i in range(3)] * 3 + rims(widths))

    *main, top = pl.pallas_call(
        main_kernel,
        out_shape=tuple(shape(*dims) for dims in kept(MAIN) + [(4, 8, MAIN[3])]),
        in_specs=vmem(4),
        out_specs=tuple(vmem(25)),
        scratch_shapes=work(MAIN),
        compiler_params=params(),
        name="main",
    )(forcing, coef, rows_even, rows_odd)
    near_lanes = 2 * MERGED[3] + 4 * MERGED[2]
    *rim, near, far = pl.pallas_call(
        rim_kernel,
        out_shape=tuple(shape(*dims) for dims in kept(RIM) + [(8, near_lanes), (8, 2 * MERGED[3])]),
        in_specs=vmem(11),
        out_specs=tuple(vmem(26)),
        scratch_shapes=work(RIM),
        compiler_params=params(),
        name="rim",
    )(forcing, coef, got_odd, got_even, rows_even, rows_odd, corner_odd, corner_even, top, main[22], main[23])
    near_even = swap(near, "gy", 0)
    near_odd = swap(near, "gy", 1)
    far_above = turn(far, "gy", 2)
    far_below = turn(far, "gy", -2)
    wide = MERGED[0]
    finest = [(8, 8, wide)] * 5 + [(9, 8, wide)] + [(8, 8, wide)] * 2
    finest += [(5, 2, 8, wide), (4, 8, wide), (2, 2, 8, wide), (2, 4, 8, wide)]
    merged = pl.pallas_call(
        merge_kernel,
        out_shape=tuple(shape(*dims) for dims in finest + kept(MERGED)[8:]),
        in_specs=vmem(48),
        out_specs=tuple(vmem(28)),
        compiler_params=params(),
        name="merge",
    )(*main, *rim)
    late = [(8, 8, wide), (10, 8, wide), (2, 2, 8, MERGED[2]), (2, 4, 8, MERGED[2])]
    return pl.pallas_call(
        up_kernel,
        out_shape=shape(2, ROWS, COLS),
        in_specs=vmem(33),
        out_specs=pl.BlockSpec(memory_space=pltpu.HBM),
        scratch_shapes=scratch([(2, COLS // 128, ROWS, 128)])
        + [pltpu.SemaphoreType.DMA((2 * COLS // 128,))]
        + scratch(late + rims(MERGED)[1:] + rims(MERGED)[1:]),
        compiler_params=params(),
        name="up",
    )(far, near_even, near_odd, far_above, far_below, *merged)


def solution(mesh):
    in_specs = (P(None, "gy", "gx"), P("gy", "gx"), P("gy", "gx"), P("gy", "gx"), P(), P())
    out_specs = P(None, "gy", "gx")
    return jax.shard_map(local, mesh=mesh, in_specs=in_specs, out_specs=out_specs, check_vma=False)
```

```python
import jax
import jax.numpy as jnp
from jax import lax
from jax.experimental import pallas as pl
from jax.experimental.pallas import tpu as pltpu
from jax.sharding import PartitionSpec as P

OMEGA = 0.6
KEEP = 1.0 - OMEGA
ROWS, COLS = 32, 1024
EDGE = 128
HALO = 16
PLANES = (8, 4, 2)
MAIN = (1024, 512, 256, 128)
RIM = (512, 256, 128, 128)
MERGED = (1152, 640, 384, 256)
VMEM_LIMIT = 16 * 1024 * 1024


def vmem(count):
    return [pl.BlockSpec(memory_space=pltpu.VMEM)] * count


def params():
    return pltpu.CompilerParams(vmem_limit_bytes=VMEM_LIMIT)


def shape(*dims):
    return jax.ShapeDtypeStruct(dims, jnp.float32)


def from_left(x):
    return pltpu.roll(x, 1, axis=1)


def from_right(x):
    return pltpu.roll(x, x.shape[1] - 1, axis=1)


def from_above(x):
    return pltpu.roll(x, 1, axis=0)


def from_below(x):
    return pltpu.roll(x, x.shape[0] - 1, axis=0)


def tiles(x):
    return [x[:, i : i + 128] for i in range(0, x.shape[1], 128)]


def lane(kind):
    return lax.broadcasted_iota(jnp.int32, (8, 128), kind)


def pick(x, index):
    return jnp.take_along_axis(x, index, axis=1, mode="promise_in_bounds")


def halve_lanes(x):
    at = lane(1)
    even = at % 2 == 0
    index = jnp.where(at < 64, 2 * at, 2 * at - 127)
    parts = tiles(x)
    if len(parts) % 2:
        parts.append(jnp.zeros_like(parts[0]))
    out = []
    for a, b in zip(parts[0::2], parts[1::2]):
        out.append(pick(jnp.where(even, a, b), index) + pick(jnp.where(even, b, a), index ^ 1))
    return jnp.concatenate(out, axis=1)


def double_lanes(x, lanes):
    at = lane(1)
    parts = tiles(x)
    count = lanes // 128 - 1
    out = [pick(parts[i // 2], at // 2 + 64 * (i % 2)) for i in range(count)]
    out.append(pick(parts[-1], jnp.where(at < 64, at // 2, at // 2 + 64)))
    return jnp.concatenate(out, axis=1)


def merge_tiles(level, main, rim):
    at = lane(1)
    if level == 0:
        low, left, right, high = rim
    else:
        low = left = pltpu.roll(rim[0], (64, 96, 112)[level - 1], axis=1)
        high = right = pltpu.roll(rim[-1], (64, 32, 80)[level - 1], axis=1)
    out = list(main)
    out[0] = jnp.where(at < 64 >> level, left, out[0])
    out[-1] = jnp.where(at < 128 - (64 >> level), out[-1], right)
    beside = jnp.where(at < 64, high, low)
    if level > 1:
        beside = jnp.where((at < EDGE >> level) | (at >= 128 - (EDGE >> level)), beside, 0.0)
    return out + [beside]


def merge(level, main, rim):
    return jnp.concatenate(merge_tiles(level, tiles(main), tiles(rim)), axis=1)


def coefficients(eta, beta, eta_below, face_above):
    ice = eta > 0.0
    eta_right = from_right(eta)
    right = jnp.where(ice & (eta_right > 0.0), 0.5 * (eta + eta_right), 0.0)
    left = from_left(right)
    below = jnp.where(ice & (eta_below > 0.0), 0.5 * (eta + eta_below), 0.0)
    above = face_above(below)
    base = beta + jnp.where(ice, 0.0, 1.0)
    diag = base + ((right + left) + (below + above))
    return right, left, below, above, 0.05 * eta_right, 0.05 * from_left(eta), diag


def gather_terms(right, left, cross_right, cross_left, below, above, here, under, over, other_step, force):
    from_west = from_left(right * here + cross_right * other_step)
    from_east = from_right(left * here - cross_left * other_step)
    return (force + (from_west + from_east)) + (below * under + above * over)


class Level:
    def __init__(self, planes, refs):
        self.planes = planes
        self.right, self.left, self.cross_right, self.cross_left, self.below, self.scale, self.force, self.field = refs

    @staticmethod
    def shapes(level, widths):
        planes, lanes = PLANES[level], widths[level]
        one = [(planes, 8, lanes)] * 4 + [(planes + 1, 8, lanes), (planes, 8, lanes)]
        return one + [(2, planes, 8, lanes), (2, planes + 2, 8, lanes)]

    def wrap(self, field):
        for k in range(2):
            field[k, 0] = from_above(field[k, self.planes])
            field[k, self.planes + 1] = from_below(field[k, 1])

    def terms(self, p, field):
        out = []
        steps = [field[k, p + 2] - field[k, p] for k in range(2)]
        for k in range(2):
            out.append(
                gather_terms(
                    self.right[p],
                    self.left[p],
                    self.cross_right[p],
                    self.cross_left[p],
                    self.below[p + 1],
                    self.below[p],
                    field[k, p + 1],
                    field[k, p + 2],
                    field[k, p],
                    steps[1 - k],
                    self.force[k, p],
                )
            )
        return out

    def sweep(self, source, target):
        for p in range(self.planes):
            terms = self.terms(p, source)
            for k in range(2):
                target[k, p + 1] = KEEP * source[k, p + 1] + self.scale[p] * terms[k]

    def setup(self, eta, beta, diag):
        planes = self.planes
        for p in range(planes):
            here = eta[p]
            ice = here > 0.0
            next_eta = eta[p + 1] if p + 1 < planes else from_below(eta[0])
            self.below[p + 1] = jnp.where(ice & (next_eta > 0.0), 0.5 * (here + next_eta), 0.0)
        self.below[0] = from_above(self.below[planes])
        for p in range(planes):
            here = eta[p]
            ice = here > 0.0
            eta_right = from_right(here)
            right = jnp.where(ice & (eta_right > 0.0), 0.5 * (here + eta_right), 0.0)
            left = from_left(right)
            base = beta[p] + jnp.where(ice, 0.0, 1.0)
            total = base + ((right + left) + (self.below[p + 1] + self.below[p]))
            self.right[p] = right
            self.left[p] = left
            self.cross_right[p] = 0.05 * eta_right
            self.cross_left[p] = 0.05 * from_left(here)
            diag[p] = total
            self.scale[p] = OMEGA / total

    def first_sweeps(self, other):
        for k in range(2):
            for p in range(self.planes):
                other[k, p + 1] = self.scale[p] * self.force[k, p]
        self.wrap(other)
        self.sweep(other, self.field)
        self.wrap(self.field)

    def restrict(self, diag, target):
        for p in range(0, self.planes, 2):
            rest = [0.0, 0.0]
            for q in (p, p + 1):
                terms = self.terms(q, self.field)
                for k in range(2):
                    rest[k] = rest[k] + (terms[k] - diag[q] * self.field[k, q + 1])
            for k in range(2):
                target(k, p // 2, halve_lanes(rest[k]))

    def last_sweeps(self, coarse, result, other):
        for k in range(2):
            for p in range(0, self.planes, 2):
                add = double_lanes(coarse(k, p // 2), self.field.shape[-1])
                result[k, p + 1] = self.field[k, p + 1] + add
                result[k, p + 2] = self.field[k, p + 2] + add
        self.wrap(result)
        self.sweep(result, other)
        self.wrap(other)
        self.sweep(other, result)


def halve_planes(source, target, planes, scale):
    for p in range(0, planes, 2):
        both = halve_lanes(source[p] + source[p + 1])
        target[p // 2] = scale * both if scale != 1.0 else both


def look_up(tables, classes, ice):
    at = lane(1)
    rows = []
    for table in tables:
        row = jnp.zeros((8, 128), jnp.float32)
        for i in range(16):
            row = jnp.where(at == i, table[i], row)
        rows.append(row)
    return [pick(row, part) * ice for row, part in zip(rows, classes)]


def start_all(pairs, sems):
    copies = [pltpu.make_async_copy(a, b, sems.at[i]) for i, (a, b) in enumerate(pairs)]
    for copy in copies:
        copy.start()
    return copies


def halves_of(axis, size, part):
    even = lax.axis_index(axis) % 2 == 0
    first = pl.multiple_of(jnp.where(even, size - part, 0), part)
    return first, pl.multiple_of(size - part - first, part)


def lookup_kernel(v_table, d_table, forcing, mask, v_class, d_class, coef, *refs):
    sides, rows = refs[0:2], refs[2:4]
    tables, ints, sems = refs[4:]
    pairs = [(v_table, tables[0]), (d_table, tables[1])]
    pairs += [(source, ints.at[i]) for i, source in enumerate((mask, v_class, d_class))]
    side_starts = halves_of("gx", COLS, EDGE)
    row_starts = halves_of("gy", ROWS, HALO)
    for start, target in zip(side_starts, sides):
        pairs.append((forcing.at[:, :, pl.ds(start, EDGE)], target.at[0:2]))
    for start, target in zip(row_starts, rows):
        pairs.append((forcing.at[:, pl.ds(start, HALO), :], target.at[0:2]))
    copies = start_all(pairs, sems)
    for copy in copies[:5]:
        copy.wait()
    for r in range(0, ROWS, 8):
        for c in range(0, COLS, 128):
            part = (slice(r, r + 8), slice(c, c + 128))
            ice = ints[(0,) + part].astype(jnp.float32)
            found = look_up(tables, [ints[(1,) + part], ints[(2,) + part]], ice)
            for k in range(2):
                coef[(k,) + part] = found[k]
    for k in range(2):
        for start, target in zip(side_starts, sides):
            target[2 + k] = coef[k, :, pl.ds(start, EDGE)]
        for start, target in zip(row_starts, rows):
            target[2 + k] = coef[k, pl.ds(start, HALO), :]
    for copy in copies[5:]:
        copy.wait()


def side_columns(get_even, get_odd):
    gx = lax.axis_index("gx")
    even = gx % 2 == 0
    a, b = get_even, get_odd
    left = jnp.where(gx == 0, 0.0, jnp.where(even, b, a))
    right = jnp.where(gx == lax.axis_size("gx") - 1, 0.0, jnp.where(even, a, b))
    return left, right


def corner_kernel(got_odd, got_even, send_even, send_odd):
    for start, target in zip(halves_of("gy", ROWS, HALO), (send_even, send_odd)):
        rows = pl.ds(start, HALO)
        for row in range(4):
            left, right = side_columns(got_even[row, rows], got_odd[row, rows])
            target[row, :, 0:EDGE] = left
            target[row, :, EDGE : 2 * EDGE] = right


def own_rows(a, b):
    upper = lax.broadcasted_iota(jnp.int32, a.shape, 0) < 4
    return jnp.where(upper, pltpu.roll(a, 6, axis=0), pltpu.roll(b, 2, axis=0))


def levels_of(refs):
    return [Level(PLANES[i], refs[8 * i : 8 * i + 8]) for i in range(3)]


def spread(above, own, below, natural, targets, cols):
    gy = lax.axis_index("gy")
    even = gy % 2 == 0
    (above_even, above_odd), (below_even, below_odd) = above, below
    natural[0:HALO] = jnp.where(gy == 0, 0.0, jnp.where(even, above_odd, above_even))
    natural[HALO : HALO + ROWS] = own
    natural[HALO + ROWS :] = jnp.where(gy == lax.axis_size("gy") - 1, 0.0, jnp.where(even, below_even, below_odd))
    for p in range(8):
        targets(p, cols, natural[pl.ds(p, 8, stride=8), :])


def descend(levels, etas, betas, diags, others):
    for level in range(3):
        here = levels[level]
        here.setup(etas[level], betas[level], diags[level])
        here.first_sweeps(others[level])
        if level < 2:
            halve_planes(etas[level], etas[level + 1], here.planes, 0.5)
            halve_planes(betas[level], betas[level + 1], here.planes, 1.0)

            def store(k, p, value, target=levels[level + 1].force):
                target[k, p] = value

            here.restrict(diags[level], store)
    found = [None, None]

    def keep(k, p, value):
        found[k] = value

    levels[2].restrict(diags[2], keep)
    eta = 0.5 * halve_lanes(etas[2][0] + etas[2][1])
    beta = halve_lanes(betas[2][0] + betas[2][1])
    return found + [eta, beta]


def plane_targets(row, levels, etas, betas):
    def target(p, cols, plane):
        if row < 2:
            levels[0].force[row, p, :, cols] = plane
        else:
            (etas, betas)[row - 2][0][p, :, cols] = plane

    return target


def main_kernel(forcing, coef, rows_even, rows_odd, *refs):
    levels = levels_of(refs)
    top, natural = refs[24:26]
    etas, betas, diags, others = (refs[26 + 3 * i : 29 + 3 * i] for i in range(4))
    for row in range(4):
        source = forcing if row < 2 else coef
        target = plane_targets(row, levels, etas, betas)
        for i in range(COLS // 128):
            cols = slice(128 * i, 128 * i + 128)
            halo = (rows_even[row, :, cols], rows_odd[row, :, cols])
            spread(halo, source[row % 2, :, cols], halo, natural.at[8 * row + i], target, cols)
    for i, value in enumerate(descend(levels, etas, betas, diags, others)):
        top[i] = value


def rim_kernel(
    forcing,
    coef,
    got_odd,
    got_even,
    rows_even,
    rows_odd,
    corner_odd,
    corner_even,
    top,
    late_force,
    late_field,
    *refs,
):
    levels = levels_of(refs)
    near, far, natural = refs[24:27]
    etas, betas, diags, others = (refs[27 + 3 * i : 30 + 3 * i] for i in range(4))
    for row in range(4):
        source = forcing if row < 2 else coef
        target = plane_targets(row, levels, etas, betas)
        sides = side_columns(got_even[row], got_odd[row])
        for i in range(4):
            if i in (0, 3):
                part = slice(0, EDGE) if i == 0 else slice(EDGE, 2 * EDGE)
                halo = (corner_even[row, :, part], corner_odd[row, :, part])
                own = sides[i // 3]
            else:
                part = slice(0, EDGE) if i == 1 else slice(COLS - EDGE, COLS)
                halo = (rows_even[row, :, part], rows_odd[row, :, part])
                own = source[row % 2, :, part]
            spread(halo, own, halo, natural.at[4 * row + i], target, slice(128 * i, 128 * i + 128))
    rim = descend(levels, etas, betas, diags, others)
    both = [merge(3, top[i], rim[i]) for i in range(4)]
    head = jnp.concatenate([own_rows(both[0], both[1]), own_rows(both[2], both[3])], axis=1)
    far[...] = head
    at = head.shape[1]
    near[:, 0:at] = head
    for source, rims, shift in ((late_field, levels[2].field, 1), (late_force, levels[2].force, 0)):
        for p in range(2):
            parts = [merge(2, source[k, p + shift], rims[k, p + shift]) for k in range(2)]
            near[:, at : at + MERGED[2]] = own_rows(parts[0], parts[1])
            at += MERGED[2]


def merge_kernel(*refs):
    late = refs[48:]
    mains, rims = levels_of(refs[:24]), levels_of(refs[24:48])

    def joined(name, *index):
        return merge(0, getattr(mains[0], name)[index], getattr(rims[0], name)[index])

    names = ("right", "left", "cross_right", "cross_left", "scale")
    for i, name in enumerate(names):
        for p in range(8):
            value = joined(name, p)
            late[i][p] = own_rows(value, value)
            if p in (0, 7):
                late[8][i, p // 7] = value
    for p in range(9):
        value = joined("below", p)
        late[5][p] = own_rows(value, value)
        if p in (0, 1, 7, 8):
            late[9][(0, 1, 7, 8).index(p)] = value
    for p in range(8):
        force = [joined("force", k, p) for k in range(2)]
        field = [joined("field", k, p + 1) for k in range(2)]
        late[6][p] = own_rows(force[0], force[1])
        late[7][p] = own_rows(field[0], field[1])
        for k in range(2):
            if p in (0, 7):
                late[10][k, p // 7] = force[k]
            if p in (0, 1, 6, 7):
                late[11][k, (0, 1, 6, 7).index(p)] = field[k]
    for level in (1, 2):
        for i in range(8):
            main, rim = (refs[24 * j + 8 * level + i] for j in range(2))
            target = late[4 + 8 * level + i]
            planes = PLANES[level]
            if i < 6:
                for p in range(main.shape[0]):
                    target[p] = merge(level, main[p], rim[p])
            else:
                for k in range(2):
                    for p in range(i - 6, planes + i - 6):
                        target[k, p] = merge(level, main[k, p], rim[k, p])


def finest_up(refs, coarse, packed, next_packed, natural, velocity, sems):
    right, left, cross_right, cross_left, scale, below, force, field = refs[:8]
    edge_coef, edge_below, edge_force, edge_field = refs[8:]
    wide = MERGED[0]
    edges = [[None] * 8, [None] * 8]
    for p in range(0, 8, 2):
        adds = [double_lanes(coarse(k, p // 2), wide) for k in range(2)]
        both = own_rows(adds[0], adds[1])
        for q in (p, p + 1):
            packed[q] = field[q] + both
            if q in (0, 1, 6, 7):
                for k in range(2):
                    edges[k][q] = edge_field[k, (0, 1, 6, 7).index(q)] + adds[k]
    found = {}
    for i, p in enumerate((0, 7)):
        under = [edges[k][1] if p == 0 else from_below(edges[k][0]) for k in range(2)]
        over = [from_above(edges[k][7]) if p == 0 else edges[k][6] for k in range(2)]
        for k in range(2):
            terms = gather_terms(
                edge_coef[0, i],
                edge_coef[1, i],
                edge_coef[2, i],
                edge_coef[3, i],
                edge_below[2 * i + 1],
                edge_below[2 * i],
                edges[k][p],
                under[k],
                over[k],
                under[1 - k] - over[1 - k],
                edge_force[k, i],
            )
            found[k, p] = KEEP * edges[k][p] + edge_coef[4, i] * terms
    next_packed[1] = own_rows(found[0, 0], found[1, 0])
    next_packed[8] = own_rows(found[0, 7], found[1, 7])
    next_packed[0] = own_rows(from_above(found[0, 7]), from_above(found[1, 7]))
    next_packed[9] = own_rows(from_below(found[0, 0]), from_below(found[1, 0]))

    def sweep(p, above, here, under, first, count, part):
        mid = slice(128, 128 + 128 * count)
        low, high = slice(0, 128 + 128 * count), slice(128, 256 + 128 * count)
        over, w, down = part(above), part(here), part(under)
        step = pltpu.roll(down - over, 4, axis=0)
        west = from_left((part(right[p]) * w + part(cross_right[p]) * step)[:, low])[:, 128:]
        east = from_right((part(left[p]) * w - part(cross_left[p]) * step)[:, high])[:, : 128 * count]
        cols = slice(128 * first, 128 * (first + count))
        terms = (force[p][:, cols] + (west + east)) + (below[p + 1][:, cols] * down[:, mid] + below[p][:, cols] * over[:, mid])
        return KEEP * w[:, mid] + scale[p][:, cols] * terms

    for p in range(1, 7):
        over, here, under = packed[p - 1], packed[p], packed[p + 1]
        terms = gather_terms(
            right[p],
            left[p],
            cross_right[p],
            cross_left[p],
            below[p + 1],
            below[p],
            here,
            under,
            over,
            pltpu.roll(under - over, 4, axis=0),
            force[p],
        )
        next_packed[p + 1] = KEEP * here + scale[p] * terms
    copies = []
    first = 0
    for count in (4, 2, 2):

        def part(x):
            end = x[:, 128 * max(first - 1, 0) : 128 * (first + count + 1)]
            return end if first else jnp.concatenate([x[:, wide - 128 :], end], axis=1)

        for p in range(8):
            done = sweep(p, next_packed[p], next_packed[p + 1], next_packed[p + 2], first, count, part)
            for i in range(count):
                tile = done[:, 128 * i : 128 * i + 128]
                for k in range(2):
                    natural[k, first + i, pl.ds(p, 4, stride=8), :] = tile[4 * k : 4 * k + 4]
        for i in range(first, first + count):
            for k in range(2):
                target = velocity.at[k, :, pl.ds(128 * i, 128)]
                copy = pltpu.make_async_copy(natural.at[k, i], target, sems.at[2 * i + k])
                copy.start()
                copies.append(copy)
        first += count
    for copy in copies:
        copy.wait()


def up_kernel(far, near_even, near_odd, far_even, far_odd, *refs):
    levels = [None] + [Level(PLANES[i], refs[4 + 8 * i : 12 + 8 * i]) for i in (1, 2)]
    velocity, natural, sems, packed, next_packed, late_force, late_field = refs[28:35]
    fields, others = (None,) + refs[35:37], (None,) + refs[37:39]
    gy = lax.axis_index("gy")
    count = lax.axis_size("gy")
    even = gy % 2 == 0

    def above(part):
        return jnp.where(gy == 0, 0.0, jnp.where(even, near_odd[:, part], near_even[:, part]))

    def below(part):
        return jnp.where(gy == count - 1, 0.0, jnp.where(even, near_even[:, part], near_odd[:, part]))

    def sublanes(like):
        return lax.broadcasted_iota(jnp.int32, like.shape, 0)

    def stacked(part):
        low = gy // 2 % 2 == 0
        m2 = jnp.where(gy < 2, 0.0, jnp.where(low, far_odd[:, part], far_even[:, part]))
        p2 = jnp.where(gy > count - 3, 0.0, jnp.where(low, far_even[:, part], far_odd[:, part]))
        m1, p1, own = above(part), below(part), far[:, part]
        upper = sublanes(own) < 4

        def halves(x, y, second):
            if second:
                return jnp.where(upper, pltpu.roll(x, 4, axis=0), y)
            return jnp.where(upper, x, pltpu.roll(y, 4, axis=0))

        zero = jnp.zeros_like(own)
        return [
            jnp.concatenate([halves(m2, m1, s), halves(own, p1, s), halves(p2, zero, s)], axis=0)
            for s in (False, True)
        ]

    force = stacked(slice(0, MERGED[3]))
    eta, beta = stacked(slice(MERGED[3], 2 * MERGED[3]))
    right, left, under, over, cross_right, cross_left, diag = coefficients(eta, beta, from_below(eta), from_above)
    scale = OMEGA / diag
    field = [scale * force[0], scale * force[1]]
    for _ in range(5):
        downs = [from_below(x) for x in field]
        ups = [from_above(x) for x in field]
        steps = [downs[k] - ups[k] for k in range(2)]
        field = [
            KEEP * field[k]
            + scale
            * gather_terms(
                right, left, cross_right, cross_left, under, over, field[k], downs[k], ups[k], steps[1 - k], force[k]
            )
            for k in range(2)
        ]
    coarsest = []
    for k in range(2):
        a, b = pltpu.roll(field[k][0:8], 2, axis=0), pltpu.roll(field[k][8:16], 2, axis=0)
        coarsest.append(jnp.where(sublanes(a) < 2, a, b))
    at = 2 * MERGED[3]
    for target, own, shift in ((late_field, levels[2].field, 1), (late_force, levels[2].force, 0)):
        for p in range(2):
            part = slice(at, at + MERGED[2])
            up, down = above(part), below(part)
            for k in range(2):
                turn = 2 if k else 6
                a, b = pltpu.roll(up, turn, axis=0), pltpu.roll(down, turn, axis=0)
                sub = sublanes(a)
                target[k, p + shift] = jnp.where(sub < 2, a, jnp.where(sub < 6, own[k, p + shift], b))
            at += MERGED[2]
    levels[2].force = late_force
    levels[2].field = late_field
    coarse = lambda k, p: coarsest[k]
    for level in (2, 1):
        levels[level].last_sweeps(coarse, fields[level], others[level])
        coarse = lambda k, p, result=fields[level]: result[k, p + 1]
    finest_up(refs[:12], coarse, packed, next_packed, natural, velocity, sems)


def swap(x, axis, odd):
    rows, cols = lax.axis_size("gy"), lax.axis_size("gx")
    count, across = (rows, cols) if axis == "gy" else (cols, rows)
    pairs = []
    for j in range(across):
        for i in range(odd, count - 1, 2):
            pairs += [((i, j), (i + 1, j)), ((i + 1, j), (i, j))]
        if odd:
            pairs += [((i, j), (i, j ^ 1)) for i in (0, count - 1)]
    place = (lambda i, j: j * rows + i) if axis == "gy" else (lambda i, j: i * rows + j)
    return lax.ppermute(x, ("gx", "gy"), [(place(*a), place(*b)) for a, b in pairs])


def swap_far(x, odd):
    count = lax.axis_size("gy")
    pairs = []
    for i in range(0, count - 2):
        if i // 2 % 2 == odd:
            pairs += [(i, i + 2), (i + 2, i)]
    if odd:
        pairs += [(i, i ^ 1) for i in (0, 1, count - 2, count - 1)]
    return lax.ppermute(x, "gy", pairs)


def local(forcing, ice_mask, viscosity_class, drag_class, viscosity_table, drag_table):
    inputs = [
        pltpu.with_memory_space_constraint(x, pltpu.HBM)
        for x in (viscosity_table, drag_table, forcing, ice_mask, viscosity_class, drag_class)
    ]
    hbm = [pl.BlockSpec(memory_space=pltpu.HBM)] * 6
    table = pltpu.SMEM((16,), jnp.float32)
    coef, side_even, side_odd, main_even, main_odd = pl.pallas_call(
        lookup_kernel,
        out_shape=(shape(2, ROWS, COLS),) + (shape(4, ROWS, EDGE),) * 2 + (shape(4, HALO, COLS),) * 2,
        in_specs=hbm,
        out_specs=tuple(vmem(5)),
        scratch_shapes=[[table, table], pltpu.VMEM((3, ROWS, COLS), jnp.int32), pltpu.SemaphoreType.DMA((9,))],
        compiler_params=params(),
        name="lookup",
    )(*inputs)
    got_odd = swap(side_odd, "gx", 1)
    got_even = swap(side_even, "gx", 0)
    rows_odd = swap(main_odd, "gy", 1)
    send_even, send_odd = pl.pallas_call(
        corner_kernel,
        out_shape=(shape(4, HALO, 2 * EDGE),) * 2,
        in_specs=vmem(2),
        out_specs=tuple(vmem(2)),
        compiler_params=params(),
        name="corners",
    )(got_odd, got_even)
    main_even, send_even = lax.optimization_barrier((main_even, send_even))
    corner_odd = swap(send_odd, "gy", 1)
    corner_even = swap(send_even, "gy", 0)
    rows_even = swap(main_even, "gy", 0)

    def kept(widths):
        return [dims for level in range(3) for dims in Level.shapes(level, widths)]

    def scratch(dims):
        return [pltpu.VMEM(one, jnp.float32) for one in dims]

    def rims(widths):
        return [(2, PLANES[i] + 2, 8, widths[i]) for i in range(3)]

    def work(widths):
        return scratch([(32, 64, 128)] + [(PLANES[i], 8, widths[i]) for i in range(3)] * 3 + rims(widths))

    *main, top = pl.pallas_call(
        main_kernel,
        out_shape=tuple(shape(*dims) for dims in kept(MAIN) + [(4, 8, MAIN[3])]),
        in_specs=vmem(4),
        out_specs=tuple(vmem(25)),
        scratch_shapes=work(MAIN),
        compiler_params=params(),
        name="main",
    )(forcing, coef, rows_even, rows_odd)
    near_lanes = 2 * MERGED[3] + 4 * MERGED[2]
    *rim, near, far = pl.pallas_call(
        rim_kernel,
        out_shape=tuple(shape(*dims) for dims in kept(RIM) + [(8, near_lanes), (8, 2 * MERGED[3])]),
        in_specs=vmem(11),
        out_specs=tuple(vmem(26)),
        scratch_shapes=work(RIM),
        compiler_params=params(),
        name="rim",
    )(forcing, coef, got_odd, got_even, rows_even, rows_odd, corner_odd, corner_even, top, main[22], main[23])
    near_even = swap(near, "gy", 0)
    near_odd = swap(near, "gy", 1)
    far_even = swap_far(far, 0)
    far_odd = swap_far(far, 1)
    wide = MERGED[0]
    finest = [(8, 8, wide)] * 5 + [(9, 8, wide)] + [(8, 8, wide)] * 2
    finest += [(5, 2, 8, wide), (4, 8, wide), (2, 2, 8, wide), (2, 4, 8, wide)]
    merged = pl.pallas_call(
        merge_kernel,
        out_shape=tuple(shape(*dims) for dims in finest + kept(MERGED)[8:]),
        in_specs=vmem(48),
        out_specs=tuple(vmem(28)),
        compiler_params=params(),
        name="merge",
    )(*main, *rim)
    late = [(8, 8, wide), (10, 8, wide), (2, 2, 8, MERGED[2]), (2, 4, 8, MERGED[2])]
    return pl.pallas_call(
        up_kernel,
        out_shape=shape(2, ROWS, COLS),
        in_specs=vmem(33),
        out_specs=pl.BlockSpec(memory_space=pltpu.HBM),
        scratch_shapes=scratch([(2, COLS // 128, ROWS, 128)])
        + [pltpu.SemaphoreType.DMA((2 * COLS // 128,))]
        + scratch(late + rims(MERGED)[1:] + rims(MERGED)[1:]),
        compiler_params=params(),
        name="up",
    )(far, near_even, near_odd, far_even, far_odd, *merged)


def solution(mesh):
    in_specs = (P(None, "gy", "gx"), P("gy", "gx"), P("gy", "gx"), P("gy", "gx"), P(), P())
    out_specs = P(None, "gy", "gx")
    return jax.shard_map(local, mesh=mesh, in_specs=in_specs, out_specs=out_specs, check_vma=False)
```

```python
import jax
import jax.numpy as jnp
from jax import lax
from jax.experimental import pallas as pl
from jax.experimental.pallas import tpu as pltpu
from jax.sharding import PartitionSpec as P

OMEGA = 0.6
KEEP = 1.0 - OMEGA
ROWS, COLS = 32, 1024
EDGE = 128
HALO = 16
PLANES = (8, 4, 2)
MAIN = (1024, 512, 256, 128)
RIM = (512, 256, 128, 128)
MERGED = (1152, 640, 384, 256)
VMEM_LIMIT = 16 * 1024 * 1024


def vmem(count):
    return [pl.BlockSpec(memory_space=pltpu.VMEM)] * count


def params():
    return pltpu.CompilerParams(vmem_limit_bytes=VMEM_LIMIT)


def shape(*dims):
    return jax.ShapeDtypeStruct(dims, jnp.float32)


def from_left(x):
    return pltpu.roll(x, 1, axis=1)


def from_right(x):
    return pltpu.roll(x, x.shape[1] - 1, axis=1)


def from_above(x):
    return pltpu.roll(x, 1, axis=0)


def from_below(x):
    return pltpu.roll(x, x.shape[0] - 1, axis=0)


def tiles(x):
    return [x[:, i : i + 128] for i in range(0, x.shape[1], 128)]


def lane(kind):
    return lax.broadcasted_iota(jnp.int32, (8, 128), kind)


def pick(x, index):
    return jnp.take_along_axis(x, index, axis=1, mode="promise_in_bounds")


def halve_lanes(x):
    at = lane(1)
    even = at % 2 == 0
    index = jnp.where(at < 64, 2 * at, 2 * at - 127)
    parts = tiles(x)
    if len(parts) % 2:
        parts.append(jnp.zeros_like(parts[0]))
    out = []
    for a, b in zip(parts[0::2], parts[1::2]):
        out.append(pick(jnp.where(even, a, b), index) + pick(jnp.where(even, b, a), index ^ 1))
    return jnp.concatenate(out, axis=1)


def double_lanes(x, lanes):
    at = lane(1)
    parts = tiles(x)
    count = lanes // 128 - 1
    out = [pick(parts[i // 2], at // 2 + 64 * (i % 2)) for i in range(count)]
    out.append(pick(parts[-1], jnp.where(at < 64, at // 2, at // 2 + 64)))
    return jnp.concatenate(out, axis=1)


def merge_tiles(level, main, rim):
    at = lane(1)
    if level == 0:
        low, left, right, high = rim
    else:
        low = left = pltpu.roll(rim[0], (64, 96, 112)[level - 1], axis=1)
        high = right = pltpu.roll(rim[-1], (64, 32, 80)[level - 1], axis=1)
    out = list(main)
    out[0] = jnp.where(at < 64 >> level, left, out[0])
    out[-1] = jnp.where(at < 128 - (64 >> level), out[-1], right)
    beside = jnp.where(at < 64, high, low)
    if level > 1:
        beside = jnp.where((at < EDGE >> level) | (at >= 128 - (EDGE >> level)), beside, 0.0)
    return out + [beside]


def merge(level, main, rim):
    return jnp.concatenate(merge_tiles(level, tiles(main), tiles(rim)), axis=1)


def coefficients(eta, beta, eta_below, face_above):
    ice = eta > 0.0
    eta_right = from_right(eta)
    right = jnp.where(ice & (eta_right > 0.0), 0.5 * (eta + eta_right), 0.0)
    left = from_left(right)
    below = jnp.where(ice & (eta_below > 0.0), 0.5 * (eta + eta_below), 0.0)
    above = face_above(below)
    base = beta + jnp.where(ice, 0.0, 1.0)
    diag = base + ((right + left) + (below + above))
    return right, left, below, above, 0.05 * eta_right, 0.05 * from_left(eta), diag


def gather_terms(right, left, cross_right, cross_left, below, above, here, under, over, other_step, force):
    from_west = from_left(right * here + cross_right * other_step)
    from_east = from_right(left * here - cross_left * other_step)
    return (force + (from_west + from_east)) + (below * under + above * over)


class Level:
    def __init__(self, planes, refs):
        self.planes = planes
        self.right, self.left, self.cross_right, self.cross_left, self.below, self.scale, self.force, self.field = refs

    @staticmethod
    def shapes(level, widths):
        planes, lanes = PLANES[level], widths[level]
        one = [(planes, 8, lanes)] * 4 + [(planes + 1, 8, lanes), (planes, 8, lanes)]
        return one + [(2, planes, 8, lanes), (2, planes + 2, 8, lanes)]

    def wrap(self, field):
        for k in range(2):
            field[k, 0] = from_above(field[k, self.planes])
            field[k, self.planes + 1] = from_below(field[k, 1])

    def terms(self, p, field):
        out = []
        steps = [field[k, p + 2] - field[k, p] for k in range(2)]
        for k in range(2):
            out.append(
                gather_terms(
                    self.right[p],
                    self.left[p],
                    self.cross_right[p],
                    self.cross_left[p],
                    self.below[p + 1],
                    self.below[p],
                    field[k, p + 1],
                    field[k, p + 2],
                    field[k, p],
                    steps[1 - k],
                    self.force[k, p],
                )
            )
        return out

    def sweep(self, source, target):
        for p in range(self.planes):
            terms = self.terms(p, source)
            for k in range(2):
                target[k, p + 1] = KEEP * source[k, p + 1] + self.scale[p] * terms[k]

    def setup(self, eta, beta, diag):
        planes = self.planes
        for p in range(planes):
            here = eta[p]
            ice = here > 0.0
            next_eta = eta[p + 1] if p + 1 < planes else from_below(eta[0])
            self.below[p + 1] = jnp.where(ice & (next_eta > 0.0), 0.5 * (here + next_eta), 0.0)
        self.below[0] = from_above(self.below[planes])
        for p in range(planes):
            here = eta[p]
            ice = here > 0.0
            eta_right = from_right(here)
            right = jnp.where(ice & (eta_right > 0.0), 0.5 * (here + eta_right), 0.0)
            left = from_left(right)
            base = beta[p] + jnp.where(ice, 0.0, 1.0)
            total = base + ((right + left) + (self.below[p + 1] + self.below[p]))
            self.right[p] = right
            self.left[p] = left
            self.cross_right[p] = 0.05 * eta_right
            self.cross_left[p] = 0.05 * from_left(here)
            diag[p] = total
            self.scale[p] = OMEGA / total

    def first_sweeps(self, other):
        for k in range(2):
            for p in range(self.planes):
                other[k, p + 1] = self.scale[p] * self.force[k, p]
        self.wrap(other)
        self.sweep(other, self.field)
        self.wrap(self.field)

    def restrict(self, diag, target):
        for p in range(0, self.planes, 2):
            rest = [0.0, 0.0]
            for q in (p, p + 1):
                terms = self.terms(q, self.field)
                for k in range(2):
                    rest[k] = rest[k] + (terms[k] - diag[q] * self.field[k, q + 1])
            for k in range(2):
                target(k, p // 2, halve_lanes(rest[k]))

    def last_sweeps(self, coarse, result, other):
        for k in range(2):
            for p in range(0, self.planes, 2):
                add = double_lanes(coarse(k, p // 2), self.field.shape[-1])
                result[k, p + 1] = self.field[k, p + 1] + add
                result[k, p + 2] = self.field[k, p + 2] + add
        self.wrap(result)
        self.sweep(result, other)
        self.wrap(other)
        self.sweep(other, result)


def halve_planes(source, target, planes, scale):
    for p in range(0, planes, 2):
        both = halve_lanes(source[p] + source[p + 1])
        target[p // 2] = scale * both if scale != 1.0 else both


def look_up(tables, classes, ice):
    at = lane(1)
    rows = []
    for table in tables:
        row = jnp.zeros((8, 128), jnp.float32)
        for i in range(16):
            row = jnp.where(at == i, table[i], row)
        rows.append(row)
    return [pick(row, part) * ice for row, part in zip(rows, classes)]


def start_all(pairs, sems):
    copies = [pltpu.make_async_copy(a, b, sems.at[i]) for i, (a, b) in enumerate(pairs)]
    for copy in copies:
        copy.start()
    return copies


def halves_of(axis, size, part):
    even = lax.axis_index(axis) % 2 == 0
    first = pl.multiple_of(jnp.where(even, size - part, 0), part)
    return first, pl.multiple_of(size - part - first, part)


def group(index):
    return (lane(1) >= 8 * index) & (lane(1) < 8 * index + 8)


def pack_side(parts, side):
    near = lane(1) < 64
    out = []
    for pair in (0, 2):
        for r in range(4):
            x, y = parts[pair][r], parts[pair + 1][r]
            x, y = (x, pltpu.roll(y, 64, axis=1)) if side == 0 else (pltpu.roll(x, 64, axis=1), y)
            out.append(jnp.where(near, x, y))
    rest = jnp.zeros_like(out[0])
    for i in range(16):
        start = 64 if side == 0 else 56
        rest = jnp.where(group(i), pltpu.roll(parts[i // 4][i % 4], (8 * i - start) % 128, axis=1), rest)
    return out + [rest]


def unpack_side(tile, side):
    out = []
    near = lane(1) < 64 if side == 0 else lane(1) >= 64
    start = 64 if side == 0 else 56
    for row in range(4):
        for r in range(4):
            x = tile[4 * (row // 2) + r]
            if row % 2 == (0 if side else 1):
                x = pltpu.roll(x, 64, axis=1)
            rest = pltpu.roll(tile[8], (start - 8 * (4 * row + r)) % 128, axis=1)
            out.append(jnp.where(near, x, jnp.where(group(start // 8), rest, 0.0)))
    return out


def lookup_kernel(v_table, d_table, forcing, mask, v_class, d_class, coef, *refs):
    sides, rows = refs[0:2], refs[2:4]
    tables, ints, edges, sems = refs[4:]
    pairs = [(v_table, tables[0]), (d_table, tables[1])]
    pairs += [(source, ints.at[i]) for i, source in enumerate((mask, v_class, d_class))]
    row_starts = halves_of("gy", ROWS, HALO)
    for i, start in enumerate((0, COLS - EDGE)):
        pairs.append((forcing.at[:, :, pl.ds(start, EDGE)], edges.at[i]))
    for start, target in zip(row_starts, rows):
        pairs.append((forcing.at[:, pl.ds(start, HALO), :], target.at[0:2]))
    copies = start_all(pairs, sems)
    for copy in copies[:5]:
        copy.wait()
    for r in range(0, ROWS, 8):
        for c in range(0, COLS, 128):
            part = (slice(r, r + 8), slice(c, c + 128))
            ice = ints[(0,) + part].astype(jnp.float32)
            found = look_up(tables, [ints[(1,) + part], ints[(2,) + part]], ice)
            for k in range(2):
                coef[(k,) + part] = found[k]
    for copy in copies[5:7]:
        copy.wait()
    even = lax.axis_index("gx") % 2 == 0
    messages = []
    for side, start in enumerate((0, COLS - EDGE)):
        parts = [[edges[side, k, 8 * r : 8 * r + 8] for r in range(4)] for k in range(2)]
        parts += [[coef[k, 8 * r : 8 * r + 8, start : start + EDGE] for r in range(4)] for k in range(2)]
        messages.append(pack_side(parts, side))
    for i in range(9):
        low, high = messages[0][i], messages[1][i]
        sides[0][8 * i : 8 * i + 8] = jnp.where(even, high, low)
        sides[1][8 * i : 8 * i + 8] = jnp.where(even, low, high)
    for k in range(2):
        for start, target in zip(row_starts, rows):
            target[2 + k] = coef[k, pl.ds(start, HALO), :]
    for copy in copies[7:]:
        copy.wait()


def corner_kernel(got_odd, got_even, sides, send_even, send_odd):
    gx = lax.axis_index("gx")
    even = gx % 2 == 0
    for side in range(2):
        end = gx == (0 if side == 0 else lax.axis_size("gx") - 1)

        def tile(i):
            rows = slice(8 * i, 8 * i + 8)
            a, b = got_even[rows], got_odd[rows]
            return jnp.where(end, 0.0, jnp.where(even, b, a) if side == 0 else jnp.where(even, a, b))

        parts = unpack_side([tile(i) for i in range(9)], 1 - side)
        for i, part in enumerate(parts):
            sides[side, i // 4, 8 * (i % 4) : 8 * (i % 4) + 8] = part
    for start, target in zip(halves_of("gy", ROWS, HALO), (send_even, send_odd)):
        for row in range(4):
            for side in range(2):
                target[row, :, side * EDGE : (side + 1) * EDGE] = sides[side, row, pl.ds(start, HALO)]


def own_rows(a, b):
    upper = lax.broadcasted_iota(jnp.int32, a.shape, 0) < 4
    return jnp.where(upper, pltpu.roll(a, 6, axis=0), pltpu.roll(b, 2, axis=0))


def levels_of(refs):
    return [Level(PLANES[i], refs[8 * i : 8 * i + 8]) for i in range(3)]


def spread(above, own, below, natural, targets, cols):
    gy = lax.axis_index("gy")
    even = gy % 2 == 0
    (above_even, above_odd), (below_even, below_odd) = above, below
    natural[0:HALO] = jnp.where(gy == 0, 0.0, jnp.where(even, above_odd, above_even))
    natural[HALO : HALO + ROWS] = own
    natural[HALO + ROWS :] = jnp.where(gy == lax.axis_size("gy") - 1, 0.0, jnp.where(even, below_even, below_odd))
    for p in range(8):
        targets(p, cols, natural[pl.ds(p, 8, stride=8), :])


def descend(levels, etas, betas, diags, others):
    for level in range(3):
        here = levels[level]
        here.setup(etas[level], betas[level], diags[level])
        here.first_sweeps(others[level])
        if level < 2:
            halve_planes(etas[level], etas[level + 1], here.planes, 0.5)
            halve_planes(betas[level], betas[level + 1], here.planes, 1.0)

            def store(k, p, value, target=levels[level + 1].force):
                target[k, p] = value

            here.restrict(diags[level], store)
    found = [None, None]

    def keep(k, p, value):
        found[k] = value

    levels[2].restrict(diags[2], keep)
    eta = 0.5 * halve_lanes(etas[2][0] + etas[2][1])
    beta = halve_lanes(betas[2][0] + betas[2][1])
    return found + [eta, beta]


def plane_targets(row, levels, etas, betas):
    def target(p, cols, plane):
        if row < 2:
            levels[0].force[row, p, :, cols] = plane
        else:
            (etas, betas)[row - 2][0][p, :, cols] = plane

    return target


def main_kernel(forcing, coef, rows_even, rows_odd, *refs):
    levels = levels_of(refs)
    top, natural = refs[24:26]
    etas, betas, diags, others = (refs[26 + 3 * i : 29 + 3 * i] for i in range(4))
    for row in range(4):
        source = forcing if row < 2 else coef
        target = plane_targets(row, levels, etas, betas)
        for i in range(COLS // 128):
            cols = slice(128 * i, 128 * i + 128)
            halo = (rows_even[row, :, cols], rows_odd[row, :, cols])
            spread(halo, source[row % 2, :, cols], halo, natural.at[8 * row + i], target, cols)
    for i, value in enumerate(descend(levels, etas, betas, diags, others)):
        top[i] = value


def rim_kernel(
    forcing,
    coef,
    sides,
    rows_even,
    rows_odd,
    corner_odd,
    corner_even,
    top,
    late_force,
    late_field,
    *refs,
):
    levels = levels_of(refs)
    near_even, near_odd, far, natural = refs[24:28]
    etas, betas, diags, others = (refs[28 + 3 * i : 31 + 3 * i] for i in range(4))
    for row in range(4):
        source = forcing if row < 2 else coef
        target = plane_targets(row, levels, etas, betas)
        for i in range(4):
            if i in (0, 3):
                part = slice(0, EDGE) if i == 0 else slice(EDGE, 2 * EDGE)
                halo = (corner_even[row, :, part], corner_odd[row, :, part])
                own = sides[i // 3, row]
            else:
                part = slice(0, EDGE) if i == 1 else slice(COLS - EDGE, COLS)
                halo = (rows_even[row, :, part], rows_odd[row, :, part])
                own = source[row % 2, :, part]
            spread(halo, own, halo, natural.at[4 * row + i], target, slice(128 * i, 128 * i + 128))
    rim = descend(levels, etas, betas, diags, others)
    both = [merge(3, top[i], rim[i]) for i in range(4)]
    head = jnp.concatenate([own_rows(both[0], both[1]), own_rows(both[2], both[3])], axis=1)
    far[...] = head
    at = head.shape[1]
    w, f = (
        [[merge(2, source[k, p + i], rims[k, p + i]) for p in range(2)] for k in range(2)]
        for i, source, rims in ((1, late_field, levels[2].field), (0, late_force, levels[2].force))
    )
    messages = []
    for picks in (
        lambda k: [(w[k][0], 4), (w[k][0], 5), (w[k][1], 4), (f[k][1], 4)],
        lambda k: [(w[k][0], 3), (w[k][1], 2), (w[k][1], 3), (f[k][0], 3)],
    ):
        rows = picks(0) + picks(1)
        message = pltpu.roll(rows[0][0], 8 - rows[0][1], axis=0)
        sub = lax.broadcasted_iota(jnp.int32, message.shape, 0)
        for i, (x, g) in enumerate(rows):
            if i:
                message = jnp.where(sub == i, pltpu.roll(x, (i - g) % 8, axis=0) if i != g else x, message)
        messages.append(message)
    even = lax.axis_index("gy") % 2 == 0
    for target, flag in ((near_even, even), (near_odd, jnp.logical_not(even))):
        target[:, 0:at] = head
        target[:, at:] = jnp.where(flag, messages[0], messages[1])


def merge_kernel(*refs):
    late = refs[48:]
    mains, rims = levels_of(refs[:24]), levels_of(refs[24:48])

    def joined(name, *index):
        return merge(0, getattr(mains[0], name)[index], getattr(rims[0], name)[index])

    names = ("right", "left", "cross_right", "cross_left", "scale")
    for i, name in enumerate(names):
        for p in range(8):
            value = joined(name, p)
            late[i][p] = own_rows(value, value)
            if p in (0, 7):
                late[8][i, p // 7] = value
    for p in range(9):
        value = joined("below", p)
        late[5][p] = own_rows(value, value)
        if p in (0, 1, 7, 8):
            late[9][(0, 1, 7, 8).index(p)] = value
    for p in range(8):
        force = [joined("force", k, p) for k in range(2)]
        field = [joined("field", k, p + 1) for k in range(2)]
        late[6][p] = own_rows(force[0], force[1])
        late[7][p] = own_rows(field[0], field[1])
        for k in range(2):
            if p in (0, 7):
                late[10][k, p // 7] = force[k]
            if p in (0, 1, 6, 7):
                late[11][k, (0, 1, 6, 7).index(p)] = field[k]
    for level in (1, 2):
        for i in range(8):
            main, rim = (refs[24 * j + 8 * level + i] for j in range(2))
            target = late[4 + 8 * level + i]
            planes = PLANES[level]
            if i < 6:
                for p in range(main.shape[0]):
                    target[p] = merge(level, main[p], rim[p])
            else:
                for k in range(2):
                    for p in range(i - 6, planes + i - 6):
                        target[k, p] = merge(level, main[k, p], rim[k, p])


def finest_up(refs, coarse, packed, next_packed, natural, velocity, sems):
    right, left, cross_right, cross_left, scale, below, force, field = refs[:8]
    edge_coef, edge_below, edge_force, edge_field = refs[8:]
    wide = MERGED[0]
    edges = [[None] * 8, [None] * 8]
    for p in range(0, 8, 2):
        adds = [double_lanes(coarse(k, p // 2), wide) for k in range(2)]
        both = own_rows(adds[0], adds[1])
        for q in (p, p + 1):
            packed[q] = field[q] + both
            if q in (0, 1, 6, 7):
                for k in range(2):
                    edges[k][q] = edge_field[k, (0, 1, 6, 7).index(q)] + adds[k]
    found = {}
    for i, p in enumerate((0, 7)):
        under = [edges[k][1] if p == 0 else from_below(edges[k][0]) for k in range(2)]
        over = [from_above(edges[k][7]) if p == 0 else edges[k][6] for k in range(2)]
        for k in range(2):
            terms = gather_terms(
                edge_coef[0, i],
                edge_coef[1, i],
                edge_coef[2, i],
                edge_coef[3, i],
                edge_below[2 * i + 1],
                edge_below[2 * i],
                edges[k][p],
                under[k],
                over[k],
                under[1 - k] - over[1 - k],
                edge_force[k, i],
            )
            found[k, p] = KEEP * edges[k][p] + edge_coef[4, i] * terms
    next_packed[1] = own_rows(found[0, 0], found[1, 0])
    next_packed[8] = own_rows(found[0, 7], found[1, 7])
    next_packed[0] = own_rows(from_above(found[0, 7]), from_above(found[1, 7]))
    next_packed[9] = own_rows(from_below(found[0, 0]), from_below(found[1, 0]))

    def sweep(p, above, here, under, first, count, part):
        mid = slice(128, 128 + 128 * count)
        low, high = slice(0, 128 + 128 * count), slice(128, 256 + 128 * count)
        over, w, down = part(above), part(here), part(under)
        step = pltpu.roll(down - over, 4, axis=0)
        west = from_left((part(right[p]) * w + part(cross_right[p]) * step)[:, low])[:, 128:]
        east = from_right((part(left[p]) * w - part(cross_left[p]) * step)[:, high])[:, : 128 * count]
        cols = slice(128 * first, 128 * (first + count))
        terms = (force[p][:, cols] + (west + east)) + (below[p + 1][:, cols] * down[:, mid] + below[p][:, cols] * over[:, mid])
        return KEEP * w[:, mid] + scale[p][:, cols] * terms

    for p in range(1, 7):
        over, here, under = packed[p - 1], packed[p], packed[p + 1]
        terms = gather_terms(
            right[p],
            left[p],
            cross_right[p],
            cross_left[p],
            below[p + 1],
            below[p],
            here,
            under,
            over,
            pltpu.roll(under - over, 4, axis=0),
            force[p],
        )
        next_packed[p + 1] = KEEP * here + scale[p] * terms
    copies = []
    first = 0
    for count in (4, 2, 2):

        def part(x):
            end = x[:, 128 * max(first - 1, 0) : 128 * (first + count + 1)]
            return end if first else jnp.concatenate([x[:, wide - 128 :], end], axis=1)

        for p in range(8):
            done = sweep(p, next_packed[p], next_packed[p + 1], next_packed[p + 2], first, count, part)
            for i in range(count):
                tile = done[:, 128 * i : 128 * i + 128]
                for k in range(2):
                    natural[k, first + i, pl.ds(p, 4, stride=8), :] = tile[4 * k : 4 * k + 4]
        for i in range(first, first + count):
            for k in range(2):
                target = velocity.at[k, :, pl.ds(128 * i, 128)]
                copy = pltpu.make_async_copy(natural.at[k, i], target, sems.at[2 * i + k])
                copy.start()
                copies.append(copy)
        first += count
    for copy in copies:
        copy.wait()


def up_kernel(far, near_even, near_odd, far_even, far_odd, *refs):
    levels = [None] + [Level(PLANES[i], refs[4 + 8 * i : 12 + 8 * i]) for i in (1, 2)]
    velocity, natural, sems, packed, next_packed, late_force, late_field = refs[28:35]
    fields, others = (None,) + refs[35:37], (None,) + refs[37:39]
    gy = lax.axis_index("gy")
    count = lax.axis_size("gy")
    even = gy % 2 == 0

    def above(part):
        return jnp.where(gy == 0, 0.0, jnp.where(even, near_odd[:, part], near_even[:, part]))

    def below(part):
        return jnp.where(gy == count - 1, 0.0, jnp.where(even, near_even[:, part], near_odd[:, part]))

    def sublanes(like):
        return lax.broadcasted_iota(jnp.int32, like.shape, 0)

    def stacked(part):
        low = gy // 2 % 2 == 0
        m2 = jnp.where(gy < 2, 0.0, jnp.where(low, far_odd[:, part], far_even[:, part]))
        p2 = jnp.where(gy > count - 3, 0.0, jnp.where(low, far_even[:, part], far_odd[:, part]))
        m1, p1, own = above(part), below(part), far[:, part]
        upper = sublanes(own) < 4

        def halves(x, y, second):
            if second:
                return jnp.where(upper, pltpu.roll(x, 4, axis=0), y)
            return jnp.where(upper, x, pltpu.roll(y, 4, axis=0))

        zero = jnp.zeros_like(own)
        return [
            jnp.concatenate([halves(m2, m1, s), halves(own, p1, s), halves(p2, zero, s)], axis=0)
            for s in (False, True)
        ]

    force = stacked(slice(0, MERGED[3]))
    eta, beta = stacked(slice(MERGED[3], 2 * MERGED[3]))
    right, left, under, over, cross_right, cross_left, diag = coefficients(eta, beta, from_below(eta), from_above)
    scale = OMEGA / diag
    field = [scale * force[0], scale * force[1]]
    for _ in range(5):
        downs = [from_below(x) for x in field]
        ups = [from_above(x) for x in field]
        steps = [downs[k] - ups[k] for k in range(2)]
        field = [
            KEEP * field[k]
            + scale
            * gather_terms(
                right, left, cross_right, cross_left, under, over, field[k], downs[k], ups[k], steps[1 - k], force[k]
            )
            for k in range(2)
        ]
    coarsest = []
    for k in range(2):
        a, b = pltpu.roll(field[k][0:8], 2, axis=0), pltpu.roll(field[k][8:16], 2, axis=0)
        coarsest.append(jnp.where(sublanes(a) < 2, a, b))
    part = slice(2 * MERGED[3], 2 * MERGED[3] + MERGED[2])
    up, down = above(part), below(part)
    sub = sublanes(up)
    own_field, own_force = levels[2].field, levels[2].force
    for k in range(2):

        def turned(x, by):
            by = (by - 4 * k) % 8
            return pltpu.roll(x, by, axis=0) if by else x

        late_field[k, 1] = jnp.where(sub < 2, turned(up, 0), jnp.where(sub < 7, own_field[k, 1], turned(down, 7)))
        late_field[k, 2] = jnp.where(sub < 1, turned(up, 6), jnp.where(sub < 6, own_field[k, 2], turned(down, 5)))
        late_force[k, 0] = jnp.where(sub < 7, own_force[k, 0], turned(down, 4))
        late_force[k, 1] = jnp.where(sub < 1, turned(up, 5), own_force[k, 1])
    levels[2].force = late_force
    levels[2].field = late_field
    coarse = lambda k, p: coarsest[k]
    for level in (2, 1):
        levels[level].last_sweeps(coarse, fields[level], others[level])
        coarse = lambda k, p, result=fields[level]: result[k, p + 1]
    finest_up(refs[:12], coarse, packed, next_packed, natural, velocity, sems)


def swap(x, axis, odd):
    rows, cols = lax.axis_size("gy"), lax.axis_size("gx")
    count, across = (rows, cols) if axis == "gy" else (cols, rows)
    pairs = []
    for j in range(across):
        for i in range(odd, count - 1, 2):
            pairs += [((i, j), (i + 1, j)), ((i + 1, j), (i, j))]
        if odd:
            pairs += [((i, j), (i, j ^ 1)) for i in (0, count - 1)]
    place = (lambda i, j: j * rows + i) if axis == "gy" else (lambda i, j: i * rows + j)
    return lax.ppermute(x, ("gx", "gy"), [(place(*a), place(*b)) for a, b in pairs])


def swap_far(x, odd):
    count = lax.axis_size("gy")
    pairs = []
    for i in range(0, count - 2):
        if i // 2 % 2 == odd:
            pairs += [(i, i + 2), (i + 2, i)]
    if odd:
        pairs += [(i, i ^ 1) for i in (0, 1, count - 2, count - 1)]
    return lax.ppermute(x, "gy", pairs)


def local(forcing, ice_mask, viscosity_class, drag_class, viscosity_table, drag_table):
    inputs = [
        pltpu.with_memory_space_constraint(x, pltpu.HBM)
        for x in (viscosity_table, drag_table, forcing, ice_mask, viscosity_class, drag_class)
    ]
    hbm = [pl.BlockSpec(memory_space=pltpu.HBM)] * 6
    table = pltpu.SMEM((16,), jnp.float32)
    coef, side_even, side_odd, main_even, main_odd = pl.pallas_call(
        lookup_kernel,
        out_shape=(shape(2, ROWS, COLS),) + (shape(72, 128),) * 2 + (shape(4, HALO, COLS),) * 2,
        in_specs=hbm,
        out_specs=tuple(vmem(5)),
        scratch_shapes=[[table, table], pltpu.VMEM((3, ROWS, COLS), jnp.int32)]
        + [pltpu.VMEM((2, 2, ROWS, EDGE), jnp.float32), pltpu.SemaphoreType.DMA((9,))],
        compiler_params=params(),
        name="lookup",
    )(*inputs)
    got_odd = swap(side_odd, "gx", 1)
    got_even = swap(side_even, "gx", 0)
    rows_odd = swap(main_odd, "gy", 1)
    sides, send_even, send_odd = pl.pallas_call(
        corner_kernel,
        out_shape=(shape(2, 4, ROWS, EDGE),) + (shape(4, HALO, 2 * EDGE),) * 2,
        in_specs=vmem(2),
        out_specs=tuple(vmem(3)),
        compiler_params=params(),
        name="corners",
    )(got_odd, got_even)
    corner_odd = swap(send_odd, "gy", 1)
    corner_even = swap(send_even, "gy", 0)
    rows_even = swap(main_even, "gy", 0)

    def kept(widths):
        return [dims for level in range(3) for dims in Level.shapes(level, widths)]

    def scratch(dims):
        return [pltpu.VMEM(one, jnp.float32) for one in dims]

    def rims(widths):
        return [(2, PLANES[i] + 2, 8, widths[i]) for i in range(3)]

    def work(widths):
        return scratch([(32, 64, 128)] + [(PLANES[i], 8, widths[i]) for i in range(3)] * 3 + rims(widths))

    *main, top = pl.pallas_call(
        main_kernel,
        out_shape=tuple(shape(*dims) for dims in kept(MAIN) + [(4, 8, MAIN[3])]),
        in_specs=vmem(4),
        out_specs=tuple(vmem(25)),
        scratch_shapes=work(MAIN),
        compiler_params=params(),
        name="main",
    )(forcing, coef, rows_even, rows_odd)
    near_lanes = 2 * MERGED[3] + MERGED[2]
    *rim, send_even, send_odd, far = pl.pallas_call(
        rim_kernel,
        out_shape=tuple(shape(*dims) for dims in kept(RIM) + [(8, near_lanes)] * 2 + [(8, 2 * MERGED[3])]),
        in_specs=vmem(10),
        out_specs=tuple(vmem(27)),
        scratch_shapes=work(RIM),
        compiler_params=params(),
        name="rim",
    )(forcing, coef, sides, rows_even, rows_odd, corner_odd, corner_even, top, main[22], main[23])
    near_even = swap(send_even, "gy", 0)
    near_odd = swap(send_odd, "gy", 1)
    far_even = swap_far(far, 0)
    far_odd = swap_far(far, 1)
    wide = MERGED[0]
    finest = [(8, 8, wide)] * 5 + [(9, 8, wide)] + [(8, 8, wide)] * 2
    finest += [(5, 2, 8, wide), (4, 8, wide), (2, 2, 8, wide), (2, 4, 8, wide)]
    merged = pl.pallas_call(
        merge_kernel,
        out_shape=tuple(shape(*dims) for dims in finest + kept(MERGED)[8:]),
        in_specs=vmem(48),
        out_specs=tuple(vmem(28)),
        compiler_params=params(),
        name="merge",
    )(*main, *rim)
    late = [(8, 8, wide), (10, 8, wide), (2, 2, 8, MERGED[2]), (2, 4, 8, MERGED[2])]
    return pl.pallas_call(
        up_kernel,
        out_shape=shape(2, ROWS, COLS),
        in_specs=vmem(33),
        out_specs=pl.BlockSpec(memory_space=pltpu.HBM),
        scratch_shapes=scratch([(2, COLS // 128, ROWS, 128)])
        + [pltpu.SemaphoreType.DMA((2 * COLS // 128,))]
        + scratch(late + rims(MERGED)[1:] + rims(MERGED)[1:]),
        compiler_params=params(),
        name="up",
    )(far, near_even, near_odd, far_even, far_odd, *merged)


def solution(mesh):
    in_specs = (P(None, "gy", "gx"), P("gy", "gx"), P("gy", "gx"), P("gy", "gx"), P(), P())
    out_specs = P(None, "gy", "gx")
    return jax.shard_map(local, mesh=mesh, in_specs=in_specs, out_specs=out_specs, check_vma=False)
```

```python
import jax
import jax.numpy as jnp
from jax import lax
from jax.experimental import pallas as pl
from jax.experimental.pallas import tpu as pltpu
from jax.sharding import PartitionSpec as P

OMEGA = 0.6
KEEP = 1.0 - OMEGA
ROWS, COLS = 32, 1024
EDGE = 128
HALO = 16
PLANES = (8, 4, 2)
MAIN = (1024, 512, 256, 128)
RIM = (512, 256, 128, 128)
MERGED = (1152, 640, 384, 256)
VMEM_LIMIT = 16 * 1024 * 1024


def vmem(count):
    return [pl.BlockSpec(memory_space=pltpu.VMEM)] * count


def params():
    return pltpu.CompilerParams(vmem_limit_bytes=VMEM_LIMIT)


def shape(*dims):
    return jax.ShapeDtypeStruct(dims, jnp.float32)


def from_left(x):
    return pltpu.roll(x, 1, axis=1)


def from_right(x):
    return pltpu.roll(x, x.shape[1] - 1, axis=1)


def from_above(x):
    return pltpu.roll(x, 1, axis=0)


def from_below(x):
    return pltpu.roll(x, x.shape[0] - 1, axis=0)


def tiles(x):
    return [x[:, i : i + 128] for i in range(0, x.shape[1], 128)]


def lane(kind):
    return lax.broadcasted_iota(jnp.int32, (8, 128), kind)


def pick(x, index):
    return jnp.take_along_axis(x, index, axis=1, mode="promise_in_bounds")


def halve_lanes(x):
    at = lane(1)
    even = at % 2 == 0
    index = jnp.where(at < 64, 2 * at, 2 * at - 127)
    parts = tiles(x)
    if len(parts) % 2:
        parts.append(jnp.zeros_like(parts[0]))
    out = []
    for a, b in zip(parts[0::2], parts[1::2]):
        out.append(pick(jnp.where(even, a, b), index) + pick(jnp.where(even, b, a), index ^ 1))
    return jnp.concatenate(out, axis=1)


def double_lanes(x, lanes):
    at = lane(1)
    parts = tiles(x)
    count = lanes // 128 - 1
    out = [pick(parts[i // 2], at // 2 + 64 * (i % 2)) for i in range(count)]
    out.append(pick(parts[-1], jnp.where(at < 64, at // 2, at // 2 + 64)))
    return jnp.concatenate(out, axis=1)


def merge_tiles(level, main, rim):
    at = lane(1)
    if level == 0:
        low, left, right, high = rim
    else:
        low = left = pltpu.roll(rim[0], (64, 96, 112)[level - 1], axis=1)
        high = right = pltpu.roll(rim[-1], (64, 32, 80)[level - 1], axis=1)
    out = list(main)
    out[0] = jnp.where(at < 64 >> level, left, out[0])
    out[-1] = jnp.where(at < 128 - (64 >> level), out[-1], right)
    beside = jnp.where(at < 64, high, low)
    if level > 1:
        beside = jnp.where((at < EDGE >> level) | (at >= 128 - (EDGE >> level)), beside, 0.0)
    return out + [beside]


def merge(level, main, rim):
    return jnp.concatenate(merge_tiles(level, tiles(main), tiles(rim)), axis=1)


def coefficients(eta, beta, eta_below, face_above):
    ice = eta > 0.0
    eta_right = from_right(eta)
    right = jnp.where(ice & (eta_right > 0.0), 0.5 * (eta + eta_right), 0.0)
    left = from_left(right)
    below = jnp.where(ice & (eta_below > 0.0), 0.5 * (eta + eta_below), 0.0)
    above = face_above(below)
    base = beta + jnp.where(ice, 0.0, 1.0)
    diag = base + ((right + left) + (below + above))
    return right, left, below, above, 0.05 * eta_right, 0.05 * from_left(eta), diag


def gather_terms(right, left, cross_right, cross_left, below, above, here, under, over, other_step, force):
    from_west = from_left(right * here + cross_right * other_step)
    from_east = from_right(left * here - cross_left * other_step)
    return (force + (from_west + from_east)) + (below * under + above * over)


class Level:
    def __init__(self, planes, refs):
        self.planes = planes
        self.right, self.left, self.cross_right, self.cross_left, self.below, self.scale, self.force, self.field = refs

    @staticmethod
    def shapes(level, widths):
        planes, lanes = PLANES[level], widths[level]
        one = [(planes, 8, lanes)] * 4 + [(planes + 1, 8, lanes), (planes, 8, lanes)]
        return one + [(2, planes, 8, lanes), (2, planes + 2, 8, lanes)]

    def wrap(self, field):
        for k in range(2):
            field[k, 0] = from_above(field[k, self.planes])
            field[k, self.planes + 1] = from_below(field[k, 1])

    def terms(self, p, field):
        out = []
        steps = [field[k, p + 2] - field[k, p] for k in range(2)]
        for k in range(2):
            out.append(
                gather_terms(
                    self.right[p],
                    self.left[p],
                    self.cross_right[p],
                    self.cross_left[p],
                    self.below[p + 1],
                    self.below[p],
                    field[k, p + 1],
                    field[k, p + 2],
                    field[k, p],
                    steps[1 - k],
                    self.force[k, p],
                )
            )
        return out

    def sweep(self, source, target):
        for p in range(self.planes):
            terms = self.terms(p, source)
            for k in range(2):
                target[k, p + 1] = KEEP * source[k, p + 1] + self.scale[p] * terms[k]

    def setup(self, eta, beta, diag):
        planes = self.planes
        for p in range(planes):
            here = eta[p]
            ice = here > 0.0
            next_eta = eta[p + 1] if p + 1 < planes else from_below(eta[0])
            self.below[p + 1] = jnp.where(ice & (next_eta > 0.0), 0.5 * (here + next_eta), 0.0)
        self.below[0] = from_above(self.below[planes])
        for p in range(planes):
            here = eta[p]
            ice = here > 0.0
            eta_right = from_right(here)
            right = jnp.where(ice & (eta_right > 0.0), 0.5 * (here + eta_right), 0.0)
            left = from_left(right)
            base = beta[p] + jnp.where(ice, 0.0, 1.0)
            total = base + ((right + left) + (self.below[p + 1] + self.below[p]))
            self.right[p] = right
            self.left[p] = left
            self.cross_right[p] = 0.05 * eta_right
            self.cross_left[p] = 0.05 * from_left(here)
            diag[p] = total
            self.scale[p] = OMEGA / total

    def first_sweeps(self, other):
        for k in range(2):
            for p in range(self.planes):
                other[k, p + 1] = self.scale[p] * self.force[k, p]
        self.wrap(other)
        self.sweep(other, self.field)
        self.wrap(self.field)

    def restrict(self, diag, target):
        for p in range(0, self.planes, 2):
            rest = [0.0, 0.0]
            for q in (p, p + 1):
                terms = self.terms(q, self.field)
                for k in range(2):
                    rest[k] = rest[k] + (terms[k] - diag[q] * self.field[k, q + 1])
            for k in range(2):
                target(k, p // 2, halve_lanes(rest[k]))

    def last_sweeps(self, coarse, result, other):
        for k in range(2):
            for p in range(0, self.planes, 2):
                add = double_lanes(coarse(k, p // 2), self.field.shape[-1])
                result[k, p + 1] = self.field[k, p + 1] + add
                result[k, p + 2] = self.field[k, p + 2] + add
        self.wrap(result)
        self.sweep(result, other)
        self.wrap(other)
        self.sweep(other, result)


def halve_planes(source, target, planes, scale):
    for p in range(0, planes, 2):
        both = halve_lanes(source[p] + source[p + 1])
        target[p // 2] = scale * both if scale != 1.0 else both


def look_up(tables, classes, ice):
    at = lane(1)
    rows = []
    for table in tables:
        row = jnp.zeros((8, 128), jnp.float32)
        for i in range(16):
            row = jnp.where(at == i, table[i], row)
        rows.append(row)
    return [pick(row, part) * ice for row, part in zip(rows, classes)]


def start_all(pairs, sems):
    copies = [pltpu.make_async_copy(a, b, sems.at[i]) for i, (a, b) in enumerate(pairs)]
    for copy in copies:
        copy.start()
    return copies


def halves_of(axis, size, part):
    even = lax.axis_index(axis) % 2 == 0
    first = pl.multiple_of(jnp.where(even, size - part, 0), part)
    return first, pl.multiple_of(size - part - first, part)


def group(index):
    return (lane(1) >= 8 * index) & (lane(1) < 8 * index + 8)


def pack_side(parts, side):
    near = lane(1) < 64
    out = []
    for pair in (0, 2):
        for r in range(4):
            x, y = parts[pair][r], parts[pair + 1][r]
            x, y = (x, pltpu.roll(y, 64, axis=1)) if side == 0 else (pltpu.roll(x, 64, axis=1), y)
            out.append(jnp.where(near, x, y))
    rest = jnp.zeros_like(out[0])
    for i in range(16):
        start = 64 if side == 0 else 56
        rest = jnp.where(group(i), pltpu.roll(parts[i // 4][i % 4], (8 * i - start) % 128, axis=1), rest)
    return out + [rest]


def unpack_side(tile, side):
    out = []
    near = lane(1) < 64 if side == 0 else lane(1) >= 64
    start = 64 if side == 0 else 56
    for row in range(4):
        for r in range(4):
            x = tile[4 * (row // 2) + r]
            if row % 2 == (0 if side else 1):
                x = pltpu.roll(x, 64, axis=1)
            rest = pltpu.roll(tile[8], (start - 8 * (4 * row + r)) % 128, axis=1)
            out.append(jnp.where(near, x, jnp.where(group(start // 8), rest, 0.0)))
    return out


def lookup_kernel(v_table, d_table, forcing, mask, v_class, d_class, coef, *refs):
    sides, rows = refs[0:2], refs[2:4]
    tables, ints, edges, sems = refs[4:]
    pairs = [(v_table, tables[0]), (d_table, tables[1])]
    pairs += [(source, ints.at[i]) for i, source in enumerate((mask, v_class, d_class))]
    row_starts = halves_of("gy", ROWS, HALO)
    for i, start in enumerate((0, COLS - EDGE)):
        pairs.append((forcing.at[:, :, pl.ds(start, EDGE)], edges.at[i]))
    for start, target in zip(row_starts, rows):
        pairs.append((forcing.at[:, pl.ds(start, HALO), :], target.at[0:2]))
    copies = start_all(pairs, sems)
    for copy in copies[:5]:
        copy.wait()
    for r in range(0, ROWS, 8):
        for c in range(0, COLS, 128):
            part = (slice(r, r + 8), slice(c, c + 128))
            ice = ints[(0,) + part].astype(jnp.float32)
            found = look_up(tables, [ints[(1,) + part], ints[(2,) + part]], ice)
            for k in range(2):
                coef[(k,) + part] = found[k]
    for copy in copies[5:7]:
        copy.wait()
    even = lax.axis_index("gx") % 2 == 0
    messages = []
    for side, start in enumerate((0, COLS - EDGE)):
        parts = [[edges[side, k, 8 * r : 8 * r + 8] for r in range(4)] for k in range(2)]
        parts += [[coef[k, 8 * r : 8 * r + 8, start : start + EDGE] for r in range(4)] for k in range(2)]
        messages.append(pack_side(parts, side))
    for i in range(9):
        low, high = messages[0][i], messages[1][i]
        sides[0][8 * i : 8 * i + 8] = jnp.where(even, high, low)
        sides[1][8 * i : 8 * i + 8] = jnp.where(even, low, high)
    for k in range(2):
        for start, target in zip(row_starts, rows):
            target[2 + k] = coef[k, pl.ds(start, HALO), :]
    for copy in copies[7:]:
        copy.wait()


def corner_kernel(got_odd, got_even, sides, send_even, send_odd):
    gx = lax.axis_index("gx")
    even = gx % 2 == 0
    for side in range(2):
        end = gx == (0 if side == 0 else lax.axis_size("gx") - 1)

        def tile(i):
            rows = slice(8 * i, 8 * i + 8)
            a, b = got_even[rows], got_odd[rows]
            return jnp.where(end, 0.0, jnp.where(even, b, a) if side == 0 else jnp.where(even, a, b))

        parts = unpack_side([tile(i) for i in range(9)], 1 - side)
        for i, part in enumerate(parts):
            sides[side, i // 4, 8 * (i % 4) : 8 * (i % 4) + 8] = part
    for start, target in zip(halves_of("gy", ROWS, HALO), (send_even, send_odd)):
        for row in range(4):
            for side in range(2):
                target[row, :, side * EDGE : (side + 1) * EDGE] = sides[side, row, pl.ds(start, HALO)]


def own_rows(a, b):
    upper = lax.broadcasted_iota(jnp.int32, a.shape, 0) < 4
    return jnp.where(upper, pltpu.roll(a, 6, axis=0), pltpu.roll(b, 2, axis=0))


def levels_of(refs):
    return [Level(PLANES[i], refs[8 * i : 8 * i + 8]) for i in range(3)]


def spread(above, own, below, natural, targets, cols):
    gy = lax.axis_index("gy")
    even = gy % 2 == 0
    (above_even, above_odd), (below_even, below_odd) = above, below
    natural[0:HALO] = jnp.where(gy == 0, 0.0, jnp.where(even, above_odd, above_even))
    natural[HALO : HALO + ROWS] = own
    natural[HALO + ROWS :] = jnp.where(gy == lax.axis_size("gy") - 1, 0.0, jnp.where(even, below_even, below_odd))
    for p in range(8):
        targets(p, cols, natural[pl.ds(p, 8, stride=8), :])


def descend(levels, etas, betas, diags, others):
    for level in range(3):
        here = levels[level]
        here.setup(etas[level], betas[level], diags[level])
        here.first_sweeps(others[level])
        if level < 2:
            halve_planes(etas[level], etas[level + 1], here.planes, 0.5)
            halve_planes(betas[level], betas[level + 1], here.planes, 1.0)

            def store(k, p, value, target=levels[level + 1].force):
                target[k, p] = value

            here.restrict(diags[level], store)
    found = [None, None]

    def keep(k, p, value):
        found[k] = value

    levels[2].restrict(diags[2], keep)
    eta = 0.5 * halve_lanes(etas[2][0] + etas[2][1])
    beta = halve_lanes(betas[2][0] + betas[2][1])
    return found + [eta, beta]


def plane_targets(row, levels, etas, betas):
    def target(p, cols, plane):
        if row < 2:
            levels[0].force[row, p, :, cols] = plane
        else:
            (etas, betas)[row - 2][0][p, :, cols] = plane

    return target


def main_kernel(forcing, coef, rows_even, rows_odd, *refs):
    levels = levels_of(refs)
    top, natural = refs[24:26]
    etas, betas, diags, others = (refs[26 + 3 * i : 29 + 3 * i] for i in range(4))
    for row in range(4):
        source = forcing if row < 2 else coef
        target = plane_targets(row, levels, etas, betas)
        for i in range(COLS // 128):
            cols = slice(128 * i, 128 * i + 128)
            halo = (rows_even[row, :, cols], rows_odd[row, :, cols])
            spread(halo, source[row % 2, :, cols], halo, natural.at[8 * row + i], target, cols)
    for i, value in enumerate(descend(levels, etas, betas, diags, others)):
        top[i] = value


def rim_kernel(
    forcing,
    coef,
    sides,
    rows_even,
    rows_odd,
    corner_odd,
    corner_even,
    top,
    late_force,
    late_field,
    *refs,
):
    levels = levels_of(refs)
    near_even, near_odd, far, natural = refs[24:28]
    etas, betas, diags, others = (refs[28 + 3 * i : 31 + 3 * i] for i in range(4))
    for row in range(4):
        source = forcing if row < 2 else coef
        target = plane_targets(row, levels, etas, betas)
        for i in range(4):
            if i in (0, 3):
                part = slice(0, EDGE) if i == 0 else slice(EDGE, 2 * EDGE)
                halo = (corner_even[row, :, part], corner_odd[row, :, part])
                own = sides[i // 3, row]
            else:
                part = slice(0, EDGE) if i == 1 else slice(COLS - EDGE, COLS)
                halo = (rows_even[row, :, part], rows_odd[row, :, part])
                own = source[row % 2, :, part]
            spread(halo, own, halo, natural.at[4 * row + i], target, slice(128 * i, 128 * i + 128))
    rim = descend(levels, etas, betas, diags, others)
    both = [merge(3, top[i], rim[i]) for i in range(4)]
    head = jnp.concatenate([own_rows(both[0], both[1]), own_rows(both[2], both[3])], axis=1)
    far[...] = head
    at = head.shape[1]
    w, f = (
        [[merge(2, source[k, p + i], rims[k, p + i]) for p in range(2)] for k in range(2)]
        for i, source, rims in ((1, late_field, levels[2].field), (0, late_force, levels[2].force))
    )
    messages = []
    for picks in (
        lambda k: [(w[k][0], 4), (w[k][0], 5), (w[k][1], 4), (f[k][1], 4)],
        lambda k: [(w[k][0], 3), (w[k][1], 2), (w[k][1], 3), (f[k][0], 3)],
    ):
        rows = picks(0) + picks(1)
        message = pltpu.roll(rows[0][0], 8 - rows[0][1], axis=0)
        sub = lax.broadcasted_iota(jnp.int32, message.shape, 0)
        for i, (x, g) in enumerate(rows):
            if i:
                message = jnp.where(sub == i, pltpu.roll(x, (i - g) % 8, axis=0) if i != g else x, message)
        messages.append(message)
    even = lax.axis_index("gy") % 2 == 0
    for target, flag in ((near_even, even), (near_odd, jnp.logical_not(even))):
        target[:, 0:at] = head
        target[:, at:] = jnp.where(flag, messages[0], messages[1])


def merge_kernel(*refs):
    late = refs[48:]
    mains, rims = levels_of(refs[:24]), levels_of(refs[24:48])

    def joined(name, *index):
        return merge(0, getattr(mains[0], name)[index], getattr(rims[0], name)[index])

    names = ("right", "left", "cross_right", "cross_left", "scale")
    for i, name in enumerate(names):
        for p in range(8):
            value = joined(name, p)
            late[i][p] = own_rows(value, value)
            if p in (0, 7):
                late[8][i, p // 7] = value
    for p in range(9):
        value = joined("below", p)
        late[5][p] = own_rows(value, value)
        if p in (0, 1, 7, 8):
            late[9][(0, 1, 7, 8).index(p)] = value
    for p in range(8):
        force = [joined("force", k, p) for k in range(2)]
        field = [joined("field", k, p + 1) for k in range(2)]
        late[6][p] = own_rows(force[0], force[1])
        late[7][p] = own_rows(field[0], field[1])
        for k in range(2):
            if p in (0, 7):
                late[10][k, p // 7] = force[k]
            if p in (0, 1, 6, 7):
                late[11][k, (0, 1, 6, 7).index(p)] = field[k]
    for level in (1, 2):
        for i in range(8):
            main, rim = (refs[24 * j + 8 * level + i] for j in range(2))
            target = late[4 + 8 * level + i]
            planes = PLANES[level]
            if i < 6:
                for p in range(main.shape[0]):
                    target[p] = merge(level, main[p], rim[p])
            else:
                for k in range(2):
                    for p in range(i - 6, planes + i - 6):
                        target[k, p] = merge(level, main[k, p], rim[k, p])


def finest_up(refs, coarse, packed, next_packed, natural, velocity, sems):
    right, left, cross_right, cross_left, scale, below, force, field = refs[:8]
    edge_coef, edge_below, edge_force, edge_field = refs[8:]
    wide = MERGED[0]
    edges = [[None] * 8, [None] * 8]
    for p in range(0, 8, 2):
        below_this = [coarse(k, p // 2) for k in range(2)]
        both = double_lanes(own_rows(below_this[0], below_this[1]), wide)
        adds = [double_lanes(x, wide) if p in (0, 6) else None for x in below_this]
        for q in (p, p + 1):
            packed[q] = field[q] + both
            if q in (0, 1, 6, 7):
                for k in range(2):
                    edges[k][q] = edge_field[k, (0, 1, 6, 7).index(q)] + adds[k]
    found = {}
    for i, p in enumerate((0, 7)):
        under = [edges[k][1] if p == 0 else from_below(edges[k][0]) for k in range(2)]
        over = [from_above(edges[k][7]) if p == 0 else edges[k][6] for k in range(2)]
        for k in range(2):
            terms = gather_terms(
                edge_coef[0, i],
                edge_coef[1, i],
                edge_coef[2, i],
                edge_coef[3, i],
                edge_below[2 * i + 1],
                edge_below[2 * i],
                edges[k][p],
                under[k],
                over[k],
                under[1 - k] - over[1 - k],
                edge_force[k, i],
            )
            found[k, p] = KEEP * edges[k][p] + edge_coef[4, i] * terms
    next_packed[1] = own_rows(found[0, 0], found[1, 0])
    next_packed[8] = own_rows(found[0, 7], found[1, 7])
    next_packed[0] = own_rows(from_above(found[0, 7]), from_above(found[1, 7]))
    next_packed[9] = own_rows(from_below(found[0, 0]), from_below(found[1, 0]))

    def sweep(p, above, here, under, first, count, part):
        mid = slice(128, 128 + 128 * count)
        low, high = slice(0, 128 + 128 * count), slice(128, 256 + 128 * count)
        over, w, down = part(above), part(here), part(under)
        step = pltpu.roll(down - over, 4, axis=0)
        west = from_left((part(right[p]) * w + part(cross_right[p]) * step)[:, low])[:, 128:]
        east = from_right((part(left[p]) * w - part(cross_left[p]) * step)[:, high])[:, : 128 * count]
        cols = slice(128 * first, 128 * (first + count))
        terms = (force[p][:, cols] + (west + east)) + (below[p + 1][:, cols] * down[:, mid] + below[p][:, cols] * over[:, mid])
        return KEEP * w[:, mid] + scale[p][:, cols] * terms

    for p in range(1, 7):
        over, here, under = packed[p - 1], packed[p], packed[p + 1]
        terms = gather_terms(
            right[p],
            left[p],
            cross_right[p],
            cross_left[p],
            below[p + 1],
            below[p],
            here,
            under,
            over,
            pltpu.roll(under - over, 4, axis=0),
            force[p],
        )
        next_packed[p + 1] = KEEP * here + scale[p] * terms
    copies = []
    first = 0
    for count in (4, 3, 1):

        def part(x):
            end = x[:, 128 * max(first - 1, 0) : 128 * (first + count + 1)]
            return end if first else jnp.concatenate([x[:, wide - 128 :], end], axis=1)

        for p in range(8):
            done = sweep(p, next_packed[p], next_packed[p + 1], next_packed[p + 2], first, count, part)
            for i in range(count):
                tile = done[:, 128 * i : 128 * i + 128]
                for k in range(2):
                    natural[k, first + i, pl.ds(p, 4, stride=8), :] = tile[4 * k : 4 * k + 4]
        for i in range(first, first + count):
            for k in range(2):
                target = velocity.at[k, :, pl.ds(128 * i, 128)]
                copy = pltpu.make_async_copy(natural.at[k, i], target, sems.at[2 * i + k])
                copy.start()
                copies.append(copy)
        first += count
    for copy in copies:
        copy.wait()


def up_kernel(far, near_even, near_odd, far_even, far_odd, *refs):
    levels = [None] + [Level(PLANES[i], refs[4 + 8 * i : 12 + 8 * i]) for i in (1, 2)]
    velocity, natural, sems, packed, next_packed, late_force, late_field = refs[28:35]
    fields, others = (None,) + refs[35:37], (None,) + refs[37:39]
    gy = lax.axis_index("gy")
    count = lax.axis_size("gy")
    even = gy % 2 == 0

    def above(part):
        return jnp.where(gy == 0, 0.0, jnp.where(even, near_odd[:, part], near_even[:, part]))

    def below(part):
        return jnp.where(gy == count - 1, 0.0, jnp.where(even, near_even[:, part], near_odd[:, part]))

    def sublanes(like):
        return lax.broadcasted_iota(jnp.int32, like.shape, 0)

    def stacked(part):
        low = gy // 2 % 2 == 0
        m2 = jnp.where(gy < 2, 0.0, jnp.where(low, far_odd[:, part], far_even[:, part]))
        p2 = jnp.where(gy > count - 3, 0.0, jnp.where(low, far_even[:, part], far_odd[:, part]))
        m1, p1, own = above(part), below(part), far[:, part]
        sub = sublanes(own)
        out = []
        for outer, inner in ((6, 2), (2, 6)):

            def tile(x, y, z):
                x, z = pltpu.roll(x, outer, axis=0), pltpu.roll(z, outer, axis=0)
                return jnp.where(sub < 2, x, jnp.where(sub < 6, pltpu.roll(y, inner, axis=0), z))

            if outer == 6:
                ends = jnp.where(sub < 4, m2, pltpu.roll(p2, 4, axis=0))
            else:
                ends = jnp.where(sub < 4, pltpu.roll(m2, 4, axis=0), p2)
            out.append((jnp.concatenate([tile(m2, m1, own), tile(own, p1, p2)], axis=0), ends))
        return out

    force = stacked(slice(0, MERGED[3]))
    (eta, eta_ends), (beta, beta_ends) = stacked(slice(MERGED[3], 2 * MERGED[3]))
    row = sublanes(eta)

    def shifted_down(x, ends):
        first = pltpu.roll(ends, 7, axis=0)
        return jnp.where(row == 0, jnp.concatenate([first, first], axis=0), from_above(x))

    def shifted_up(x, ends):
        last = pltpu.roll(ends, 1, axis=0)
        return jnp.where(row == 15, jnp.concatenate([last, last], axis=0), from_below(x))

    ends = coefficients(eta_ends, beta_ends, from_below(eta_ends), from_above)
    right, left, under, over, cross_right, cross_left, diag = coefficients(
        eta, beta, shifted_up(eta, eta_ends), lambda x: shifted_down(x, ends[2])
    )
    scale = OMEGA / diag
    scale_ends = OMEGA / ends[6]
    field = [scale * force[k][0] for k in range(2)]
    for step in range(5):
        if step == 0:
            field_ends = [scale_ends * force[k][1] for k in range(2)]
            downs = [shifted_up(field[k], field_ends[k]) for k in range(2)]
            ups = [shifted_down(field[k], field_ends[k]) for k in range(2)]
        else:
            downs = [from_below(x) for x in field]
            ups = [from_above(x) for x in field]
        steps = [downs[k] - ups[k] for k in range(2)]
        field = [
            KEEP * field[k]
            + scale
            * gather_terms(
                right, left, cross_right, cross_left, under, over, field[k], downs[k], ups[k], steps[1 - k], force[k][0]
            )
            for k in range(2)
        ]
    coarsest = []
    for k in range(2):
        a, b = pltpu.roll(field[k][0:8], 4, axis=0), pltpu.roll(field[k][8:16], 4, axis=0)
        coarsest.append(jnp.where(sublanes(a) < 4, a, b))
    part = slice(2 * MERGED[3], 2 * MERGED[3] + MERGED[2])
    up, down = above(part), below(part)
    sub = sublanes(up)
    own_field, own_force = levels[2].field, levels[2].force
    for k in range(2):

        def turned(x, by):
            by = (by - 4 * k) % 8
            return pltpu.roll(x, by, axis=0) if by else x

        late_field[k, 1] = jnp.where(sub < 2, turned(up, 0), jnp.where(sub < 7, own_field[k, 1], turned(down, 7)))
        late_field[k, 2] = jnp.where(sub < 1, turned(up, 6), jnp.where(sub < 6, own_field[k, 2], turned(down, 5)))
        late_force[k, 0] = jnp.where(sub < 7, own_force[k, 0], turned(down, 4))
        late_force[k, 1] = jnp.where(sub < 1, turned(up, 5), own_force[k, 1])
    levels[2].force = late_force
    levels[2].field = late_field
    coarse = lambda k, p: coarsest[k]
    for level in (2, 1):
        levels[level].last_sweeps(coarse, fields[level], others[level])
        coarse = lambda k, p, result=fields[level]: result[k, p + 1]
    finest_up(refs[:12], coarse, packed, next_packed, natural, velocity, sems)


def swap(x, axis, odd):
    rows, cols = lax.axis_size("gy"), lax.axis_size("gx")
    count, across = (rows, cols) if axis == "gy" else (cols, rows)
    pairs = []
    for j in range(across):
        for i in range(odd, count - 1, 2):
            pairs += [((i, j), (i + 1, j)), ((i + 1, j), (i, j))]
        if odd:
            pairs += [((i, j), (i, j ^ 1)) for i in (0, count - 1)]
    place = (lambda i, j: j * rows + i) if axis == "gy" else (lambda i, j: i * rows + j)
    return lax.ppermute(x, ("gx", "gy"), [(place(*a), place(*b)) for a, b in pairs])


def swap_far(x, odd):
    count = lax.axis_size("gy")
    pairs = []
    for i in range(0, count - 2):
        if i // 2 % 2 == odd:
            pairs += [(i, i + 2), (i + 2, i)]
    if odd:
        pairs += [(i, i ^ 1) for i in (0, 1, count - 2, count - 1)]
    return lax.ppermute(x, "gy", pairs)


def local(forcing, ice_mask, viscosity_class, drag_class, viscosity_table, drag_table):
    inputs = [
        pltpu.with_memory_space_constraint(x, pltpu.HBM)
        for x in (viscosity_table, drag_table, forcing, ice_mask, viscosity_class, drag_class)
    ]
    hbm = [pl.BlockSpec(memory_space=pltpu.HBM)] * 6
    table = pltpu.SMEM((16,), jnp.float32)
    coef, side_even, side_odd, main_even, main_odd = pl.pallas_call(
        lookup_kernel,
        out_shape=(shape(2, ROWS, COLS),) + (shape(72, 128),) * 2 + (shape(4, HALO, COLS),) * 2,
        in_specs=hbm,
        out_specs=tuple(vmem(5)),
        scratch_shapes=[[table, table], pltpu.VMEM((3, ROWS, COLS), jnp.int32)]
        + [pltpu.VMEM((2, 2, ROWS, EDGE), jnp.float32), pltpu.SemaphoreType.DMA((9,))],
        compiler_params=params(),
        name="lookup",
    )(*inputs)
    got_odd = swap(side_odd, "gx", 1)
    got_even = swap(side_even, "gx", 0)
    rows_odd = swap(main_odd, "gy", 1)
    sides, send_even, send_odd = pl.pallas_call(
        corner_kernel,
        out_shape=(shape(2, 4, ROWS, EDGE),) + (shape(4, HALO, 2 * EDGE),) * 2,
        in_specs=vmem(2),
        out_specs=tuple(vmem(3)),
        compiler_params=params(),
        name="corners",
    )(got_odd, got_even)
    corner_odd = swap(send_odd, "gy", 1)
    corner_even = swap(send_even, "gy", 0)
    rows_even = swap(main_even, "gy", 0)

    def kept(widths):
        return [dims for level in range(3) for dims in Level.shapes(level, widths)]

    def scratch(dims):
        return [pltpu.VMEM(one, jnp.float32) for one in dims]

    def rims(widths):
        return [(2, PLANES[i] + 2, 8, widths[i]) for i in range(3)]

    def work(widths):
        return scratch([(32, 64, 128)] + [(PLANES[i], 8, widths[i]) for i in range(3)] * 3 + rims(widths))

    *main, top = pl.pallas_call(
        main_kernel,
        out_shape=tuple(shape(*dims) for dims in kept(MAIN) + [(4, 8, MAIN[3])]),
        in_specs=vmem(4),
        out_specs=tuple(vmem(25)),
        scratch_shapes=work(MAIN),
        compiler_params=params(),
        name="main",
    )(forcing, coef, rows_even, rows_odd)
    near_lanes = 2 * MERGED[3] + MERGED[2]
    *rim, send_even, send_odd, far = pl.pallas_call(
        rim_kernel,
        out_shape=tuple(shape(*dims) for dims in kept(RIM) + [(8, near_lanes)] * 2 + [(8, 2 * MERGED[3])]),
        in_specs=vmem(10),
        out_specs=tuple(vmem(27)),
        scratch_shapes=work(RIM),
        compiler_params=params(),
        name="rim",
    )(forcing, coef, sides, rows_even, rows_odd, corner_odd, corner_even, top, main[22], main[23])
    near_even = swap(send_even, "gy", 0)
    near_odd = swap(send_odd, "gy", 1)
    far_even = swap_far(far, 0)
    far_odd = swap_far(far, 1)
    wide = MERGED[0]
    finest = [(8, 8, wide)] * 5 + [(9, 8, wide)] + [(8, 8, wide)] * 2
    finest += [(5, 2, 8, wide), (4, 8, wide), (2, 2, 8, wide), (2, 4, 8, wide)]
    merged = pl.pallas_call(
        merge_kernel,
        out_shape=tuple(shape(*dims) for dims in finest + kept(MERGED)[8:]),
        in_specs=vmem(48),
        out_specs=tuple(vmem(28)),
        compiler_params=params(),
        name="merge",
    )(*main, *rim)
    late = [(8, 8, wide), (10, 8, wide), (2, 2, 8, MERGED[2]), (2, 4, 8, MERGED[2])]
    return pl.pallas_call(
        up_kernel,
        out_shape=shape(2, ROWS, COLS),
        in_specs=vmem(33),
        out_specs=pl.BlockSpec(memory_space=pltpu.HBM),
        scratch_shapes=scratch([(2, COLS // 128, ROWS, 128)])
        + [pltpu.SemaphoreType.DMA((2 * COLS // 128,))]
        + scratch(late + rims(MERGED)[1:] + rims(MERGED)[1:]),
        compiler_params=params(),
        name="up",
    )(far, near_even, near_odd, far_even, far_odd, *merged)


def solution(mesh):
    in_specs = (P(None, "gy", "gx"), P("gy", "gx"), P("gy", "gx"), P("gy", "gx"), P(), P())
    out_specs = P(None, "gy", "gx")
    return jax.shard_map(local, mesh=mesh, in_specs=in_specs, out_specs=out_specs, check_vma=False)
```

```python
import jax
import jax.numpy as jnp
from jax import lax
from jax.experimental import pallas as pl
from jax.experimental.pallas import tpu as pltpu
from jax.sharding import PartitionSpec as P

OMEGA = 0.6
KEEP = 1.0 - OMEGA
ROWS, COLS = 32, 1024
EDGE = 128
HALO = 16
PLANES = (8, 4, 2)
MAIN = (1024, 512, 256, 128)
RIM = (512, 256, 128, 128)
MERGED = (1152, 640, 384, 256)
VMEM_LIMIT = 16 * 1024 * 1024


def vmem(count):
    return [pl.BlockSpec(memory_space=pltpu.VMEM)] * count


def params():
    return pltpu.CompilerParams(vmem_limit_bytes=VMEM_LIMIT)


def shape(*dims):
    return jax.ShapeDtypeStruct(dims, jnp.float32)


def from_left(x):
    return pltpu.roll(x, 1, axis=1)


def from_right(x):
    return pltpu.roll(x, x.shape[1] - 1, axis=1)


def from_above(x):
    return pltpu.roll(x, 1, axis=0)


def from_below(x):
    return pltpu.roll(x, x.shape[0] - 1, axis=0)


def tiles(x):
    return [x[:, i : i + 128] for i in range(0, x.shape[1], 128)]


def lane(kind):
    return lax.broadcasted_iota(jnp.int32, (8, 128), kind)


def pick(x, index):
    return jnp.take_along_axis(x, index, axis=1, mode="promise_in_bounds")


def halve_lanes(x):
    at = lane(1)
    even = at % 2 == 0
    index = jnp.where(at < 64, 2 * at, 2 * at - 127)
    parts = tiles(x)
    if len(parts) % 2:
        parts.append(jnp.zeros_like(parts[0]))
    out = []
    for a, b in zip(parts[0::2], parts[1::2]):
        out.append(pick(jnp.where(even, a, b), index) + pick(jnp.where(even, b, a), index ^ 1))
    return jnp.concatenate(out, axis=1)


def double_lanes(x, lanes):
    at = lane(1)
    parts = tiles(x)
    count = lanes // 128 - 1
    out = [pick(parts[i // 2], at // 2 + 64 * (i % 2)) for i in range(count)]
    out.append(pick(parts[-1], jnp.where(at < 64, at // 2, at // 2 + 64)))
    return jnp.concatenate(out, axis=1)


def merge_tiles(level, main, rim):
    at = lane(1)
    if level == 0:
        low, left, right, high = rim
    else:
        low = left = pltpu.roll(rim[0], (64, 96, 112)[level - 1], axis=1)
        high = right = pltpu.roll(rim[-1], (64, 32, 80)[level - 1], axis=1)
    out = list(main)
    out[0] = jnp.where(at < 64 >> level, left, out[0])
    out[-1] = jnp.where(at < 128 - (64 >> level), out[-1], right)
    beside = jnp.where(at < 64, high, low)
    if level > 1:
        beside = jnp.where((at < EDGE >> level) | (at >= 128 - (EDGE >> level)), beside, 0.0)
    return out + [beside]


def merge(level, main, rim):
    return jnp.concatenate(merge_tiles(level, tiles(main), tiles(rim)), axis=1)


def coefficients(eta, beta, eta_below, face_above):
    ice = eta > 0.0
    eta_right = from_right(eta)
    right = jnp.where(ice & (eta_right > 0.0), 0.5 * (eta + eta_right), 0.0)
    left = from_left(right)
    below = jnp.where(ice & (eta_below > 0.0), 0.5 * (eta + eta_below), 0.0)
    above = face_above(below)
    base = beta + jnp.where(ice, 0.0, 1.0)
    diag = base + ((right + left) + (below + above))
    return right, left, below, above, 0.05 * eta_right, 0.05 * from_left(eta), diag


def gather_terms(right, left, cross_right, cross_left, below, above, here, under, over, other_step, force):
    from_west = from_left(right * here + cross_right * other_step)
    from_east = from_right(left * here - cross_left * other_step)
    return (force + (from_west + from_east)) + (below * under + above * over)


class Level:
    def __init__(self, planes, refs):
        self.planes = planes
        self.right, self.left, self.cross_right, self.cross_left, self.below, self.scale, self.force, self.field = refs

    @staticmethod
    def shapes(level, widths):
        planes, lanes = PLANES[level], widths[level]
        one = [(planes, 8, lanes)] * 4 + [(planes + 1, 8, lanes), (planes, 8, lanes)]
        return one + [(2, planes, 8, lanes), (2, planes + 2, 8, lanes)]

    def wrap(self, field):
        for k in range(2):
            field[k, 0] = from_above(field[k, self.planes])
            field[k, self.planes + 1] = from_below(field[k, 1])

    def terms(self, p, field):
        out = []
        steps = [field[k, p + 2] - field[k, p] for k in range(2)]
        for k in range(2):
            out.append(
                gather_terms(
                    self.right[p],
                    self.left[p],
                    self.cross_right[p],
                    self.cross_left[p],
                    self.below[p + 1],
                    self.below[p],
                    field[k, p + 1],
                    field[k, p + 2],
                    field[k, p],
                    steps[1 - k],
                    self.force[k, p],
                )
            )
        return out

    def sweep(self, source, target):
        for p in range(self.planes):
            terms = self.terms(p, source)
            for k in range(2):
                target[k, p + 1] = KEEP * source[k, p + 1] + self.scale[p] * terms[k]

    def setup(self, eta, beta, diag):
        planes = self.planes
        for p in range(planes):
            here = eta[p]
            ice = here > 0.0
            next_eta = eta[p + 1] if p + 1 < planes else from_below(eta[0])
            self.below[p + 1] = jnp.where(ice & (next_eta > 0.0), 0.5 * (here + next_eta), 0.0)
        self.below[0] = from_above(self.below[planes])
        for p in range(planes):
            here = eta[p]
            ice = here > 0.0
            eta_right = from_right(here)
            right = jnp.where(ice & (eta_right > 0.0), 0.5 * (here + eta_right), 0.0)
            left = from_left(right)
            base = beta[p] + jnp.where(ice, 0.0, 1.0)
            total = base + ((right + left) + (self.below[p + 1] + self.below[p]))
            self.right[p] = right
            self.left[p] = left
            self.cross_right[p] = 0.05 * eta_right
            self.cross_left[p] = 0.05 * from_left(here)
            diag[p] = total
            self.scale[p] = OMEGA / total

    def first_sweeps(self, other):
        for k in range(2):
            for p in range(self.planes):
                other[k, p + 1] = self.scale[p] * self.force[k, p]
        self.wrap(other)
        self.sweep(other, self.field)
        self.wrap(self.field)

    def restrict(self, diag, target):
        for p in range(0, self.planes, 2):
            rest = [0.0, 0.0]
            for q in (p, p + 1):
                terms = self.terms(q, self.field)
                for k in range(2):
                    rest[k] = rest[k] + (terms[k] - diag[q] * self.field[k, q + 1])
            for k in range(2):
                target(k, p // 2, halve_lanes(rest[k]))

    def last_sweeps(self, coarse, result, other):
        for k in range(2):
            for p in range(0, self.planes, 2):
                add = double_lanes(coarse(k, p // 2), self.field.shape[-1])
                result[k, p + 1] = self.field[k, p + 1] + add
                result[k, p + 2] = self.field[k, p + 2] + add
        self.wrap(result)
        self.sweep(result, other)
        self.wrap(other)
        self.sweep(other, result)


def halve_planes(source, target, planes, scale):
    for p in range(0, planes, 2):
        both = halve_lanes(source[p] + source[p + 1])
        target[p // 2] = scale * both if scale != 1.0 else both


def look_up(tables, classes, ice):
    at = lane(1)
    rows = []
    for table in tables:
        row = jnp.zeros((8, 128), jnp.float32)
        for i in range(16):
            row = jnp.where(at == i, table[i], row)
        rows.append(row)
    return [pick(row, part) * ice for row, part in zip(rows, classes)]


def start_all(pairs, sems):
    copies = [pltpu.make_async_copy(a, b, sems.at[i]) for i, (a, b) in enumerate(pairs)]
    for copy in copies:
        copy.start()
    return copies


def halves_of(axis, size, part):
    even = lax.axis_index(axis) % 2 == 0
    first = pl.multiple_of(jnp.where(even, size - part, 0), part)
    return first, pl.multiple_of(size - part - first, part)


def group(index):
    return (lane(1) >= 8 * index) & (lane(1) < 8 * index + 8)


def pack_side(parts, side):
    near = lane(1) < 64
    out = []
    for pair in (0, 2):
        for r in range(4):
            x, y = parts[pair][r], parts[pair + 1][r]
            x, y = (x, pltpu.roll(y, 64, axis=1)) if side == 0 else (pltpu.roll(x, 64, axis=1), y)
            out.append(jnp.where(near, x, y))
    rest = jnp.zeros_like(out[0])
    for i in range(16):
        start = 64 if side == 0 else 56
        rest = jnp.where(group(i), pltpu.roll(parts[i // 4][i % 4], (8 * i - start) % 128, axis=1), rest)
    return out + [rest]


def unpack_side(tile, side):
    out = []
    near = lane(1) < 64 if side == 0 else lane(1) >= 64
    start = 64 if side == 0 else 56
    for row in range(4):
        for r in range(4):
            x = tile[4 * (row // 2) + r]
            if row % 2 == (0 if side else 1):
                x = pltpu.roll(x, 64, axis=1)
            rest = pltpu.roll(tile[8], (start - 8 * (4 * row + r)) % 128, axis=1)
            out.append(jnp.where(near, x, jnp.where(group(start // 8), rest, 0.0)))
    return out


def lookup_kernel(v_table, d_table, forcing, mask, v_class, d_class, coef, *refs):
    sides, rows = refs[0:2], refs[2:4]
    tables, ints, edges, sems = refs[4:]
    pairs = [(v_table, tables[0]), (d_table, tables[1])]
    pairs += [(source, ints.at[i]) for i, source in enumerate((mask, v_class, d_class))]
    row_starts = halves_of("gy", ROWS, HALO)
    for i, start in enumerate((0, COLS - EDGE)):
        pairs.append((forcing.at[:, :, pl.ds(start, EDGE)], edges.at[i]))
    for start, target in zip(row_starts, rows):
        pairs.append((forcing.at[:, pl.ds(start, HALO), :], target.at[0:2]))
    copies = start_all(pairs, sems)
    for copy in copies[:5]:
        copy.wait()
    for r in range(0, ROWS, 8):
        for c in range(0, COLS, 128):
            part = (slice(r, r + 8), slice(c, c + 128))
            ice = ints[(0,) + part].astype(jnp.float32)
            found = look_up(tables, [ints[(1,) + part], ints[(2,) + part]], ice)
            for k in range(2):
                coef[(k,) + part] = found[k]
    for copy in copies[5:7]:
        copy.wait()
    even = lax.axis_index("gx") % 2 == 0
    messages = []
    for side, start in enumerate((0, COLS - EDGE)):
        parts = [[edges[side, k, 8 * r : 8 * r + 8] for r in range(4)] for k in range(2)]
        parts += [[coef[k, 8 * r : 8 * r + 8, start : start + EDGE] for r in range(4)] for k in range(2)]
        messages.append(pack_side(parts, side))
    for i in range(9):
        low, high = messages[0][i], messages[1][i]
        sides[0][8 * i : 8 * i + 8] = jnp.where(even, high, low)
        sides[1][8 * i : 8 * i + 8] = jnp.where(even, low, high)
    for k in range(2):
        for start, target in zip(row_starts, rows):
            target[2 + k] = coef[k, pl.ds(start, HALO), :]
    for copy in copies[7:]:
        copy.wait()


def corner_kernel(got_odd, got_even, sides, send_even, send_odd):
    gx = lax.axis_index("gx")
    even = gx % 2 == 0
    for side in range(2):
        end = gx == (0 if side == 0 else lax.axis_size("gx") - 1)

        def tile(i):
            rows = slice(8 * i, 8 * i + 8)
            a, b = got_even[rows], got_odd[rows]
            return jnp.where(end, 0.0, jnp.where(even, b, a) if side == 0 else jnp.where(even, a, b))

        parts = unpack_side([tile(i) for i in range(9)], 1 - side)
        for i, part in enumerate(parts):
            sides[side, i // 4, 8 * (i % 4) : 8 * (i % 4) + 8] = part
    for start, target in zip(halves_of("gy", ROWS, HALO), (send_even, send_odd)):
        for row in range(4):
            for side in range(2):
                target[row, :, side * EDGE : (side + 1) * EDGE] = sides[side, row, pl.ds(start, HALO)]


def own_rows(a, b):
    upper = lax.broadcasted_iota(jnp.int32, a.shape, 0) < 4
    return jnp.where(upper, pltpu.roll(a, 6, axis=0), pltpu.roll(b, 2, axis=0))


def levels_of(refs):
    return [Level(PLANES[i], refs[8 * i : 8 * i + 8]) for i in range(3)]


def spread(above, own, below, natural, targets, cols):
    gy = lax.axis_index("gy")
    even = gy % 2 == 0
    (above_even, above_odd), (below_even, below_odd) = above, below
    natural[0:HALO] = jnp.where(gy == 0, 0.0, jnp.where(even, above_odd, above_even))
    natural[HALO : HALO + ROWS] = own
    natural[HALO + ROWS : 2 * HALO + ROWS] = jnp.where(gy == lax.axis_size("gy") - 1, 0.0, jnp.where(even, below_even, below_odd))
    for p in range(8):
        targets(p, cols, natural[pl.ds(p, 8, stride=8), :])


def descend(levels, etas, betas, diags, others):
    for level in range(3):
        here = levels[level]
        here.setup(etas[level], betas[level], diags[level])
        here.first_sweeps(others[level])
        if level < 2:
            halve_planes(etas[level], etas[level + 1], here.planes, 0.5)
            halve_planes(betas[level], betas[level + 1], here.planes, 1.0)

            def store(k, p, value, target=levels[level + 1].force):
                target[k, p] = value

            here.restrict(diags[level], store)
    found = [None, None]

    def keep(k, p, value):
        found[k] = value

    levels[2].restrict(diags[2], keep)
    eta = 0.5 * halve_lanes(etas[2][0] + etas[2][1])
    beta = halve_lanes(betas[2][0] + betas[2][1])
    return found + [eta, beta]


def plane_targets(row, levels, etas, betas):
    def target(p, cols, plane):
        if row < 2:
            levels[0].force[row, p, :, cols] = plane
        else:
            (etas, betas)[row - 2][0][p, :, cols] = plane

    return target


def main_kernel(forcing, coef, rows_even, rows_odd, *refs):
    levels = levels_of(refs)
    top, natural = refs[24:26]
    etas, betas, diags, others = (refs[26 + 3 * i : 29 + 3 * i] for i in range(4))
    for row in range(4):
        source = forcing if row < 2 else coef
        target = plane_targets(row, levels, etas, betas)
        for i in range(COLS // 128):
            cols = slice(128 * i, 128 * i + 128)
            halo = (rows_even[row, :, cols], rows_odd[row, :, cols])
            spread(halo, source[row % 2, :, cols], halo, natural.at[8 * row + i], target, cols)
    for i, value in enumerate(descend(levels, etas, betas, diags, others)):
        top[i] = value


def rim_kernel(
    forcing,
    coef,
    sides,
    rows_even,
    rows_odd,
    corner_odd,
    corner_even,
    top,
    late_force,
    late_field,
    *refs,
):
    levels = levels_of(refs)
    near_even, near_odd, far, natural = refs[24:28]
    etas, betas, diags, others = (refs[28 + 3 * i : 31 + 3 * i] for i in range(4))
    for row in range(4):
        source = forcing if row < 2 else coef
        target = plane_targets(row, levels, etas, betas)
        for i in range(4):
            if i in (0, 3):
                part = slice(0, EDGE) if i == 0 else slice(EDGE, 2 * EDGE)
                halo = (corner_even[row, :, part], corner_odd[row, :, part])
                own = sides[i // 3, row]
            else:
                part = slice(0, EDGE) if i == 1 else slice(COLS - EDGE, COLS)
                halo = (rows_even[row, :, part], rows_odd[row, :, part])
                own = source[row % 2, :, part]
            spread(halo, own, halo, natural.at[4 * row + i], target, slice(128 * i, 128 * i + 128))
    rim = descend(levels, etas, betas, diags, others)
    both = [merge(3, top[i], rim[i]) for i in range(4)]
    head = jnp.concatenate([own_rows(both[0], both[1]), own_rows(both[2], both[3])], axis=1)
    far[...] = head
    at = head.shape[1]
    w, f = (
        [[merge(2, source[k, p + i], rims[k, p + i]) for p in range(2)] for k in range(2)]
        for i, source, rims in ((1, late_field, levels[2].field), (0, late_force, levels[2].force))
    )
    messages = []
    for picks in (
        lambda k: [(w[k][0], 4), (w[k][0], 5), (w[k][1], 4), (f[k][1], 4)],
        lambda k: [(w[k][0], 3), (w[k][1], 2), (w[k][1], 3), (f[k][0], 3)],
    ):
        rows = picks(0) + picks(1)
        message = pltpu.roll(rows[0][0], 8 - rows[0][1], axis=0)
        sub = lax.broadcasted_iota(jnp.int32, message.shape, 0)
        for i, (x, g) in enumerate(rows):
            if i:
                message = jnp.where(sub == i, pltpu.roll(x, (i - g) % 8, axis=0) if i != g else x, message)
        messages.append(message)
    even = lax.axis_index("gy") % 2 == 0
    for target, flag in ((near_even, even), (near_odd, jnp.logical_not(even))):
        target[:, 0:at] = head
        target[:, at:] = jnp.where(flag, messages[0], messages[1])


def merge_kernel(*refs):
    late = refs[48:]
    mains, rims = levels_of(refs[:24]), levels_of(refs[24:48])

    def joined(name, *index):
        return merge(0, getattr(mains[0], name)[index], getattr(rims[0], name)[index])

    names = ("right", "left", "cross_right", "cross_left", "scale")
    for i, name in enumerate(names):
        for p in range(8):
            value = joined(name, p)
            late[i][p] = own_rows(value, value)
            if p in (0, 7):
                late[8][i, p // 7] = value
    for p in range(9):
        value = joined("below", p)
        late[5][p] = own_rows(value, value)
        if p in (0, 1, 7, 8):
            late[9][(0, 1, 7, 8).index(p)] = value
    for p in range(8):
        force = [joined("force", k, p) for k in range(2)]
        field = [joined("field", k, p + 1) for k in range(2)]
        late[6][p] = own_rows(force[0], force[1])
        late[7][p] = own_rows(field[0], field[1])
        for k in range(2):
            if p in (0, 7):
                late[10][k, p // 7] = force[k]
            if p in (0, 1, 6, 7):
                late[11][k, (0, 1, 6, 7).index(p)] = field[k]
    for level in (1, 2):
        for i in range(8):
            main, rim = (refs[24 * j + 8 * level + i] for j in range(2))
            target = late[4 + 8 * level + i]
            planes = PLANES[level]
            if i < 6:
                for p in range(main.shape[0]):
                    target[p] = merge(level, main[p], rim[p])
            else:
                for k in range(2):
                    for p in range(i - 6, planes + i - 6):
                        target[k, p] = merge(level, main[k, p], rim[k, p])


def finest_up(refs, coarse, packed, next_packed, natural, velocity, sems):
    right, left, cross_right, cross_left, scale, below, force, field = refs[:8]
    edge_coef, edge_below, edge_force, edge_field = refs[8:]
    wide = MERGED[0]
    edges = [[None] * 8, [None] * 8]
    for p in range(0, 8, 2):
        below_this = [coarse(k, p // 2) for k in range(2)]
        both = double_lanes(own_rows(below_this[0], below_this[1]), wide)
        adds = [double_lanes(x, wide) if p in (0, 6) else None for x in below_this]
        for q in (p, p + 1):
            packed[q] = field[q] + both
            if q in (0, 1, 6, 7):
                for k in range(2):
                    edges[k][q] = edge_field[k, (0, 1, 6, 7).index(q)] + adds[k]
    found = {}
    for i, p in enumerate((0, 7)):
        under = [edges[k][1] if p == 0 else from_below(edges[k][0]) for k in range(2)]
        over = [from_above(edges[k][7]) if p == 0 else edges[k][6] for k in range(2)]
        for k in range(2):
            terms = gather_terms(
                edge_coef[0, i],
                edge_coef[1, i],
                edge_coef[2, i],
                edge_coef[3, i],
                edge_below[2 * i + 1],
                edge_below[2 * i],
                edges[k][p],
                under[k],
                over[k],
                under[1 - k] - over[1 - k],
                edge_force[k, i],
            )
            found[k, p] = KEEP * edges[k][p] + edge_coef[4, i] * terms
    next_packed[1] = own_rows(found[0, 0], found[1, 0])
    next_packed[8] = own_rows(found[0, 7], found[1, 7])
    next_packed[0] = own_rows(from_above(found[0, 7]), from_above(found[1, 7]))
    next_packed[9] = own_rows(from_below(found[0, 0]), from_below(found[1, 0]))

    def sweep(p, above, here, under, first, count, part):
        mid = slice(128, 128 + 128 * count)
        low, high = slice(0, 128 + 128 * count), slice(128, 256 + 128 * count)
        over, w, down = part(above), part(here), part(under)
        step = pltpu.roll(down - over, 4, axis=0)
        west = from_left((part(right[p]) * w + part(cross_right[p]) * step)[:, low])[:, 128:]
        east = from_right((part(left[p]) * w - part(cross_left[p]) * step)[:, high])[:, : 128 * count]
        cols = slice(128 * first, 128 * (first + count))
        terms = (force[p][:, cols] + (west + east)) + (below[p + 1][:, cols] * down[:, mid] + below[p][:, cols] * over[:, mid])
        return KEEP * w[:, mid] + scale[p][:, cols] * terms

    for p in range(1, 7):
        over, here, under = packed[p - 1], packed[p], packed[p + 1]
        terms = gather_terms(
            right[p],
            left[p],
            cross_right[p],
            cross_left[p],
            below[p + 1],
            below[p],
            here,
            under,
            over,
            pltpu.roll(under - over, 4, axis=0),
            force[p],
        )
        next_packed[p + 1] = KEEP * here + scale[p] * terms
    copies = []
    first = 0
    for count in (4, 3, 1):

        def part(x):
            end = x[:, 128 * max(first - 1, 0) : 128 * (first + count + 1)]
            return end if first else jnp.concatenate([x[:, wide - 128 :], end], axis=1)

        for p in range(8):
            done = sweep(p, next_packed[p], next_packed[p + 1], next_packed[p + 2], first, count, part)
            for i in range(count):
                tile = done[:, 128 * i : 128 * i + 128]
                for k in range(2):
                    natural[k, first + i, pl.ds(p, 4, stride=8), :] = tile[4 * k : 4 * k + 4]
        for i in range(first, first + count):
            for k in range(2):
                target = velocity.at[k, :, pl.ds(128 * i, 128)]
                copy = pltpu.make_async_copy(natural.at[k, i, pl.ds(0, ROWS)], target, sems.at[2 * i + k])
                copy.start()
                copies.append(copy)
        first += count
    for copy in copies:
        copy.wait()


def up_kernel(far, near_odd, far_even, far_odd, near_even, *refs):
    levels = [None] + [Level(PLANES[i], refs[4 + 8 * i : 12 + 8 * i]) for i in (1, 2)]
    velocity, natural, sems, packed, next_packed, late_force, late_field = refs[28:35]
    fields, others = (None,) + refs[35:37], (None,) + refs[37:39]
    gy = lax.axis_index("gy")
    count = lax.axis_size("gy")
    even = gy % 2 == 0

    def above(part):
        return jnp.where(gy == 0, 0.0, jnp.where(even, near_odd[:, part], near_even[:, part]))

    def below(part):
        return jnp.where(gy == count - 1, 0.0, jnp.where(even, near_even[:, part], near_odd[:, part]))

    def sublanes(like):
        return lax.broadcasted_iota(jnp.int32, like.shape, 0)

    def stacked(part):
        low = gy // 2 % 2 == 0
        m2 = jnp.where(gy < 2, 0.0, jnp.where(low, far_odd[:, part], far_even[:, part]))
        p2 = jnp.where(gy > count - 3, 0.0, jnp.where(low, far_even[:, part], far_odd[:, part]))
        m1, p1, own = above(part), below(part), far[:, part]
        sub = sublanes(own)
        out = []
        for outer, inner in ((6, 2), (2, 6)):

            def tile(x, y, z):
                x, z = pltpu.roll(x, outer, axis=0), pltpu.roll(z, outer, axis=0)
                return jnp.where(sub < 2, x, jnp.where(sub < 6, pltpu.roll(y, inner, axis=0), z))

            if outer == 6:
                ends = jnp.where(sub < 4, m2, pltpu.roll(p2, 4, axis=0))
            else:
                ends = jnp.where(sub < 4, pltpu.roll(m2, 4, axis=0), p2)
            out.append((jnp.concatenate([tile(m2, m1, own), tile(own, p1, p2)], axis=0), ends))
        return out

    force = stacked(slice(0, MERGED[3]))
    (eta, eta_ends), (beta, beta_ends) = stacked(slice(MERGED[3], 2 * MERGED[3]))
    row = sublanes(eta)

    def shifted_down(x, ends):
        first = pltpu.roll(ends, 7, axis=0)
        return jnp.where(row == 0, jnp.concatenate([first, first], axis=0), from_above(x))

    def shifted_up(x, ends):
        last = pltpu.roll(ends, 1, axis=0)
        return jnp.where(row == 15, jnp.concatenate([last, last], axis=0), from_below(x))

    ends = coefficients(eta_ends, beta_ends, from_below(eta_ends), from_above)
    right, left, under, over, cross_right, cross_left, diag = coefficients(
        eta, beta, shifted_up(eta, eta_ends), lambda x: shifted_down(x, ends[2])
    )
    scale = OMEGA / diag
    scale_ends = OMEGA / ends[6]
    field = [scale * force[k][0] for k in range(2)]
    for step in range(5):
        if step == 0:
            field_ends = [scale_ends * force[k][1] for k in range(2)]
            downs = [shifted_up(field[k], field_ends[k]) for k in range(2)]
            ups = [shifted_down(field[k], field_ends[k]) for k in range(2)]
        else:
            downs = [from_below(x) for x in field]
            ups = [from_above(x) for x in field]
        steps = [downs[k] - ups[k] for k in range(2)]
        field = [
            KEEP * field[k]
            + scale
            * gather_terms(
                right, left, cross_right, cross_left, under, over, field[k], downs[k], ups[k], steps[1 - k], force[k][0]
            )
            for k in range(2)
        ]
    coarsest = []
    for k in range(2):
        a, b = pltpu.roll(field[k][0:8], 4, axis=0), pltpu.roll(field[k][8:16], 4, axis=0)
        coarsest.append(jnp.where(sublanes(a) < 4, a, b))
    part = slice(2 * MERGED[3], 2 * MERGED[3] + MERGED[2])
    up, down = above(part), below(part)
    sub = sublanes(up)
    own_field, own_force = levels[2].field, levels[2].force
    for k in range(2):

        def turned(x, by):
            by = (by - 4 * k) % 8
            return pltpu.roll(x, by, axis=0) if by else x

        late_field[k, 1] = jnp.where(sub < 2, turned(up, 0), jnp.where(sub < 7, own_field[k, 1], turned(down, 7)))
        late_field[k, 2] = jnp.where(sub < 1, turned(up, 6), jnp.where(sub < 6, own_field[k, 2], turned(down, 5)))
        late_force[k, 0] = jnp.where(sub < 7, own_force[k, 0], turned(down, 4))
        late_force[k, 1] = jnp.where(sub < 1, turned(up, 5), own_force[k, 1])
    levels[2].force = late_force
    levels[2].field = late_field
    coarse = lambda k, p: coarsest[k]
    for level in (2, 1):
        levels[level].last_sweeps(coarse, fields[level], others[level])
        coarse = lambda k, p, result=fields[level]: result[k, p + 1]
    finest_up(refs[:12], coarse, packed, next_packed, natural, velocity, sems)


def swap(x, axis, odd):
    rows, cols = lax.axis_size("gy"), lax.axis_size("gx")
    count, across = (rows, cols) if axis == "gy" else (cols, rows)
    pairs = []
    for j in range(across):
        for i in range(odd, count - 1, 2):
            pairs += [((i, j), (i + 1, j)), ((i + 1, j), (i, j))]
        if odd:
            pairs += [((i, j), (i, j ^ 1)) for i in (0, count - 1)]
    place = (lambda i, j: j * rows + i) if axis == "gy" else (lambda i, j: i * rows + j)
    return lax.ppermute(x, ("gx", "gy"), [(place(*a), place(*b)) for a, b in pairs])


def swap_far(x, odd):
    count = lax.axis_size("gy")
    pairs = []
    for i in range(0, count - 2):
        if i // 2 % 2 == odd:
            pairs += [(i, i + 2), (i + 2, i)]
    if odd:
        pairs += [(i, i ^ 1) for i in (0, 1, count - 2, count - 1)]
    return lax.ppermute(x, "gy", pairs)


def local(forcing, ice_mask, viscosity_class, drag_class, viscosity_table, drag_table):
    inputs = [
        pltpu.with_memory_space_constraint(x, pltpu.HBM)
        for x in (viscosity_table, drag_table, forcing, ice_mask, viscosity_class, drag_class)
    ]
    hbm = [pl.BlockSpec(memory_space=pltpu.HBM)] * 6
    table = pltpu.SMEM((16,), jnp.float32)
    coef, side_even, side_odd, main_even, main_odd = pl.pallas_call(
        lookup_kernel,
        out_shape=(shape(2, ROWS, COLS),) + (shape(72, 128),) * 2 + (shape(4, HALO, COLS),) * 2,
        in_specs=hbm,
        out_specs=tuple(vmem(5)),
        scratch_shapes=[[table, table], pltpu.VMEM((3, ROWS, COLS), jnp.int32)]
        + [pltpu.VMEM((2, 2, ROWS, EDGE), jnp.float32), pltpu.SemaphoreType.DMA((9,))],
        compiler_params=params(),
        name="lookup",
    )(*inputs)
    got_odd = swap(side_odd, "gx", 1)
    got_even = swap(side_even, "gx", 0)
    rows_odd = swap(main_odd, "gy", 1)
    sides, send_even, send_odd = pl.pallas_call(
        corner_kernel,
        out_shape=(shape(2, 4, ROWS, EDGE),) + (shape(4, HALO, 2 * EDGE),) * 2,
        in_specs=vmem(2),
        out_specs=tuple(vmem(3)),
        compiler_params=params(),
        name="corners",
    )(got_odd, got_even)
    corner_odd = swap(send_odd, "gy", 1)
    corner_even = swap(send_even, "gy", 0)
    rows_even = swap(main_even, "gy", 0)

    def kept(widths):
        return [dims for level in range(3) for dims in Level.shapes(level, widths)]

    def scratch(dims):
        return [pltpu.VMEM(one, jnp.float32) for one in dims]

    def rims(widths):
        return [(2, PLANES[i] + 2, 8, widths[i]) for i in range(3)]

    def work(widths):
        return scratch([(32, 72, 128)] + [(PLANES[i], 8, widths[i]) for i in range(3)] * 3 + rims(widths))

    *main, top = pl.pallas_call(
        main_kernel,
        out_shape=tuple(shape(*dims) for dims in kept(MAIN) + [(4, 8, MAIN[3])]),
        in_specs=vmem(4),
        out_specs=tuple(vmem(25)),
        scratch_shapes=work(MAIN),
        compiler_params=params(),
        name="main",
    )(forcing, coef, rows_even, rows_odd)
    near_lanes = 2 * MERGED[3] + MERGED[2]
    *rim, send_even, send_odd, far = pl.pallas_call(
        rim_kernel,
        out_shape=tuple(shape(*dims) for dims in kept(RIM) + [(8, near_lanes)] * 2 + [(8, 2 * MERGED[3])]),
        in_specs=vmem(10),
        out_specs=tuple(vmem(27)),
        scratch_shapes=work(RIM),
        compiler_params=params(),
        name="rim",
    )(forcing, coef, sides, rows_even, rows_odd, corner_odd, corner_even, top, main[22], main[23])
    near_even = swap(send_even, "gy", 0)
    near_odd = swap(send_odd, "gy", 1)
    far_even = swap_far(far, 0)
    far_odd = swap_far(far, 1)
    wide = MERGED[0]
    finest = [(8, 8, wide)] * 5 + [(9, 8, wide)] + [(8, 8, wide)] * 2
    finest += [(5, 2, 8, wide), (4, 8, wide), (2, 2, 8, wide), (2, 4, 8, wide)]
    merged = pl.pallas_call(
        merge_kernel,
        out_shape=tuple(shape(*dims) for dims in finest + kept(MERGED)[8:]),
        in_specs=vmem(48),
        out_specs=tuple(vmem(28)),
        compiler_params=params(),
        name="merge",
    )(*main, *rim)
    late = [(8, 8, wide), (10, 8, wide), (2, 2, 8, MERGED[2]), (2, 4, 8, MERGED[2])]
    return pl.pallas_call(
        up_kernel,
        out_shape=shape(2, ROWS, COLS),
        in_specs=vmem(33),
        out_specs=pl.BlockSpec(memory_space=pltpu.HBM),
        scratch_shapes=scratch([(2, COLS // 128, ROWS + 8, 128)])
        + [pltpu.SemaphoreType.DMA((2 * COLS // 128,))]
        + scratch(late + rims(MERGED)[1:] + rims(MERGED)[1:]),
        compiler_params=params(),
        name="up",
    )(far, near_odd, far_even, far_odd, near_even, *merged)


def solution(mesh):
    in_specs = (P(None, "gy", "gx"), P("gy", "gx"), P("gy", "gx"), P("gy", "gx"), P(), P())
    out_specs = P(None, "gy", "gx")
    return jax.shard_map(local, mesh=mesh, in_specs=in_specs, out_specs=out_specs, check_vma=False)
```
